32 devices in a mesh: dp: 2 (over y), expert: 16 (over z, x, core).
Axes of the slice: x: 2, y: 2, z: 4, core: 2. Of those that a mesh axis runs over, the one named last changes fastest.
Arguments:
- hidden_rows: bfloat16 [768, 4096], P(None, ('dp', 'expert')), may hold values from -6 to 6
- grad_rows: bfloat16 [4096, 2560], P(('dp', 'expert')), may hold values from -0.1796875 to 0.1796875
- block_slot: int32 [32, 1], P(('dp', 'expert')), may hold values from 0 to 1
- live_rows: int32 [32], P(('dp', 'expert')), may hold values from 16 to 128
- replica_plan: int32 [16], replicated, may hold values from 0 to 3
- master: float32 [16, 768, 640], P('expert', 'dp'), may hold values from -0.21875 to 0.21875
- moment_one: float32 [16, 768, 640], P('expert', 'dp'), may hold values from -1.8 to 1.8
- moment_two: float32 [16, 768, 640], P('expert', 'dp'), may hold values from 0.01 to 1
Outputs:
- master_new: float32 [16, 768, 640], P('expert', 'dp')
- first_new: float32 [16, 768, 640], P('expert', 'dp')
- second_new: float32 [16, 768, 640], P('expert', 'dp')
- replica_weight: bfloat16 [16, 768, 2560], P('expert', 'dp')
The draws below stay inside these ranges and needn't reach their ends.
Inputs may be any that keep to these rules, and one draw needn't show every extreme that they name: replica_plan[j] is the expert of which the devices at index j along the expert axis host a replica; it may equal j mod 4. `block_slot`: 0 marks a block of the primary expert, 1 a block of the replica.
All inputs are finite; a program needn't handle non-finite values.
Results may differ from the reference program's by a relative error of at most 0.001.
Values may be sent and summed in bfloat16 or wider, within the bound.
No kernel may reach another device: no remote copies, remote signals or barrier semaphores. Data moves between devices by JAX's collectives and lax.ppermute only.
A program may use at most 64 MiB of HBM per device.

```python
import math
import jax
import jax.numpy as jnp
import numpy as np
from jax import lax

D = 2560
HID = 768
QUART = 4
BLK = 128
BLOCKS = 1
ROWS = 128
EXPERTS = 4
N_DP = 2
N_EXPERT = 16


def with_ends(drawn, key, smallest, largest):
    longest = drawn.shape.index(max(drawn.shape))
    spots = []
    for shift in (0, 1):
        where = [jax.random.randint(jax.random.fold_in(key, axis), (), 0, length) for axis, length in enumerate(drawn.shape)]
        where[longest] = (where[longest] + shift) % drawn.shape[longest]
        spots.append(tuple(where))
    return drawn.at[spots[0]].set(smallest).at[spots[1]].set(largest)


def steps_of(key, dims, cuts, smallest, top_value):
    gain, own = 1.0, jax.random.fold_in(key, 6)
    for axis_at, blocks in cuts:
        draws = jnp.exp(jax.random.uniform(jax.random.fold_in(own, axis_at), (blocks,), jnp.float32, smallest / len(cuts), top_value / len(cuts)))
        gain = gain * jnp.repeat(draws, dims[axis_at] // blocks).reshape([-1 if axis == axis_at else 1 for axis in range(len(dims))])
    return gain


def rank_bounds(count, slope):
    loads = [(1 << 20) // math.isqrt(standing ** slope) + 1 for standing in range(1, count + 1)]
    scale = 1 + sum(loads) // (1 << 30)
    return np.cumsum(np.array([max(1, weight // scale) for weight in loads]))


def ranked(stream_key, dims, amount, slope):
    grid = rank_bounds(amount, slope)
    lot = jax.random.randint(jax.random.fold_in(stream_key, 1), dims, 0, int(grid[amount - 1]))
    rank = jnp.searchsorted(jnp.asarray(grid, jnp.int32), lot, side="right")
    return jax.random.permutation(jax.random.fold_in(stream_key, 2), amount)[rank].astype(jnp.int32)


def centred(key, dims, spread, bound, shards=(), dtype=jnp.bfloat16):
    result = jax.random.normal(key, dims, jnp.float32) * spread
    if len(shards) > 0:
        result = steps_of(key, dims, shards, -0.22, 0.18) * result
    return jnp.clip(result, min=-bound, max=bound).astype(dtype)


def setup_inputs(seed: int = 0) -> dict:
    arg_keys = jax.random.split(jax.random.key(seed), 9)
    return {
        "hidden_rows": centred(arg_keys[0], (HID, N_DP * N_EXPERT * ROWS), 1.0, 6.0, ((1, 32),)),
        "grad_rows": centred(arg_keys[1], (N_DP * N_EXPERT * ROWS, D), 0.03, 0.1796875, ((0, 32),)),
        "block_slot": with_ends(jax.random.randint(arg_keys[2], (N_DP * N_EXPERT, BLOCKS), 0, 2), jax.random.fold_in(arg_keys[2], 1), 0, 1).astype(jnp.int32),
        "live_rows": with_ends(jax.random.randint(arg_keys[3], (N_DP * N_EXPERT,), ROWS // 8, ROWS + 1), jax.random.fold_in(arg_keys[3], 1), ROWS // 8, ROWS).astype(jnp.int32),
        "replica_plan": with_ends(ranked(arg_keys[4], (N_EXPERT,), EXPERTS, 2), jax.random.fold_in(arg_keys[4], 3), 0, EXPERTS - 1).astype(jnp.int32),
        "master": centred(arg_keys[5], (N_EXPERT, HID, D // QUART), HID ** -0.5, 0.21875, ((0, 16), (1, 2)), jnp.float32),
        "moment_one": centred(arg_keys[6], (N_EXPERT, HID, D // QUART), 0.3, 1.8, ((0, 16), (1, 2)), jnp.float32),
        "moment_two": jnp.clip(jnp.exp(math.log(1.0) - 4.6051702 * jax.random.uniform(arg_keys[7], (N_EXPERT, HID, D // QUART), jnp.float32) ** steps_of(arg_keys[7], (N_EXPERT, HID, D // QUART), ((0, 16), (1, 2)), -0.2, 0.2)), 0.01, 1.0),
    }


beta_one = 0.9
beta_two = 0.95
learn_rate = 0.01
decay_rate = 0.1
epsilon = 1e-08
step_count = 10.0

def adam_update(weights, first, second, gradient):
    first_next = beta_one * first + (1.0 - beta_one) * gradient
    second_next = beta_two * second + (1.0 - beta_two) * gradient * gradient
    scaled_first = first_next / (1.0 - beta_one ** step_count)
    scaled_second = second_next / (1.0 - beta_two ** step_count)
    direction = scaled_first / (jnp.sqrt(scaled_second) + epsilon)
    weights_next = weights - learn_rate * (direction + decay_rate * weights)
    return (weights_next, first_next, second_next)

def add_into(total, index, term):
    current = lax.dynamic_index_in_dim(total, index, 0, False)
    return lax.dynamic_update_index_in_dim(total, current + term, index, 0)

def reference(hidden_rows, grad_rows, block_slot, live_rows, replica_plan, master, moment_one, moment_two):
    device_count = N_DP * N_EXPERT
    tok_rows = BLK * BLOCKS
    expert_total = N_EXPERT // QUART
    block_width = D // QUART
    hidden_all = jnp.transpose(hidden_rows.reshape(HID, device_count, tok_rows), (1, 0, 2))
    grad_all = grad_rows.reshape(device_count, tok_rows, D)
    positions = lax.iota(jnp.int32, tok_rows)

    def one_device(total, inputs):
        hidden_dev, grad_dev, slots, live, index = inputs
        kept_rows = positions < live
        row_slot = jnp.repeat(slots, BLK)
        zeros_like = jnp.zeros_like(grad_dev)
        grad_primary = jnp.where((kept_rows & (row_slot == 0))[:, None], grad_dev, zeros_like)
        grad_replica = jnp.where((kept_rows & (row_slot == 1))[:, None], grad_dev, zeros_like)
        primary = jnp.dot(hidden_dev, grad_primary, preferred_element_type=jnp.float32)
        replica_low = lax.optimization_barrier(jnp.dot(hidden_dev, grad_replica, preferred_element_type=jnp.float32).astype(jnp.bfloat16))
        replica = replica_low.astype(jnp.float32)
        column = (index % N_EXPERT).astype(jnp.int32)
        owner = (column % expert_total).astype(jnp.int32)
        host = lax.dynamic_index_in_dim(replica_plan, column, 0, False).astype(jnp.int32)
        total = add_into(total, owner, primary)
        total = add_into(total, host, replica)
        return (total, None)
    start = jnp.zeros((expert_total, HID, D), jnp.float32)
    indices = lax.iota(jnp.int32, device_count)
    gradient, unused = lax.scan(one_device, start, (hidden_all, grad_all, block_slot, live_rows, indices))
    grad_state = jnp.transpose(gradient.reshape(expert_total, HID, QUART, block_width), (2, 0, 1, 3)).reshape(N_EXPERT, HID, block_width)
    master_new, first_new, second_new = adam_update(master, moment_one, moment_two, grad_state)
    full_weights = jnp.transpose(master_new.reshape(QUART, expert_total, HID, block_width), (1, 2, 0, 3)).reshape(expert_total, HID, D)
    replica_weight = jnp.take(full_weights.astype(jnp.bfloat16), replica_plan, axis=0)
    return (master_new, first_new, second_new, replica_weight)
```

```python
import functools

import jax
import jax.numpy as jnp
from jax import lax
from jax.experimental import pallas as pl
from jax.experimental.pallas import tpu as pltpu
from jax.sharding import PartitionSpec as P

QUART = 4
LANES = 128
META_ROWS = 16


beta_one = 0.9
beta_two = 0.95
learn_rate = 0.01
decay_rate = 0.1
epsilon = 1e-08
step_count = 10.0

VMEM = pl.BlockSpec(memory_space=pltpu.VMEM)
SMEM = pl.BlockSpec(memory_space=pltpu.SMEM)


def vmem_for(*arrays):
    return int(sum(a.size * a.dtype.itemsize for a in arrays) * 5 // 4) + (8 << 20)


def call(kernel, out_shapes, scalars, arrays, flops=0):
    moved = sum(a.size * a.dtype.itemsize for a in (*arrays, *out_shapes))
    return pl.pallas_call(
        kernel,
        out_shape=tuple(out_shapes),
        in_specs=[SMEM] * len(scalars) + [VMEM] * len(arrays),
        out_specs=tuple([VMEM] * len(out_shapes)),
        compiler_params=pltpu.CompilerParams(vmem_limit_bytes=vmem_for(*arrays, *out_shapes)),
        cost_estimate=pl.CostEstimate(flops=flops, bytes_accessed=moved, transcendentals=0),
    )(*scalars, *arrays)


def from_behind(block, axis, distance):
    devices = range(lax.axis_size(axis))
    route = [((i - distance) % len(devices), i) for i in devices]
    return lax.ppermute(block, axis, route)


def from_mate(block, axis, bit):
    return lax.ppermute(block, axis, [(i ^ bit, i) for i in range(lax.axis_size(axis))])


def gather_mates(block, axis, count):
    held = {0: block}
    bit = count // 2
    while bit:
        held.update({m | bit: from_mate(held[m], axis, bit) for m in list(held)})
        bit //= 2
    return [held[m] for m in range(count)]


def place(owner_count):
    own = lax.axis_index("expert")
    return own // owner_count, own % owner_count


def message_kernel(owner_count, slot_ref, live_ref, hidden_ref, grad_ref, *message_refs):
    own_block, _ = place(owner_count)
    hidden_units, tok_rows = hidden_ref.shape
    block_width = grad_ref.shape[1] // QUART
    live = live_ref[0]
    slot = slot_ref[0, 0]
    kept = lax.broadcasted_iota(jnp.int32, (tok_rows, LANES), 0) < live
    meta = jnp.full((META_ROWS, LANES), slot.astype(jnp.float32)).astype(jnp.bfloat16)
    for step, message in enumerate(message_refs):
        target = lax.rem(own_block + step, QUART)
        message[:hidden_units, :] = hidden_ref[...]
        for part in range(block_width // LANES):
            start = pl.multiple_of(target * block_width + part * LANES, LANES)
            columns = grad_ref[:, pl.ds(start, LANES)].astype(jnp.float32)
            row = hidden_units + part * tok_rows
            message[row : row + tok_rows, :] = jnp.where(kept, columns, 0.0).astype(jnp.bfloat16)
        message[hidden_units + (block_width // LANES) * tok_rows :, :] = meta


def partial_kernel(owner_count, hidden_units, tok_rows, steps, plan_ref, *refs):
    messages, totals = refs[: -len(steps)], refs[-len(steps) :]
    own_block, own_expert = place(owner_count)
    group, groups = lax.axis_index("dp"), lax.axis_size("dp")
    share_rows, block_width = totals[0].shape
    for total in totals:
        total[...] = jnp.zeros_like(total)
    parts = block_width // LANES
    meta_row = hidden_units + parts * tok_rows
    chunk = next(c for c in (128, 64, 48, 32, 16) if share_rows % c == 0)
    for at, message in enumerate(messages):
        step, mate = divmod(at, owner_count)
        source_expert = own_expert ^ mate
        source = lax.rem(own_block + QUART - step, QUART) * owner_count + source_expert
        is_replica = jnp.max(message[meta_row:, :].astype(jnp.float32)) > 0.5
        target = jnp.where(is_replica, plan_ref[source], source_expert)

        @pl.when(target == own_expert)
        def _():
            columns = jnp.concatenate(
                [
                    message[hidden_units + p * tok_rows : hidden_units + (p + 1) * tok_rows, :]
                    for p in range(parts)
                ],
                axis=1,
            )
            for total, ahead in zip(totals, steps):
                first = lax.rem(group + ahead, groups) * share_rows

                @pl.loop(0, share_rows // chunk)
                def _(i):
                    rows = pl.multiple_of(first + i * chunk, 16)
                    term = jnp.dot(
                        message[pl.ds(rows, chunk), :], columns, preferred_element_type=jnp.float32
                    )
                    rounded = term.astype(jnp.bfloat16).astype(jnp.float32)
                    into = pl.ds(pl.multiple_of(i * chunk, 16), chunk)
                    total[into, :] += jnp.where(is_replica, rounded, term)


def update_kernel(parts, *refs):
    terms, (master, one, two), (master_out, one_out, two_out, fresh) = (
        refs[:parts],
        refs[parts : parts + 3],
        refs[parts + 3 :],
    )
    gradient = terms[0][...]
    for term in terms[1:]:
        gradient = gradient + term[...]
    weights = master[...]
    first_next = beta_one * one[...] + (1.0 - beta_one) * gradient
    second_next = beta_two * two[...] + (1.0 - beta_two) * gradient * gradient
    scaled_first = first_next / (1.0 - beta_one**step_count)
    scaled_second = second_next / (1.0 - beta_two**step_count)
    direction = scaled_first / (jnp.sqrt(scaled_second) + epsilon)
    weights_next = weights - learn_rate * (direction + decay_rate * weights)
    master_out[...] = weights_next
    one_out[...] = first_next
    two_out[...] = second_next
    fresh[...] = weights_next.astype(jnp.bfloat16)


def choose_kernel(owner_count, plan_ref, *refs):
    candidates, chosen = refs[:owner_count], refs[owner_count:]
    own_block, own_expert = place(owner_count)
    for step, out in enumerate(chosen):
        wanted = plan_ref[lax.rem(own_block + step, QUART) * owner_count + own_expert]
        for mate, candidate in enumerate(candidates):

            @pl.when(wanted == own_expert ^ mate)
            def _():
                out[...] = candidate[...]


def assemble_kernel(owner_count, *refs):
    out = refs[-1]
    own_block, _ = place(owner_count)
    for step, block in enumerate(refs[:-1]):
        width = block.shape[1]
        start = lax.rem(own_block + QUART - step, QUART) * width
        out[:, pl.ds(pl.multiple_of(start, LANES), width)] = block[...]


def per_device(
    hidden_rows, grad_rows, block_slot, live_rows, replica_plan, master, moment_one, moment_two
):
    owner_count = lax.axis_size("expert") // QUART
    groups = lax.axis_size("dp")
    hidden_units, tok_rows = hidden_rows.shape
    block_width = grad_rows.shape[1] // QUART
    share_rows = hidden_units // groups
    assert block_slot.shape[1] == 1 and tok_rows == LANES and block_width % LANES == 0
    shape = jax.ShapeDtypeStruct

    length = hidden_units + (block_width // LANES) * tok_rows + META_ROWS
    messages = call(
        functools.partial(message_kernel, owner_count),
        [shape((length, LANES), jnp.bfloat16)] * QUART,
        (block_slot, live_rows),
        (hidden_rows, grad_rows),
    )
    gathered = []
    for step, message in enumerate(messages):
        if step:
            message = from_behind(message, "expert", step * owner_count)
        gathered += gather_mates(message, "expert", owner_count)

    def partials(steps):
        return call(
            functools.partial(partial_kernel, owner_count, hidden_units, tok_rows, steps),
            [shape((share_rows, block_width), jnp.float32)] * len(steps),
            (replica_plan,),
            gathered,
            2 * len(steps) * share_rows * tok_rows * block_width * QUART,
        )

    ahead = tuple(range(1, groups))
    far = [from_behind(p, "dp", step) for step, p in zip(ahead, partials(ahead))]
    near = partials((0,))
    state = shape((share_rows, block_width), jnp.float32)
    weights_next, first_next, second_next, fresh = call(
        functools.partial(update_kernel, groups),
        [state, state, state, shape((share_rows, block_width), jnp.bfloat16)],
        (),
        (*near, *far, master[0], moment_one[0], moment_two[0]),
    )
    candidates = gather_mates(fresh, "expert", owner_count)
    chosen = call(
        functools.partial(choose_kernel, owner_count),
        [shape((share_rows, block_width), jnp.bfloat16)] * QUART,
        (replica_plan,),
        candidates,
    )
    received = [
        from_behind(block, "expert", step * owner_count) if step else block
        for step, block in enumerate(chosen)
    ]
    (replica_weight,) = call(
        functools.partial(assemble_kernel, owner_count),
        [shape((share_rows, QUART * block_width), jnp.bfloat16)],
        (),
        received,
    )
    return (weights_next[None], first_next[None], second_next[None], replica_weight[None])


def solution(mesh):
    return jax.shard_map(
        per_device,
        mesh=mesh,
        in_specs=(
            P(None, ("dp", "expert")),
            P(("dp", "expert"), None),
            P(("dp", "expert"), None),
            P(("dp", "expert")),
            P(),
            P("expert", "dp", None),
            P("expert", "dp", None),
            P("expert", "dp", None),
        ),
        out_specs=(
            P("expert", "dp", None),
            P("expert", "dp", None),
            P("expert", "dp", None),
            P("expert", "dp", None),
        ),
        check_vma=False,
    )
```

```python
import functools

import jax
import jax.numpy as jnp
from jax import lax
from jax.experimental import pallas as pl
from jax.experimental.pallas import tpu as pltpu
from jax.sharding import PartitionSpec as P

QUART = 4
LANES = 128
META_ROWS = 16


beta_one = 0.9
beta_two = 0.95
learn_rate = 0.01
decay_rate = 0.1
epsilon = 1e-08
step_count = 10.0

VMEM = pl.BlockSpec(memory_space=pltpu.VMEM)
SMEM = pl.BlockSpec(memory_space=pltpu.SMEM)


def vmem_for(*arrays):
    return int(sum(a.size * a.dtype.itemsize for a in arrays) * 5 // 4) + (8 << 20)


def call(kernel, out_shapes, scalars, arrays, flops=0):
    moved = sum(a.size * a.dtype.itemsize for a in (*arrays, *out_shapes))
    return pl.pallas_call(
        kernel,
        out_shape=tuple(out_shapes),
        in_specs=[SMEM] * len(scalars) + [VMEM] * len(arrays),
        out_specs=tuple([VMEM] * len(out_shapes)),
        compiler_params=pltpu.CompilerParams(vmem_limit_bytes=vmem_for(*arrays, *out_shapes)),
        cost_estimate=pl.CostEstimate(flops=flops, bytes_accessed=moved, transcendentals=0),
    )(*scalars, *arrays)


def from_behind(block, axis, distance):
    devices = range(lax.axis_size(axis))
    route = [((i - distance) % len(devices), i) for i in devices]
    return lax.ppermute(block, axis, route)


def from_mate(block, axis, bit):
    return lax.ppermute(block, axis, [(i ^ bit, i) for i in range(lax.axis_size(axis))])


def gather_mates(block, axis, count):
    held = {0: block}
    bit = count // 2
    while bit:
        held.update({m | bit: from_mate(held[m], axis, bit) for m in list(held)})
        bit //= 2
    return [held[m] for m in range(count)]


def place(owner_count):
    own = lax.axis_index("expert")
    return own // owner_count, own % owner_count


def message_kernel(owner_count, spans, slot_ref, live_ref, hidden_ref, grad_ref, *message_refs):
    own_block, _ = place(owner_count)
    groups = lax.axis_size("dp")
    hidden_units, tok_rows = hidden_ref.shape
    share_rows = hidden_units // groups
    block_width = grad_ref.shape[1] // QUART
    parts = block_width // LANES
    live = live_ref[0]
    slot = slot_ref[0, 0]
    kept = lax.broadcasted_iota(jnp.int32, (tok_rows, LANES), 0) < live
    meta = jnp.full((META_ROWS, LANES), slot.astype(jnp.float32)).astype(jnp.bfloat16)

    def put_hidden(message, row, span):
        first, length = span
        for group in range(groups):
            start = group * share_rows + first
            message[row : row + length, :] = hidden_ref[start : start + length, :]
            row += length

    for step, message in enumerate(message_refs[:QUART]):
        target = lax.rem(own_block + step, QUART)
        for part in range(parts):
            start = pl.multiple_of(target * block_width + part * LANES, LANES)
            columns = grad_ref[:, pl.ds(start, LANES)].astype(jnp.float32)
            row = part * tok_rows
            message[row : row + tok_rows, :] = jnp.where(kept, columns, 0.0).astype(jnp.bfloat16)
        row = parts * tok_rows
        message[row : row + META_ROWS, :] = meta
        put_hidden(message, row + META_ROWS, spans[0])
    for message, span in zip(message_refs[QUART:], spans[1:]):
        put_hidden(message, 0, span)


def partial_kernel(owner_count, tok_rows, base, steps, plan_ref, *refs):
    totals = refs[-len(steps) :]
    heads = refs[: QUART * owner_count]
    tails = refs[: -len(steps)][-QUART * owner_count :]
    own_block, own_expert = place(owner_count)
    group, groups = lax.axis_index("dp"), lax.axis_size("dp")
    rows, block_width = totals[0].shape
    parts = block_width // LANES
    chunk = next(c for c in (128, 64, 32, 16) if rows % c == 0)
    bits = []
    for first in range(0, len(heads), 16):
        packed = jnp.zeros((META_ROWS, LANES), jnp.float32)
        for at, head in enumerate(heads[first : first + 16]):
            meta = head[parts * tok_rows : parts * tok_rows + META_ROWS, :]
            packed = packed + meta.astype(jnp.float32) * float(1 << at)
        bits.append(jnp.max(packed).astype(jnp.int32))
    for total in totals:
        total[...] = jnp.zeros_like(total)
    for at, (head, tail) in enumerate(zip(heads, tails)):
        step, mate = divmod(at, owner_count)
        source_expert = own_expert ^ mate
        source = lax.rem(own_block + QUART - step, QUART) * owner_count + source_expert
        is_replica = ((bits[at // 16] >> (at % 16)) & 1) == 1
        target = jnp.where(is_replica, plan_ref[source], source_expert)

        @pl.when(target == own_expert)
        def _():
            columns = jnp.concatenate(
                [head[p * tok_rows : (p + 1) * tok_rows, :] for p in range(parts)], axis=1
            )
            for total, ahead in zip(totals, steps):
                start = base + lax.rem(group + ahead, groups) * rows

                @pl.loop(0, rows // chunk)
                def _(i):
                    term = jnp.dot(
                        tail[pl.ds(pl.multiple_of(start + i * chunk, 16), chunk), :],
                        columns,
                        preferred_element_type=jnp.float32,
                    )
                    rounded = term.astype(jnp.bfloat16).astype(jnp.float32)
                    into = pl.ds(pl.multiple_of(i * chunk, 16), chunk)
                    total[into, :] += jnp.where(is_replica, rounded, term)


def update_kernel(parts, *refs):
    terms, (master, one, two) = refs[:parts], refs[parts : parts + 3]
    master_out, one_out, two_out, fresh = refs[-4:]
    gradient = terms[0][...]
    for term in terms[1:]:
        gradient = gradient + term[...]
    weights = master[...]
    first_next = beta_one * one[...] + (1.0 - beta_one) * gradient
    second_next = beta_two * two[...] + (1.0 - beta_two) * gradient * gradient
    scaled_first = first_next / (1.0 - beta_one**step_count)
    scaled_second = second_next / (1.0 - beta_two**step_count)
    direction = scaled_first / (jnp.sqrt(scaled_second) + epsilon)
    weights_next = weights - learn_rate * (direction + decay_rate * weights)
    master_out[...] = weights_next
    one_out[...] = first_next
    two_out[...] = second_next
    fresh[...] = weights_next.astype(jnp.bfloat16)


def update(terms, states, span, held):
    first, length = span
    rows, width = states[0].shape
    block = next(c for c in (128, 64, 32, 16) if first % c == 0 and length % c == 0)
    inside = pl.BlockSpec((block, width), lambda i: (i, 0))
    placed = pl.BlockSpec((block, width), lambda i: (i + first // block, 0))
    whole = jax.ShapeDtypeStruct((rows, width), jnp.float32)
    inputs = len(terms) + len(states)
    return pl.pallas_call(
        functools.partial(update_kernel, len(terms)),
        grid=(length // block,),
        out_shape=(whole, whole, whole, jax.ShapeDtypeStruct((length, width), jnp.bfloat16)),
        in_specs=[inside] * len(terms)
        + [placed] * len(states)
        + [pl.BlockSpec(memory_space=pl.ANY)] * len(held),
        out_specs=(placed, placed, placed, inside),
        input_output_aliases={inputs + i: i for i in range(len(held))},
        compiler_params=pltpu.CompilerParams(vmem_limit_bytes=24 << 20),
        cost_estimate=pl.CostEstimate(
            flops=20 * length * width, bytes_accessed=34 * length * width, transcendentals=0
        ),
    )(*terms, *states, *held)


def choose_kernel(owner_count, plan_ref, *refs):
    candidates, chosen = refs[:owner_count], refs[owner_count:]
    own_block, own_expert = place(owner_count)
    for step, out in enumerate(chosen):
        wanted = plan_ref[lax.rem(own_block + step, QUART) * owner_count + own_expert]
        for mate, candidate in enumerate(candidates):

            @pl.when(wanted == own_expert ^ mate)
            def _():
                out[...] = candidate[...]


def assemble_kernel(owner_count, spans, *refs):
    out = refs[-1]
    own_block, _ = place(owner_count)
    for at, block in enumerate(refs[:-1]):
        (first, length), step = spans[at // QUART], at % QUART
        width = block.shape[1]
        start = lax.rem(own_block + QUART - step, QUART) * width
        out[first : first + length, pl.ds(pl.multiple_of(start, LANES), width)] = block[...]


def after(value, *others):
    return lax.optimization_barrier((value, *others))[0]


def per_device(
    hidden_rows, grad_rows, block_slot, live_rows, replica_plan, master, moment_one, moment_two
):
    owner_count = lax.axis_size("expert") // QUART
    groups = lax.axis_size("dp")
    hidden_units, tok_rows = hidden_rows.shape
    block_width = grad_rows.shape[1] // QUART
    share_rows = hidden_units // groups
    assert block_slot.shape[1] == 1 and tok_rows == LANES and block_width % LANES == 0
    shape = jax.ShapeDtypeStruct
    lead = share_rows // 3
    spans = ((0, lead), (lead, share_rows - lead))

    head_rows = (block_width // LANES) * tok_rows + META_ROWS
    messages = call(
        functools.partial(message_kernel, owner_count, spans),
        [shape((head_rows + groups * lead, LANES), jnp.bfloat16)] * QUART
        + [shape((groups * length, LANES), jnp.bfloat16) for _, length in spans[1:]],
        (block_slot, live_rows),
        (hidden_rows, grad_rows),
    )
    outgoing = [messages[:QUART]] + [[m] * QUART for m in messages[QUART:]]
    gathered = []
    arrived = None
    for sent in outgoing:
        came = {0: sent[0]}
        for step in (1, 3, 2):
            block = sent[step]
            if step == 2:
                block = after(block, came[1], came[3])
            elif arrived is not None:
                block = after(block, arrived)
            came[step] = from_behind(block, "expert", step * owner_count)
        arrived = came[2]
        gathered.append(
            [b for s in range(QUART) for b in gather_mates(came[s], "expert", owner_count)]
        )

    states = (master[0], moment_one[0], moment_two[0])
    held, received = (), []
    ahead = tuple(range(1, groups))
    for at, (first, length) in enumerate(spans):
        tokens = gathered[0] if at == 0 else gathered[0] + gathered[at]

        def partials(steps):
            return call(
                functools.partial(
                    partial_kernel, owner_count, tok_rows, 0 if at else head_rows, steps
                ),
                [shape((length, block_width), jnp.float32)] * len(steps),
                (replica_plan,),
                tokens,
                2 * len(steps) * length * tok_rows * block_width * QUART,
            )

        far = [from_behind(p, "dp", step) for step, p in zip(ahead, partials(ahead))]
        near = partials((0,))
        *held, fresh = update((*near, *far), states, (first, length), held)
        chosen = call(
            functools.partial(choose_kernel, owner_count),
            [shape((length, block_width), jnp.bfloat16)] * QUART,
            (replica_plan,),
            gather_mates(fresh, "expert", owner_count),
        )
        received += [
            from_behind(block, "expert", step * owner_count) if step else block
            for step, block in enumerate(chosen)
        ]
    (replica_weight,) = call(
        functools.partial(assemble_kernel, owner_count, spans),
        [shape((share_rows, QUART * block_width), jnp.bfloat16)],
        (),
        received,
    )
    return (*(state[None] for state in held), replica_weight[None])


def solution(mesh):
    return jax.shard_map(
        per_device,
        mesh=mesh,
        in_specs=(
            P(None, ("dp", "expert")),
            P(("dp", "expert"), None),
            P(("dp", "expert"), None),
            P(("dp", "expert")),
            P(),
            P("expert", "dp", None),
            P("expert", "dp", None),
            P("expert", "dp", None),
        ),
        out_specs=(
            P("expert", "dp", None),
            P("expert", "dp", None),
            P("expert", "dp", None),
            P("expert", "dp", None),
        ),
        check_vma=False,
    )
```

```python
import functools

import jax
import jax.numpy as jnp
from jax import lax
from jax.experimental import pallas as pl
from jax.experimental.pallas import tpu as pltpu
from jax.sharding import PartitionSpec as P

QUART = 4
LANES = 128
META_ROWS = 16


beta_one = 0.9
beta_two = 0.95
learn_rate = 0.01
decay_rate = 0.1
epsilon = 1e-08
step_count = 10.0

VMEM = pl.BlockSpec(memory_space=pltpu.VMEM)
SMEM = pl.BlockSpec(memory_space=pltpu.SMEM)


def vmem_for(*arrays):
    return int(sum(a.size * a.dtype.itemsize for a in arrays) * 5 // 4) + (8 << 20)


def call(kernel, out_shapes, scalars, arrays, flops=0):
    moved = sum(a.size * a.dtype.itemsize for a in (*arrays, *out_shapes))
    return pl.pallas_call(
        kernel,
        out_shape=tuple(out_shapes),
        in_specs=[SMEM] * len(scalars) + [VMEM] * len(arrays),
        out_specs=tuple([VMEM] * len(out_shapes)),
        compiler_params=pltpu.CompilerParams(vmem_limit_bytes=vmem_for(*arrays, *out_shapes)),
        cost_estimate=pl.CostEstimate(flops=flops // 64, bytes_accessed=moved // 64, transcendentals=0),
    )(*scalars, *arrays)


def from_behind(block, axis, distance):
    devices = range(lax.axis_size(axis))
    route = [((i - distance) % len(devices), i) for i in devices]
    return lax.ppermute(block, axis, route)


def from_mate(block, axis, bit):
    return lax.ppermute(block, axis, [(i ^ bit, i) for i in range(lax.axis_size(axis))])


def gather_mates(block, axis, count, wait_for=()):
    held = {0: block}
    bit = count // 2
    while bit:
        held.update({m | bit: from_mate(held[m], axis, bit) for m in list(held)})
        if wait_for:
            held = {m: after(b, *wait_for) for m, b in held.items()}
        bit //= 2
    return [held[m] for m in range(count)]


def after(value, *others):
    return lax.optimization_barrier((value, *others))[0] if others else value


def place(owner_count):
    own = lax.axis_index("expert")
    return own // owner_count, own % owner_count


def message_kernel(owner_count, slot_ref, live_ref, hidden_ref, grad_ref, *message_refs):
    own_block, _ = place(owner_count)
    hidden_units, tok_rows = hidden_ref.shape
    block_width = grad_ref.shape[1] // QUART
    parts = block_width // LANES
    live = live_ref[0]
    slot = slot_ref[0, 0]
    kept = lax.broadcasted_iota(jnp.int32, (tok_rows, LANES), 0) < live
    meta = jnp.full((META_ROWS, LANES), slot.astype(jnp.float32)).astype(jnp.bfloat16)
    for step, message in enumerate(message_refs):
        target = lax.rem(own_block + step, QUART)
        for part in range(parts):
            start = pl.multiple_of(target * block_width + part * LANES, LANES)
            columns = grad_ref[:, pl.ds(start, LANES)].astype(jnp.float32)
            row = part * tok_rows
            message[row : row + tok_rows, :] = jnp.where(kept, columns, 0.0).astype(jnp.bfloat16)
        row = parts * tok_rows
        message[row : row + META_ROWS, :] = meta
        message[row + META_ROWS :, :] = hidden_ref[...]


def partial_kernel(owner_count, tok_rows, share_rows, first, steps, plan_ref, *refs):
    messages, totals = refs[: -len(steps)], refs[-len(steps) :]
    own_block, own_expert = place(owner_count)
    group, groups = lax.axis_index("dp"), lax.axis_size("dp")
    rows, block_width = totals[0].shape
    parts = block_width // LANES
    base = parts * tok_rows + META_ROWS + first
    chunk = next(c for c in (192, 128, 64, 48, 32, 16) if rows % c == 0)
    bits = []
    for start in range(0, len(messages), 16):
        packed = jnp.zeros((META_ROWS, LANES), jnp.float32)
        for at, message in enumerate(messages[start : start + 16]):
            meta = message[parts * tok_rows : parts * tok_rows + META_ROWS, :]
            packed = packed + meta.astype(jnp.float32) * float(1 << at)
        bits.append(jnp.max(packed).astype(jnp.int32))
    for total in totals:
        total[...] = jnp.zeros_like(total)
    for at, message in enumerate(messages):
        step, mate = divmod(at, owner_count)
        source_expert = own_expert ^ mate
        source = lax.rem(own_block + QUART - step, QUART) * owner_count + source_expert
        is_replica = ((bits[at // 16] >> (at % 16)) & 1) == 1
        target = jnp.where(is_replica, plan_ref[source], source_expert)

        @pl.when(target == own_expert)
        def _():
            columns = jnp.concatenate(
                [message[p * tok_rows : (p + 1) * tok_rows, :] for p in range(parts)], axis=1
            )
            for total, ahead in zip(totals, steps):
                start = base + lax.rem(group + ahead, groups) * share_rows

                @pl.loop(0, rows // chunk)
                def _(i):
                    term = jnp.dot(
                        message[pl.ds(pl.multiple_of(start + i * chunk, 16), chunk), :],
                        columns,
                        preferred_element_type=jnp.float32,
                    )
                    rounded = term.astype(jnp.bfloat16).astype(jnp.float32)
                    into = pl.ds(pl.multiple_of(i * chunk, 16), chunk)
                    total[into, :] += jnp.where(is_replica, rounded, term)


def update_kernel(parts, *refs):
    terms, (master, one, two) = refs[:parts], refs[parts : parts + 3]
    master_out, one_out, two_out, fresh = refs[-4:]
    gradient = terms[0][...]
    for term in terms[1:]:
        gradient = gradient + term[...]
    weights = master[...]
    first_next = beta_one * one[...] + (1.0 - beta_one) * gradient
    second_next = beta_two * two[...] + (1.0 - beta_two) * gradient * gradient
    scaled_first = first_next / (1.0 - beta_one**step_count)
    scaled_second = second_next / (1.0 - beta_two**step_count)
    direction = scaled_first / (jnp.sqrt(scaled_second) + epsilon)
    weights_next = weights - learn_rate * (direction + decay_rate * weights)
    master_out[...] = weights_next
    one_out[...] = first_next
    two_out[...] = second_next
    fresh[...] = weights_next.astype(jnp.bfloat16)


def update(terms, states, span, held):
    first, length = span
    rows, width = states[0].shape
    block = next(c for c in (128, 64, 32, 16) if first % c == 0 and length % c == 0)
    inside = pl.BlockSpec((block, width), lambda i: (i, 0))
    placed = pl.BlockSpec((block, width), lambda i: (i + first // block, 0))
    whole = jax.ShapeDtypeStruct((rows, width), jnp.float32)
    inputs = len(terms) + len(states)
    return pl.pallas_call(
        functools.partial(update_kernel, len(terms)),
        grid=(length // block,),
        out_shape=(whole, whole, whole, jax.ShapeDtypeStruct((length, width), jnp.bfloat16)),
        in_specs=[inside] * len(terms)
        + [placed] * len(states)
        + [pl.BlockSpec(memory_space=pl.ANY)] * len(held),
        out_specs=(placed, placed, placed, inside),
        input_output_aliases={inputs + i: i for i in range(len(held))},
        compiler_params=pltpu.CompilerParams(vmem_limit_bytes=24 << 20),
        cost_estimate=pl.CostEstimate(
            flops=length * width, bytes_accessed=length * width, transcendentals=0
        ),
    )(*terms, *states, *held)


def choose_kernel(owner_count, plan_ref, *refs):
    candidates, out = refs[:-1], refs[-1]
    _, own_expert = place(owner_count)
    for block in range(QUART):
        wanted = plan_ref[block * owner_count + own_expert]
        for mate, candidate in enumerate(candidates):

            @pl.when(wanted == own_expert ^ mate)
            def _():
                out[block] = candidate[...]


def assemble_kernel(spans, *refs):
    out = refs[-1]
    for (first, length), blocks in zip(spans, refs[:-1]):
        width = blocks.shape[2]
        for block in range(QUART):
            columns = slice(block * width, (block + 1) * width)
            out[first : first + length, columns] = blocks[block]


def per_device(
    hidden_rows, grad_rows, block_slot, live_rows, replica_plan, master, moment_one, moment_two
):
    owner_count = lax.axis_size("expert") // QUART
    groups = lax.axis_size("dp")
    hidden_units, tok_rows = hidden_rows.shape
    block_width = grad_rows.shape[1] // QUART
    share_rows = hidden_units // groups
    assert block_slot.shape[1] == 1 and tok_rows == LANES and block_width % LANES == 0
    shape = jax.ShapeDtypeStruct
    lead = share_rows // 2
    spans = ((0, lead), (lead, share_rows - lead))

    length = hidden_units + (block_width // LANES) * tok_rows + META_ROWS
    messages = call(
        functools.partial(message_kernel, owner_count),
        [shape((length, LANES), jnp.bfloat16)] * QUART,
        (block_slot, live_rows),
        (hidden_rows, grad_rows),
    )

    def across(block, step):
        return from_behind(block, "expert", step * owner_count) if step else block

    gathered = []
    for step, message in enumerate(messages):
        gathered += gather_mates(across(message, step), "expert", owner_count)

    def partials(at, steps, wait_for):
        first, rows = spans[at]
        return call(
            functools.partial(
                partial_kernel, owner_count, tok_rows, share_rows, first, steps
            ),
            [shape((rows, block_width), jnp.float32)] * len(steps),
            (after(replica_plan, *wait_for),),
            gathered,
            2 * len(steps) * rows * tok_rows * block_width * QUART,
        )

    columns_of = [
        [block * owner_count + expert for block in range(QUART)] for expert in range(owner_count)
    ]

    def spread(at, blocks):
        (chosen,) = call(
            functools.partial(choose_kernel, owner_count),
            [shape((QUART, spans[at][1], block_width), jnp.bfloat16)],
            (replica_plan,),
            blocks,
        )
        moved = lax.all_to_all(
            chosen, "expert", 0, 0, axis_index_groups=columns_of, tiled=True
        )
        return chosen, moved

    states = (master[0], moment_one[0], moment_two[0])
    ahead = tuple(range(1, groups))
    far, came, near, held, received, chosen = (), (), (), (), [], ()
    for at, span in enumerate(spans):
        far = partials(at, ahead, near)
        came = [from_behind(after(p, *came), "dp", step) for step, p in zip(ahead, far)]
        near = partials(at, (0,), far)
        arrived = [after(term, chosen) for term in came] if at else came
        *held, fresh = update((*near, *arrived), states, span, held)
        chosen, moved = spread(at, gather_mates(fresh, "expert", owner_count))
        received += [moved]
    (replica_weight,) = call(
        functools.partial(assemble_kernel, spans),
        [shape((share_rows, QUART * block_width), jnp.bfloat16)],
        (),
        received,
    )
    return (*(state[None] for state in held), replica_weight[None])


def solution(mesh):
    return jax.shard_map(
        per_device,
        mesh=mesh,
        in_specs=(
            P(None, ("dp", "expert")),
            P(("dp", "expert"), None),
            P(("dp", "expert"), None),
            P(("dp", "expert")),
            P(),
            P("expert", "dp", None),
            P("expert", "dp", None),
            P("expert", "dp", None),
        ),
        out_specs=(
            P("expert", "dp", None),
            P("expert", "dp", None),
            P("expert", "dp", None),
            P("expert", "dp", None),
        ),
        check_vma=False,
    )
```

```python
import functools

import jax
import jax.numpy as jnp
from jax import lax
from jax.experimental import pallas as pl
from jax.experimental.pallas import tpu as pltpu
from jax.sharding import PartitionSpec as P

QUART = 4
LANES = 128
META_ROWS = 16


beta_one = 0.9
beta_two = 0.95
learn_rate = 0.01
decay_rate = 0.1
epsilon = 1e-08
step_count = 10.0

VMEM = pl.BlockSpec(memory_space=pltpu.VMEM)
SMEM = pl.BlockSpec(memory_space=pltpu.SMEM)


def vmem_for(*arrays):
    return int(sum(a.size * a.dtype.itemsize for a in arrays) * 5 // 4) + (8 << 20)


def call(kernel, out_shapes, scalars, arrays, flops=0):
    moved = sum(a.size * a.dtype.itemsize for a in (*arrays, *out_shapes))
    return pl.pallas_call(
        kernel,
        out_shape=tuple(out_shapes),
        in_specs=[SMEM] * len(scalars) + [VMEM] * len(arrays),
        out_specs=tuple([VMEM] * len(out_shapes)),
        compiler_params=pltpu.CompilerParams(vmem_limit_bytes=vmem_for(*arrays, *out_shapes)),
        cost_estimate=pl.CostEstimate(flops=flops // 64, bytes_accessed=moved // 64, transcendentals=0),
    )(*scalars, *arrays)


def from_behind(block, axis, distance):
    devices = range(lax.axis_size(axis))
    route = [((i - distance) % len(devices), i) for i in devices]
    return lax.ppermute(block, axis, route)


def from_mate(block, axis, bit):
    return lax.ppermute(block, axis, [(i ^ bit, i) for i in range(lax.axis_size(axis))])


def gather_mates(block, axis, count, least=1):
    held = {0: block}
    bit = count // 2
    while bit >= least:
        held.update({m | bit: from_mate(held[m], axis, bit) for m in list(held)})
        bit //= 2
    return [held.get(m) for m in range(count)]


def after(value, *others):
    return lax.optimization_barrier((value, *others))[0] if others else value


def place(owner_count):
    own = lax.axis_index("expert")
    return own // owner_count, own % owner_count


def message_kernel(owner_count, slot_ref, live_ref, hidden_ref, grad_ref, *message_refs):
    own_block, _ = place(owner_count)
    hidden_units, tok_rows = hidden_ref.shape
    block_width = grad_ref.shape[1] // QUART
    parts = block_width // LANES
    live = live_ref[0]
    slot = slot_ref[0, 0]
    kept = lax.broadcasted_iota(jnp.int32, (tok_rows, LANES), 0) < live
    meta = jnp.full((META_ROWS, LANES), slot.astype(jnp.float32)).astype(jnp.bfloat16)
    for step, message in enumerate(message_refs):
        target = lax.rem(own_block + step, QUART)
        for part in range(parts):
            start = pl.multiple_of(target * block_width + part * LANES, LANES)
            columns = grad_ref[:, pl.ds(start, LANES)].astype(jnp.float32)
            row = part * tok_rows
            message[row : row + tok_rows, :] = jnp.where(kept, columns, 0.0).astype(jnp.bfloat16)
        row = parts * tok_rows
        message[row : row + META_ROWS, :] = meta
        message[row + META_ROWS :, :] = hidden_ref[...]


def partial_kernel(owner_count, tok_rows, share_rows, first, steps, plan_ref, *refs):
    messages, totals = refs[: -len(steps)], refs[-len(steps) :]
    own_block, own_expert = place(owner_count)
    group, groups = lax.axis_index("dp"), lax.axis_size("dp")
    rows, block_width = totals[0].shape
    parts = block_width // LANES
    base = parts * tok_rows + META_ROWS + first
    chunk = next(c for c in (192, 160, 128, 112, 96, 64, 48, 32, 16) if rows % c == 0)
    bits = []
    for start in range(0, len(messages), 16):
        packed = jnp.zeros((META_ROWS, LANES), jnp.float32)
        for at, message in enumerate(messages[start : start + 16]):
            meta = message[parts * tok_rows : parts * tok_rows + META_ROWS, :]
            packed = packed + meta.astype(jnp.float32) * float(1 << at)
        bits.append(jnp.max(packed).astype(jnp.int32))
    for total in totals:
        total[...] = jnp.zeros_like(total)
    for at, message in enumerate(messages):
        step, mate = divmod(at, owner_count)
        source_expert = own_expert ^ mate
        source = lax.rem(own_block + QUART - step, QUART) * owner_count + source_expert
        is_replica = ((bits[at // 16] >> (at % 16)) & 1) == 1
        target = jnp.where(is_replica, plan_ref[source], source_expert)

        @pl.when(target == own_expert)
        def _():
            columns = jnp.concatenate(
                [message[p * tok_rows : (p + 1) * tok_rows, :] for p in range(parts)], axis=1
            )
            for total, ahead in zip(totals, steps):
                start = base + lax.rem(group + ahead, groups) * share_rows

                @pl.loop(0, rows // chunk)
                def _(i):
                    term = jnp.dot(
                        message[pl.ds(pl.multiple_of(start + i * chunk, 16), chunk), :],
                        columns,
                        preferred_element_type=jnp.float32,
                    )
                    rounded = term.astype(jnp.bfloat16).astype(jnp.float32)
                    into = pl.ds(pl.multiple_of(i * chunk, 16), chunk)
                    total[into, :] += jnp.where(is_replica, rounded, term)


def update_kernel(parts, held, span, block, *refs):
    terms, (master, one, two) = refs[:parts], refs[parts : parts + 3]
    *outs, fresh, new_rows, sems = refs[parts + 3 + held :]
    first, length = span
    copies = []
    for at in range(length // block):
        inside, placed = pl.ds(at * block, block), pl.ds(first + at * block, block)
        gradient = terms[0][inside, :]
        for term in terms[1:]:
            gradient = gradient + term[inside, :]
        weights = master[placed, :]
        first_next = beta_one * one[placed, :] + (1.0 - beta_one) * gradient
        second_next = beta_two * two[placed, :] + (1.0 - beta_two) * gradient * gradient
        scaled_first = first_next / (1.0 - beta_one**step_count)
        scaled_second = second_next / (1.0 - beta_two**step_count)
        direction = scaled_first / (jnp.sqrt(scaled_second) + epsilon)
        weights_next = weights - learn_rate * (direction + decay_rate * weights)
        fresh[inside, :] = weights_next.astype(jnp.bfloat16)
        for which, value in enumerate((weights_next, first_next, second_next)):
            new_rows[which, inside, :] = value
            copies.append(
                pltpu.make_async_copy(
                    new_rows.at[which, inside, :], outs[which].at[placed, :], sems.at[which, at]
                )
            )
            copies[-1].start()
    for copy in copies:
        copy.wait()


def update(terms, states, span, held):
    length = span[1]
    rows, width = states[0].shape
    block = next(c for c in (64, 48, 32, 16) if length % c == 0)
    whole = jax.ShapeDtypeStruct((rows, width), jnp.float32)
    anywhere = pl.BlockSpec(memory_space=pl.ANY)
    inputs = len(terms) + len(states)
    return pl.pallas_call(
        functools.partial(update_kernel, len(terms), len(held), span, block),
        out_shape=(whole, whole, whole, jax.ShapeDtypeStruct((length, width), jnp.bfloat16)),
        in_specs=[VMEM] * inputs + [anywhere] * len(held),
        out_specs=(anywhere, anywhere, anywhere, VMEM),
        scratch_shapes=[
            pltpu.VMEM((3, length, width), jnp.float32),
            pltpu.SemaphoreType.DMA((3, length // block)),
        ],
        input_output_aliases={inputs + i: i for i in range(len(held))},
        compiler_params=pltpu.CompilerParams(vmem_limit_bytes=24 << 20),
        cost_estimate=pl.CostEstimate(
            flops=length * width, bytes_accessed=length * width, transcendentals=0
        ),
    )(*terms, *states, *held)


def choose_kernel(owner_count, plan_ref, *refs):
    candidates, chosen = refs[:owner_count], refs[owner_count:]
    own_block, own_expert = place(owner_count)
    for step, out in enumerate(chosen):
        wanted = plan_ref[lax.rem(own_block + step, QUART) * owner_count + own_expert]
        for mate, candidate in enumerate(candidates):

            @pl.when(wanted == own_expert ^ mate)
            def _():
                out[...] = candidate[...]


def offer_kernel(owner_count, plan_ref, *refs):
    held, out = refs[:-1], refs[-1]
    own_block, own_expert = place(owner_count)
    wanted = plan_ref[own_block * owner_count + (own_expert ^ 1)]
    half = owner_count // 2
    rows = held[0].shape[0]
    for pair in range(half):

        @pl.when((wanted ^ own_expert) >> 1 == pair)
        def _():
            out[0] = held[pair][...]
            for step in range(1, QUART):
                out[step] = held[half + pair][(step - 1) * rows : step * rows, :]


def assemble_kernel(owner_count, spans, plan_ref, *refs):
    half = owner_count // 2
    near, far, offered = refs[:half], refs[half : 2 * half], refs[2 * half]
    received, out = refs[2 * half + 1 : -1], refs[-1]
    own_block, own_expert = place(owner_count)
    apart = plan_ref[own_block * owner_count + own_expert] ^ own_expert
    width = offered.shape[2]
    (first, rows), (later, later_rows) = spans
    for step in range(QUART):
        start = pl.multiple_of(lax.rem(own_block + QUART - step, QUART) * width, LANES)
        out[later : later + later_rows, pl.ds(start, width)] = received[step][...]

        @pl.when(apart & 1 == 1)
        def _():
            out[first : first + rows, pl.ds(start, width)] = offered[step]

        for pair in range(half):

            @pl.when(apart == 2 * pair)
            def _():
                source = far[pair] if step else near[pair]
                at = pl.ds(max(step - 1, 0) * rows, rows)
                out[first : first + rows, pl.ds(start, width)] = source[at, :]


def per_device(
    hidden_rows, grad_rows, block_slot, live_rows, replica_plan, master, moment_one, moment_two
):
    owner_count = lax.axis_size("expert") // QUART
    groups = lax.axis_size("dp")
    hidden_units, tok_rows = hidden_rows.shape
    block_width = grad_rows.shape[1] // QUART
    share_rows = hidden_units // groups
    assert block_slot.shape[1] == 1 and tok_rows == LANES and block_width % LANES == 0
    shape = jax.ShapeDtypeStruct
    lead = share_rows * 7 // 12 // 16 * 16
    spans = ((0, lead), (lead, share_rows - lead))

    length = hidden_units + (block_width // LANES) * tok_rows + META_ROWS
    messages = call(
        functools.partial(message_kernel, owner_count),
        [shape((length, LANES), jnp.bfloat16)] * QUART,
        (block_slot, live_rows),
        (hidden_rows, grad_rows),
    )

    def across(block, step):
        return from_behind(block, "expert", step * owner_count) if step else block

    gathered = []
    for step, message in enumerate(messages):
        gathered += gather_mates(across(message, step), "expert", owner_count)

    def partials(at, steps, wait_for):
        first, rows = spans[at]
        return call(
            functools.partial(
                partial_kernel, owner_count, tok_rows, share_rows, first, steps
            ),
            [shape((rows, block_width), jnp.float32)] * len(steps),
            (after(replica_plan, *wait_for),),
            gathered,
            2 * len(steps) * rows * tok_rows * block_width * QUART,
        )

    states = (master[0], moment_one[0], moment_two[0])
    ahead = tuple(range(1, groups))
    block = lambda rows: shape((rows, block_width), jnp.bfloat16)

    far_one = partials(0, ahead, ())
    came_one = [from_behind(p, "dp", step) for step, p in zip(ahead, far_one)]
    far_two = partials(1, ahead, far_one)
    near_one = partials(0, (0,), far_two)
    near_two = partials(1, (0,), near_one)
    came_one = [after(term, *near_two) for term in came_one]
    came_two = [
        from_behind(after(p, *came_one), "dp", step) for step, p in zip(ahead, far_two)
    ]
    *held, fresh_one = update((*near_one, *came_one), states, spans[0], ())

    lines = [across(fresh_one, step) for step in range(QUART)]

    came_two = [after(term, fresh_one) for term in came_two]
    *held, fresh_two = update((*near_two, *came_two), states, spans[1], held)

    mates_two = gather_mates(fresh_two, "expert", owner_count)
    near_wide = gather_mates(fresh_one, "expert", owner_count, 2)[::2]
    crossed = mates_two[owner_count // 2], near_wide[-1]
    lines[1:] = [after(line, *crossed) for line in lines[1:]]
    chosen = call(
        functools.partial(choose_kernel, owner_count),
        [block(spans[1][1])] * QUART,
        (after(replica_plan, *lines),),
        mates_two,
    )
    received = [across(c, step) for step, c in enumerate(chosen)]

    stacked = jnp.concatenate(lines[1:])
    far_wide = gather_mates(stacked, "expert", owner_count, 2)[::2]
    (offer,) = call(
        functools.partial(offer_kernel, owner_count),
        [shape((QUART, spans[0][1], block_width), jnp.bfloat16)],
        (after(replica_plan, *received[1:]),),
        (*near_wide, *far_wide),
    )
    (replica_weight,) = call(
        functools.partial(assemble_kernel, owner_count, spans),
        [shape((share_rows, QUART * block_width), jnp.bfloat16)],
        (replica_plan,),
        (*near_wide, *far_wide, from_mate(offer, "expert", 1), *received),
    )
    return (*(state[None] for state in held), replica_weight[None])


def solution(mesh):
    return jax.shard_map(
        per_device,
        mesh=mesh,
        in_specs=(
            P(None, ("dp", "expert")),
            P(("dp", "expert"), None),
            P(("dp", "expert"), None),
            P(("dp", "expert")),
            P(),
            P("expert", "dp", None),
            P("expert", "dp", None),
            P("expert", "dp", None),
        ),
        out_specs=(
            P("expert", "dp", None),
            P("expert", "dp", None),
            P("expert", "dp", None),
            P("expert", "dp", None),
        ),
        check_vma=False,
    )
```

```python
import functools

import jax
import jax.numpy as jnp
from jax import lax
from jax.experimental import pallas as pl
from jax.experimental.pallas import tpu as pltpu
from jax.sharding import PartitionSpec as P

QUART = 4
LANES = 128
META_ROWS = 16


beta_one = 0.9
beta_two = 0.95
learn_rate = 0.01
decay_rate = 0.1
epsilon = 1e-08
step_count = 10.0

VMEM = pl.BlockSpec(memory_space=pltpu.VMEM)
SMEM = pl.BlockSpec(memory_space=pltpu.SMEM)


def vmem_for(*arrays):
    return int(sum(a.size * a.dtype.itemsize for a in arrays) * 5 // 4) + (8 << 20)


def call(kernel, out_shapes, scalars, arrays, flops=0):
    moved = sum(a.size * a.dtype.itemsize for a in (*arrays, *out_shapes))
    return pl.pallas_call(
        kernel,
        out_shape=tuple(out_shapes),
        in_specs=[SMEM] * len(scalars) + [VMEM] * len(arrays),
        out_specs=tuple([VMEM] * len(out_shapes)),
        compiler_params=pltpu.CompilerParams(vmem_limit_bytes=vmem_for(*arrays, *out_shapes)),
        cost_estimate=pl.CostEstimate(flops=flops // 64, bytes_accessed=moved // 64, transcendentals=0),
    )(*scalars, *arrays)


def from_behind(block, axis, distance):
    devices = range(lax.axis_size(axis))
    route = [((i - distance) % len(devices), i) for i in devices]
    return lax.ppermute(block, axis, route)


def from_mate(block, axis, bit):
    return lax.ppermute(block, axis, [(i ^ bit, i) for i in range(lax.axis_size(axis))])


def gather_mates(block, axis, count, least=1):
    held = {0: block}
    bit = count // 2
    while bit >= least:
        held.update({m | bit: from_mate(held[m], axis, bit) for m in list(held)})
        bit //= 2
    return [held.get(m) for m in range(count)]


def after(value, *others):
    return lax.optimization_barrier((value, *others))[0] if others else value


def exchange(packs, bit):
    keys = [(step, mate | bit) for pack, _ in packs for step, mate in pack]
    blocks = [block for _, block in packs]
    return keys, from_mate(jnp.concatenate(blocks) if len(blocks) > 1 else blocks[0], "expert", bit)


def places(packs, first):
    found = {}
    for at, (keys, block) in enumerate(packs):
        rows = block.shape[0] // len(keys)
        found.update({key: (first + at, i * rows) for i, key in enumerate(keys)})
    return found


def place(owner_count):
    own = lax.axis_index("expert")
    return own // owner_count, own % owner_count


def message_kernel(owner_count, spans, slot_ref, live_ref, hidden_ref, grad_ref, *message_refs):
    own_block, _ = place(owner_count)
    groups = lax.axis_size("dp")
    hidden_units, tok_rows = hidden_ref.shape
    share_rows = hidden_units // groups
    block_width = grad_ref.shape[1] // QUART
    parts = block_width // LANES
    live = live_ref[0]
    slot = slot_ref[0, 0]
    kept = lax.broadcasted_iota(jnp.int32, (tok_rows, LANES), 0) < live
    meta = jnp.full((META_ROWS, LANES), slot.astype(jnp.float32)).astype(jnp.bfloat16)

    def put_hidden(message, row, span):
        first, length = span
        for group in range(groups):
            start = group * share_rows + first
            message[row : row + length, :] = hidden_ref[start : start + length, :]
            row += length

    for step, message in enumerate(message_refs[:QUART]):
        target = lax.rem(own_block + step, QUART)
        for part in range(parts):
            start = pl.multiple_of(target * block_width + part * LANES, LANES)
            columns = grad_ref[:, pl.ds(start, LANES)].astype(jnp.float32)
            row = part * tok_rows
            message[row : row + tok_rows, :] = jnp.where(kept, columns, 0.0).astype(jnp.bfloat16)
        row = parts * tok_rows
        message[row : row + META_ROWS, :] = meta
        put_hidden(message, row + META_ROWS, spans[0])
    for message, span in zip(message_refs[QUART:], spans[1:]):
        put_hidden(message, 0, span)


def partial_kernel(owner_count, tok_rows, where, base, steps, plan_ref, *refs):
    totals = refs[-len(steps) :]
    own_block, own_expert = place(owner_count)
    group, groups = lax.axis_index("dp"), lax.axis_size("dp")
    rows, block_width = totals[0].shape
    parts = block_width // LANES
    chunk = next(c for c in (192, 160, 128, 112, 96, 64, 48, 32, 16) if rows % c == 0)
    bits = []
    for first in range(0, len(where), 16):
        packed = jnp.zeros((META_ROWS, LANES), jnp.float32)
        for at, (_, (head, row), _) in enumerate(where[first : first + 16]):
            meta = refs[head][row + parts * tok_rows : row + parts * tok_rows + META_ROWS, :]
            packed = packed + meta.astype(jnp.float32) * float(1 << at)
        bits.append(jnp.max(packed).astype(jnp.int32))
    for total in totals:
        total[...] = jnp.zeros_like(total)
    for at, ((step, mate), (head, head_row), (tail, tail_row)) in enumerate(where):
        source_expert = own_expert ^ mate
        source = lax.rem(own_block + QUART - step, QUART) * owner_count + source_expert
        is_replica = ((bits[at // 16] >> (at % 16)) & 1) == 1
        target = jnp.where(is_replica, plan_ref[source], source_expert)

        @pl.when(target == own_expert)
        def _():
            columns = jnp.concatenate(
                [
                    refs[head][head_row + p * tok_rows : head_row + (p + 1) * tok_rows, :]
                    for p in range(parts)
                ],
                axis=1,
            )
            for total, ahead in zip(totals, steps):
                start = tail_row + base + lax.rem(group + ahead, groups) * rows

                @pl.loop(0, rows // chunk)
                def _(i):
                    term = jnp.dot(
                        refs[tail][pl.ds(pl.multiple_of(start + i * chunk, 16), chunk), :],
                        columns,
                        preferred_element_type=jnp.float32,
                    )
                    rounded = term.astype(jnp.bfloat16).astype(jnp.float32)
                    into = pl.ds(pl.multiple_of(i * chunk, 16), chunk)
                    total[into, :] += jnp.where(is_replica, rounded, term)


def update_kernel(parts, held, span, block, *refs):
    terms, (master, one, two) = refs[:parts], refs[parts : parts + 3]
    *outs, fresh, new_rows, sems = refs[parts + 3 + held :]
    first, length = span
    copies = []
    for at in range(length // block):
        inside, placed = pl.ds(at * block, block), pl.ds(first + at * block, block)
        gradient = terms[0][inside, :]
        for term in terms[1:]:
            gradient = gradient + term[inside, :]
        weights = master[placed, :]
        first_next = beta_one * one[placed, :] + (1.0 - beta_one) * gradient
        second_next = beta_two * two[placed, :] + (1.0 - beta_two) * gradient * gradient
        scaled_first = first_next / (1.0 - beta_one**step_count)
        scaled_second = second_next / (1.0 - beta_two**step_count)
        direction = scaled_first / (jnp.sqrt(scaled_second) + epsilon)
        weights_next = weights - learn_rate * (direction + decay_rate * weights)
        fresh[inside, :] = weights_next.astype(jnp.bfloat16)
        for which, value in enumerate((weights_next, first_next, second_next)):
            new_rows[which, inside, :] = value
            copies.append(
                pltpu.make_async_copy(
                    new_rows.at[which, inside, :], outs[which].at[placed, :], sems.at[which, at]
                )
            )
            copies[-1].start()
    for copy in copies:
        copy.wait()


def update(terms, states, span, held):
    length = span[1]
    rows, width = states[0].shape
    block = next(c for c in (64, 48, 32, 16) if length % c == 0)
    whole = jax.ShapeDtypeStruct((rows, width), jnp.float32)
    anywhere = pl.BlockSpec(memory_space=pl.ANY)
    inputs = len(terms) + len(states)
    return pl.pallas_call(
        functools.partial(update_kernel, len(terms), len(held), span, block),
        out_shape=(whole, whole, whole, jax.ShapeDtypeStruct((length, width), jnp.bfloat16)),
        in_specs=[VMEM] * inputs + [anywhere] * len(held),
        out_specs=(anywhere, anywhere, anywhere, VMEM),
        scratch_shapes=[
            pltpu.VMEM((3, length, width), jnp.float32),
            pltpu.SemaphoreType.DMA((3, length // block)),
        ],
        input_output_aliases={inputs + i: i for i in range(len(held))},
        compiler_params=pltpu.CompilerParams(vmem_limit_bytes=24 << 20),
        cost_estimate=pl.CostEstimate(
            flops=length * width, bytes_accessed=length * width, transcendentals=0
        ),
    )(*terms, *states, *held)


def choose_kernel(owner_count, plan_ref, *refs):
    candidates, chosen = refs[:owner_count], refs[owner_count:]
    own_block, own_expert = place(owner_count)
    for step, out in enumerate(chosen):
        wanted = plan_ref[lax.rem(own_block + step, QUART) * owner_count + own_expert]
        for mate, candidate in enumerate(candidates):

            @pl.when(wanted == own_expert ^ mate)
            def _():
                out[...] = candidate[...]


def offer_kernel(owner_count, plan_ref, *refs):
    held, out = refs[:-1], refs[-1]
    own_block, own_expert = place(owner_count)
    wanted = plan_ref[own_block * owner_count + (own_expert ^ 1)]
    half = owner_count // 2
    rows = held[0].shape[0]
    for pair in range(half):

        @pl.when((wanted ^ own_expert) >> 1 == pair)
        def _():
            out[0] = held[pair][...]
            for step in range(1, QUART):
                out[step] = held[half + pair][(step - 1) * rows : step * rows, :]


def assemble_kernel(owner_count, spans, plan_ref, *refs):
    half = owner_count // 2
    near, far, offered = refs[:half], refs[half : 2 * half], refs[2 * half]
    received, out = refs[2 * half + 1 : -1], refs[-1]
    own_block, own_expert = place(owner_count)
    apart = plan_ref[own_block * owner_count + own_expert] ^ own_expert
    width = offered.shape[2]
    (first, rows), (later, later_rows) = spans
    for step in range(QUART):
        start = pl.multiple_of(lax.rem(own_block + QUART - step, QUART) * width, LANES)
        out[later : later + later_rows, pl.ds(start, width)] = received[step][...]

        @pl.when(apart & 1 == 1)
        def _():
            out[first : first + rows, pl.ds(start, width)] = offered[step]

        for pair in range(half):

            @pl.when(apart == 2 * pair)
            def _():
                source = far[pair] if step else near[pair]
                at = pl.ds(max(step - 1, 0) * rows, rows)
                out[first : first + rows, pl.ds(start, width)] = source[at, :]


def per_device(
    hidden_rows, grad_rows, block_slot, live_rows, replica_plan, master, moment_one, moment_two
):
    owner_count = lax.axis_size("expert") // QUART
    groups = lax.axis_size("dp")
    hidden_units, tok_rows = hidden_rows.shape
    block_width = grad_rows.shape[1] // QUART
    share_rows = hidden_units // groups
    assert block_slot.shape[1] == 1 and tok_rows == LANES and block_width % LANES == 0
    shape = jax.ShapeDtypeStruct
    lead = share_rows * 7 // 12 // 16 * 16
    spans = ((0, lead), (lead, share_rows - lead))

    head_rows = (block_width // LANES) * tok_rows + META_ROWS
    messages = call(
        functools.partial(message_kernel, owner_count, spans),
        [shape((head_rows + groups * lead, LANES), jnp.bfloat16)] * QUART
        + [shape((groups * (share_rows - lead), LANES), jnp.bfloat16)],
        (block_slot, live_rows),
        (hidden_rows, grad_rows),
    )

    def across(block, step):
        return from_behind(block, "expert", step * owner_count) if step else block

    first_bit = owner_count // 2
    other_bits = [1 << i for i in reversed(range(first_bit.bit_length() - 1))]
    own = [([(0, 0)], messages[0])]
    sides = [([(step, 0)], across(messages[step], step)) for step in (1, 3)]
    own += [exchange(own, first_bit)]
    last = across(after(messages[2], *(block for _, block in sides)), 2)
    crossed = [exchange(sides, first_bit)]
    own += sides
    for bit in other_bits:
        own += [exchange(own, bit)]
    later = after(messages[QUART], last)
    rest = [([(0, 0)], messages[QUART])]
    rest += [([(step, 0)], across(later, step)) for step in (1, 2, 3)]
    last = [([(2, 0)], last)]
    crossed_last = exchange(last, first_bit)
    crossed_last = crossed_last[0], after(crossed_last[1], *(block for _, block in rest[1:]))
    token_groups = [[*crossed, *last, crossed_last]]
    rest = [(sum((keys for keys, _ in rest), []), jnp.concatenate([block for _, block in rest]))]
    rest += [exchange(rest, first_bit)]
    for group in token_groups:
        for bit in other_bits:
            group += [exchange(group, bit)]
    heads = sum(token_groups, own)
    rests = [[pack] for pack in rest]
    for group in rests:
        for bit in other_bits:
            group += [exchange(group, bit)]
    rests = sum(rests, [])
    head_at, rest_at = places(heads, 0), places(rests, len(heads))

    def partials(at, steps, wait_for):
        rows = spans[at][1]
        packs = heads + rests if at else heads
        where = [(key, found, rest_at[key] if at else found) for key, found in head_at.items()]
        return call(
            functools.partial(
                partial_kernel, owner_count, tok_rows, where, 0 if at else head_rows, steps
            ),
            [shape((rows, block_width), jnp.float32)] * len(steps),
            (after(replica_plan, *wait_for),),
            [block for _, block in packs],
            2 * len(steps) * rows * tok_rows * block_width * QUART,
        )

    states = (master[0], moment_one[0], moment_two[0])
    ahead = tuple(range(1, groups))
    block = lambda rows: shape((rows, block_width), jnp.bfloat16)

    far_one = partials(0, ahead, ())
    came_one = [from_behind(p, "dp", step) for step, p in zip(ahead, far_one)]
    near_one = partials(0, (0,), far_one)
    far_two = partials(1, ahead, near_one)
    near_two = partials(1, (0,), far_two)
    came_one = [after(term, *near_two) for term in came_one]
    came_two = [
        from_behind(after(p, *came_one), "dp", step) for step, p in zip(ahead, far_two)
    ]
    *held, fresh_one = update((*near_one, *came_one), states, spans[0], ())

    lines = [across(fresh_one, step) for step in range(QUART)]

    came_two = [after(term, fresh_one) for term in came_two]
    *held, fresh_two = update((*near_two, *came_two), states, spans[1], held)

    mates_two = gather_mates(fresh_two, "expert", owner_count)
    near_wide = gather_mates(fresh_one, "expert", owner_count, 2)[::2]
    crossed = mates_two[owner_count // 2], near_wide[-1]
    lines[1:] = [after(line, *crossed) for line in lines[1:]]
    chosen = call(
        functools.partial(choose_kernel, owner_count),
        [block(spans[1][1])] * QUART,
        (after(replica_plan, *lines),),
        mates_two,
    )
    received = [across(c, step) for step, c in enumerate(chosen)]

    stacked = jnp.concatenate(lines[1:])
    far_wide = gather_mates(stacked, "expert", owner_count, 2)[::2]
    (offer,) = call(
        functools.partial(offer_kernel, owner_count),
        [shape((QUART, spans[0][1], block_width), jnp.bfloat16)],
        (after(replica_plan, *received[1:]),),
        (*near_wide, *far_wide),
    )
    (replica_weight,) = call(
        functools.partial(assemble_kernel, owner_count, spans),
        [shape((share_rows, QUART * block_width), jnp.bfloat16)],
        (replica_plan,),
        (*near_wide, *far_wide, from_mate(offer, "expert", 1), *received),
    )
    return (*(state[None] for state in held), replica_weight[None])


def solution(mesh):
    return jax.shard_map(
        per_device,
        mesh=mesh,
        in_specs=(
            P(None, ("dp", "expert")),
            P(("dp", "expert"), None),
            P(("dp", "expert"), None),
            P(("dp", "expert")),
            P(),
            P("expert", "dp", None),
            P("expert", "dp", None),
            P("expert", "dp", None),
        ),
        out_specs=(
            P("expert", "dp", None),
            P("expert", "dp", None),
            P("expert", "dp", None),
            P("expert", "dp", None),
        ),
        check_vma=False,
    )
```

```python
import functools

import jax
import jax.numpy as jnp
from jax import lax
from jax.experimental import pallas as pl
from jax.experimental.pallas import tpu as pltpu
from jax.sharding import PartitionSpec as P

QUART = 4
LANES = 128
META_ROWS = 16


beta_one = 0.9
beta_two = 0.95
learn_rate = 0.01
decay_rate = 0.1
epsilon = 1e-08
step_count = 10.0

VMEM = pl.BlockSpec(memory_space=pltpu.VMEM)
SMEM = pl.BlockSpec(memory_space=pltpu.SMEM)
ANYWHERE = pl.BlockSpec(memory_space=pl.ANY)


def vmem_for(*arrays):
    return int(sum(a.size * a.dtype.itemsize for a in arrays) * 5 // 4) + (8 << 20)


def call(kernel, out_shapes, scalars, arrays, flops=0):
    moved = sum(a.size * a.dtype.itemsize for a in (*arrays, *out_shapes))
    return pl.pallas_call(
        kernel,
        out_shape=tuple(out_shapes),
        in_specs=[SMEM] * len(scalars) + [VMEM] * len(arrays),
        out_specs=tuple([VMEM] * len(out_shapes)),
        compiler_params=pltpu.CompilerParams(vmem_limit_bytes=vmem_for(*arrays, *out_shapes)),
        cost_estimate=pl.CostEstimate(flops=flops // 64, bytes_accessed=moved // 64, transcendentals=0),
    )(*scalars, *arrays)


def from_behind(block, axis, distance):
    devices = range(lax.axis_size(axis))
    route = [((i - distance) % len(devices), i) for i in devices]
    return lax.ppermute(block, axis, route)


def from_mate(block, axis, bit):
    return lax.ppermute(block, axis, [(i ^ bit, i) for i in range(lax.axis_size(axis))])


def gather_mates(block, axis, count, least=1):
    held = {0: block}
    bit = count // 2
    while bit >= least:
        held.update({m | bit: from_mate(held[m], axis, bit) for m in list(held)})
        bit //= 2
    return [held.get(m) for m in range(count)]


def after(value, *others):
    return lax.optimization_barrier((value, *others))[0] if others else value


def exchange(packs, bit):
    keys = [(step, mate | bit) for pack, _ in packs for step, mate in pack]
    blocks = [block for _, block in packs]
    return keys, from_mate(jnp.concatenate(blocks) if len(blocks) > 1 else blocks[0], "expert", bit)


def places(packs, first):
    found = {}
    for at, (keys, block) in enumerate(packs):
        rows = block.shape[0] // len(keys)
        found.update({key: (first + at, i * rows) for i, key in enumerate(keys)})
    return found


def place(owner_count):
    own = lax.axis_index("expert")
    return own // owner_count, own % owner_count


def message_kernel(owner_count, slot_ref, live_ref, hidden_hbm, grad_hbm, *refs):
    *message_refs, hidden_ref, grad_ref, sems = refs
    loads = [
        pltpu.make_async_copy(hidden_hbm, hidden_ref, sems.at[0]),
        pltpu.make_async_copy(grad_hbm, grad_ref, sems.at[1]),
    ]
    for load in loads:
        load.start()
    for load in loads:
        load.wait()
    own_block, _ = place(owner_count)
    hidden_units, tok_rows = hidden_ref.shape
    block_width = grad_ref.shape[1] // QUART
    parts = block_width // LANES
    live = live_ref[0]
    slot = slot_ref[0, 0]
    kept = lax.broadcasted_iota(jnp.int32, (tok_rows, LANES), 0) < live
    meta = jnp.full((META_ROWS, LANES), slot.astype(jnp.float32)).astype(jnp.bfloat16)

    for step, message in enumerate(message_refs):
        target = lax.rem(own_block + step, QUART)
        for part in range(parts):
            start = pl.multiple_of(target * block_width + part * LANES, LANES)
            columns = grad_ref[:, pl.ds(start, LANES)].astype(jnp.float32)
            row = part * tok_rows
            message[row : row + tok_rows, :] = jnp.where(kept, columns, 0.0).astype(jnp.bfloat16)
        row = parts * tok_rows
        message[row : row + META_ROWS, :] = meta
        message[row + META_ROWS :, :] = hidden_ref[...]


def partial_kernel(owner_count, tok_rows, share_rows, where, base, steps, plan_ref, *refs):
    totals = refs[-len(steps) :]
    own_block, own_expert = place(owner_count)
    group, groups = lax.axis_index("dp"), lax.axis_size("dp")
    rows, block_width = totals[0].shape
    parts = block_width // LANES
    chunk = next(c for c in (208, 192, 176, 128, 112, 96, 64, 48, 32, 16) if rows % c == 0)
    bits = []
    for first in range(0, len(where), 16):
        packed = jnp.zeros((META_ROWS, LANES), jnp.float32)
        for at, (_, (ref, row)) in enumerate(where[first : first + 16]):
            meta = refs[ref][row + parts * tok_rows : row + parts * tok_rows + META_ROWS, :]
            packed = packed + meta.astype(jnp.float32) * float(1 << at)
        bits.append(jnp.max(packed).astype(jnp.int32))
    for total in totals:
        total[...] = jnp.zeros_like(total)
    for at, ((step, mate), (ref, row)) in enumerate(where):
        source_expert = own_expert ^ mate
        source = lax.rem(own_block + QUART - step, QUART) * owner_count + source_expert
        is_replica = ((bits[at // 16] >> (at % 16)) & 1) == 1
        target = jnp.where(is_replica, plan_ref[source], source_expert)

        @pl.when(target == own_expert)
        def _():
            columns = jnp.concatenate(
                [refs[ref][row + p * tok_rows : row + (p + 1) * tok_rows, :] for p in range(parts)],
                axis=1,
            )
            for total, ahead in zip(totals, steps):
                start = row + base + lax.rem(group + ahead, groups) * share_rows

                @pl.loop(0, rows // chunk)
                def _(i):
                    term = jnp.dot(
                        refs[ref][pl.ds(pl.multiple_of(start + i * chunk, 16), chunk), :],
                        columns,
                        preferred_element_type=jnp.float32,
                    )
                    rounded = term.astype(jnp.bfloat16).astype(jnp.float32)
                    into = pl.ds(pl.multiple_of(i * chunk, 16), chunk)
                    total[into, :] += jnp.where(is_replica, rounded, term)


def update_kernel(parts, held, span, pieces, *refs):
    terms, (master, one, two) = refs[:parts], refs[parts : parts + 3]
    *outs, fresh, new_rows, sems = refs[parts + 3 + held :]
    first, _ = span
    copies = []
    for at, (start, size) in enumerate(pieces):
        inside, placed = pl.ds(start, size), pl.ds(first + start, size)
        gradient = terms[0][inside, :]
        for term in terms[1:]:
            gradient = gradient + term[inside, :]
        weights = master[placed, :]
        first_next = beta_one * one[placed, :] + (1.0 - beta_one) * gradient
        second_next = beta_two * two[placed, :] + (1.0 - beta_two) * gradient * gradient
        scaled_first = first_next / (1.0 - beta_one**step_count)
        scaled_second = second_next / (1.0 - beta_two**step_count)
        direction = scaled_first / (jnp.sqrt(scaled_second) + epsilon)
        weights_next = weights - learn_rate * (direction + decay_rate * weights)
        fresh[inside, :] = weights_next.astype(jnp.bfloat16)
        for which, value in enumerate((weights_next, first_next, second_next)):
            new_rows[which, inside, :] = value
            copies.append(
                pltpu.make_async_copy(
                    new_rows.at[which, inside, :], outs[which].at[placed, :], sems.at[which, at]
                )
            )
            copies[-1].start()
    for copy in copies:
        copy.wait()


def update(terms, states, span, held):
    length = span[1]
    rows, width = states[0].shape
    pieces = [(start, min(64, length - start)) for start in range(0, length, 64)]
    whole = jax.ShapeDtypeStruct((rows, width), jnp.float32)
    inputs = len(terms) + len(states)
    return pl.pallas_call(
        functools.partial(update_kernel, len(terms), len(held), span, pieces),
        out_shape=(whole, whole, whole, jax.ShapeDtypeStruct((length, width), jnp.bfloat16)),
        in_specs=[VMEM] * inputs + [ANYWHERE] * len(held),
        out_specs=(ANYWHERE, ANYWHERE, ANYWHERE, VMEM),
        scratch_shapes=[
            pltpu.VMEM((3, length, width), jnp.float32),
            pltpu.SemaphoreType.DMA((3, len(pieces))),
        ],
        input_output_aliases={inputs + i: i for i in range(len(held))},
        compiler_params=pltpu.CompilerParams(vmem_limit_bytes=24 << 20),
        cost_estimate=pl.CostEstimate(
            flops=length * width, bytes_accessed=length * width, transcendentals=0
        ),
    )(*terms, *states, *held)


def choose_kernel(owner_count, plan_ref, *refs):
    candidates, chosen = refs[:owner_count], refs[owner_count:]
    own_block, own_expert = place(owner_count)
    for step, out in enumerate(chosen):
        wanted = plan_ref[lax.rem(own_block + step, QUART) * owner_count + own_expert]
        for mate, candidate in enumerate(candidates):

            @pl.when(wanted == own_expert ^ mate)
            def _():
                out[...] = candidate[...]


def offer_kernel(owner_count, plan_ref, *refs):
    held, out = refs[:-1], refs[-1]
    own_block, own_expert = place(owner_count)
    wanted = plan_ref[own_block * owner_count + (own_expert ^ 1)]
    half = owner_count // 2
    rows = held[0].shape[0]
    for pair in range(half):

        @pl.when((wanted ^ own_expert) >> 1 == pair)
        def _():
            out[0] = held[pair][...]
            for step in range(1, QUART):
                out[step] = held[half + pair][(step - 1) * rows : step * rows, :]


def assemble_kernel(owner_count, span, later, plan_ref, *refs):
    *blocks, out, sems = refs
    own_block, own_expert = place(owner_count)
    apart = plan_ref[own_block * owner_count + own_expert] ^ own_expert
    first, rows = span
    half = owner_count // 2

    def put(sources, start):
        copies = []
        for step, source in enumerate(sources):
            width = source.shape[1]
            column = pl.multiple_of(lax.rem(own_block + QUART - step, QUART) * width, LANES)
            target = out.at[pl.ds(start, source.shape[0]), pl.ds(column, width)]
            copies.append(pltpu.make_async_copy(source, target, sems.at[step]))
            copies[-1].start()
        for copy in copies:
            copy.wait()

    if later:
        offered, _ = blocks

        @pl.when(apart & 1 == 1)
        def _():
            put([offered.at[step] for step in range(QUART)], first)

        return

    near, far, received = blocks[:half], blocks[half : 2 * half], blocks[2 * half :]
    put(received, first + rows)
    for pair in range(half):

        @pl.when(apart == 2 * pair)
        def _():
            sources = [far[pair].at[pl.ds(step * rows, rows), :] for step in range(QUART - 1)]
            put([near[pair], *sources], first)


def assemble(owner_count, span, plan, blocks, shape, held=None):
    later = held is not None
    inputs = [*blocks, held] if later else blocks
    return pl.pallas_call(
        functools.partial(assemble_kernel, owner_count, span, later),
        out_shape=shape,
        in_specs=[SMEM] + [VMEM] * len(blocks) + [ANYWHERE] * later,
        out_specs=ANYWHERE,
        scratch_shapes=[pltpu.SemaphoreType.DMA((QUART,))],
        input_output_aliases={1 + len(blocks): 0} if later else {},
        compiler_params=pltpu.CompilerParams(vmem_limit_bytes=vmem_for(*blocks)),
        cost_estimate=pl.CostEstimate(flops=1, bytes_accessed=1 << 14, transcendentals=0),
    )(plan, *inputs)


def per_device(
    hidden_rows, grad_rows, block_slot, live_rows, replica_plan, master, moment_one, moment_two
):
    owner_count = lax.axis_size("expert") // QUART
    groups = lax.axis_size("dp")
    hidden_units, tok_rows = hidden_rows.shape
    block_width = grad_rows.shape[1] // QUART
    share_rows = hidden_units // groups
    assert block_slot.shape[1] == 1 and tok_rows == LANES and block_width % LANES == 0
    shape = jax.ShapeDtypeStruct
    lead = share_rows * 13 // 24 // 16 * 16
    spans = ((0, lead), (lead, share_rows - lead))

    head_rows = (block_width // LANES) * tok_rows + META_ROWS
    outs = [shape((head_rows + hidden_units, LANES), jnp.bfloat16)] * QUART
    messages = pl.pallas_call(
        functools.partial(message_kernel, owner_count),
        out_shape=tuple(outs),
        in_specs=[SMEM, SMEM, ANYWHERE, ANYWHERE],
        out_specs=tuple([VMEM] * len(outs)),
        scratch_shapes=[
            pltpu.VMEM(hidden_rows.shape, hidden_rows.dtype),
            pltpu.VMEM(grad_rows.shape, grad_rows.dtype),
            pltpu.SemaphoreType.DMA((2,)),
        ],
        compiler_params=pltpu.CompilerParams(
            vmem_limit_bytes=vmem_for(hidden_rows, grad_rows, *outs)
        ),
        cost_estimate=pl.CostEstimate(flops=1, bytes_accessed=1 << 14, transcendentals=0),
    )(block_slot, live_rows, hidden_rows, grad_rows)

    def across(block, step):
        return from_behind(block, "expert", step * owner_count) if step else block

    first_bit = owner_count // 2
    other_bits = [1 << i for i in reversed(range(first_bit.bit_length() - 1))]
    own = [([(0, 0)], messages[0])]
    sides = [([(step, 0)], across(messages[step], step)) for step in (1, 3)]
    own += [exchange(own, first_bit)]
    last = across(after(messages[2], *(block for _, block in sides)), 2)
    crossed = [exchange(sides, first_bit)]
    own += sides
    for bit in other_bits:
        own += [exchange(own, bit)]
    last = [([(2, 0)], last)]
    last += [exchange(last, first_bit)]
    last = crossed + last
    for bit in other_bits:
        last += [exchange(last, bit)]
    heads = own + last
    head_at = places(heads, 0)

    def partials(at, steps, wait_for):
        first, rows = spans[at]
        return call(
            functools.partial(
                partial_kernel,
                owner_count,
                tok_rows,
                share_rows,
                tuple(head_at.items()),
                head_rows + first,
                steps,
            ),
            [shape((rows, block_width), jnp.float32)] * len(steps),
            (after(replica_plan, *wait_for),),
            [block for _, block in heads],
            2 * len(steps) * rows * tok_rows * block_width * QUART,
        )

    states = (master[0], moment_one[0], moment_two[0])
    ahead = tuple(range(1, groups))
    block = lambda rows: shape((rows, block_width), jnp.bfloat16)

    far_one = partials(0, ahead, ())
    came_one = [from_behind(p, "dp", step) for step, p in zip(ahead, far_one)]
    near_one = partials(0, (0,), far_one)
    far_two = partials(1, ahead, near_one)
    near_two = partials(1, (0,), far_two)
    came_one = [after(term, *near_two) for term in came_one]
    came_two = [
        from_behind(after(p, *came_one), "dp", step) for step, p in zip(ahead, far_two)
    ]
    *held, fresh_one = update((*near_one, *came_one), states, spans[0], ())

    lines = [across(fresh_one, step) for step in range(QUART)]

    came_two = [after(term, fresh_one) for term in came_two]
    *held, fresh_two = update((*near_two, *came_two), states, spans[1], held)

    mates_two = gather_mates(fresh_two, "expert", owner_count)
    near_wide = gather_mates(fresh_one, "expert", owner_count, 2)[::2]
    crossed = mates_two[owner_count // 2], near_wide[-1]
    lines[1:] = [after(line, *crossed) for line in lines[1:]]
    chosen = call(
        functools.partial(choose_kernel, owner_count),
        [block(spans[1][1])] * QUART,
        (after(replica_plan, *lines),),
        mates_two,
    )
    received = [across(c, step) for step, c in enumerate(chosen)]

    stacked = jnp.concatenate(lines[1:])
    far_wide = gather_mates(stacked, "expert", owner_count, 2)[::2]
    (offer,) = call(
        functools.partial(offer_kernel, owner_count),
        [shape((QUART, spans[0][1], block_width), jnp.bfloat16)],
        (after(replica_plan, *received[1:]),),
        (*near_wide, *far_wide),
    )
    result = shape((share_rows, QUART * block_width), jnp.bfloat16)
    placed = assemble(
        owner_count, spans[0], replica_plan, [*near_wide, *far_wide, *received], result
    )
    offer = from_mate(offer, "expert", 1)
    replica_weight = assemble(owner_count, spans[0], replica_plan, [offer], result, placed)
    return (*(state[None] for state in held), replica_weight[None])


def solution(mesh):
    return jax.shard_map(
        per_device,
        mesh=mesh,
        in_specs=(
            P(None, ("dp", "expert")),
            P(("dp", "expert"), None),
            P(("dp", "expert"), None),
            P(("dp", "expert")),
            P(),
            P("expert", "dp", None),
            P("expert", "dp", None),
            P("expert", "dp", None),
        ),
        out_specs=(
            P("expert", "dp", None),
            P("expert", "dp", None),
            P("expert", "dp", None),
            P("expert", "dp", None),
        ),
        check_vma=False,
    )
```

```python
import functools

import jax
import jax.numpy as jnp
from jax import lax
from jax.experimental import pallas as pl
from jax.experimental.pallas import tpu as pltpu
from jax.sharding import PartitionSpec as P

QUART = 4
LANES = 128
META_ROWS = 16


beta_one = 0.9
beta_two = 0.95
learn_rate = 0.01
decay_rate = 0.1
epsilon = 1e-08
step_count = 10.0

VMEM = pl.BlockSpec(memory_space=pltpu.VMEM)
SMEM = pl.BlockSpec(memory_space=pltpu.SMEM)
ANYWHERE = pl.BlockSpec(memory_space=pl.ANY)


def vmem_for(*arrays):
    return int(sum(a.size * a.dtype.itemsize for a in arrays) * 5 // 4) + (8 << 20)


def call(kernel, out_shapes, scalars, arrays, flops=0):
    moved = sum(a.size * a.dtype.itemsize for a in (*arrays, *out_shapes))
    return pl.pallas_call(
        kernel,
        out_shape=tuple(out_shapes),
        in_specs=[SMEM] * len(scalars) + [VMEM] * len(arrays),
        out_specs=tuple([VMEM] * len(out_shapes)),
        compiler_params=pltpu.CompilerParams(vmem_limit_bytes=vmem_for(*arrays, *out_shapes)),
        cost_estimate=pl.CostEstimate(flops=flops // 64, bytes_accessed=moved // 64, transcendentals=0),
    )(*scalars, *arrays)


def from_behind(block, axis, distance):
    devices = range(lax.axis_size(axis))
    route = [((i - distance) % len(devices), i) for i in devices]
    return lax.ppermute(block, axis, route)


def from_mate(block, axis, bit):
    return lax.ppermute(block, axis, [(i ^ bit, i) for i in range(lax.axis_size(axis))])


def gather_mates(block, axis, count, least=1):
    held = {0: block}
    bit = count // 2
    while bit >= least:
        held.update({m | bit: from_mate(held[m], axis, bit) for m in list(held)})
        bit //= 2
    return [held.get(m) for m in range(count)]


def after(value, *others):
    return lax.optimization_barrier((value, *others))[0] if others else value


def exchange(packs, bit):
    keys = [(step, mate | bit) for pack, _ in packs for step, mate in pack]
    blocks = [block for _, block in packs]
    return keys, from_mate(jnp.concatenate(blocks) if len(blocks) > 1 else blocks[0], "expert", bit)


def places(packs, first):
    found = {}
    for at, (keys, block) in enumerate(packs):
        rows = block.shape[0] // len(keys)
        found.update({key: (first + at, i * rows) for i, key in enumerate(keys)})
    return found


def place(owner_count):
    own = lax.axis_index("expert")
    return own // owner_count, own % owner_count


def message_kernel(owner_count, spans, slot_ref, live_ref, hidden_ref, grad_ref, *message_refs):
    own_block, _ = place(owner_count)
    groups = lax.axis_size("dp")
    hidden_units, tok_rows = hidden_ref.shape
    share_rows = hidden_units // groups
    block_width = grad_ref.shape[1] // QUART
    parts = block_width // LANES
    live = live_ref[0]
    slot = slot_ref[0, 0]
    kept = lax.broadcasted_iota(jnp.int32, (tok_rows, LANES), 0) < live
    meta = jnp.full((META_ROWS, LANES), slot.astype(jnp.float32)).astype(jnp.bfloat16)

    def put_hidden(message, row, span):
        first, length = span
        for group in range(groups):
            start = group * share_rows + first
            message[row : row + length, :] = hidden_ref[start : start + length, :]
            row += length

    for step, message in enumerate(message_refs[:QUART]):
        target = lax.rem(own_block + step, QUART)
        for part in range(parts):
            start = pl.multiple_of(target * block_width + part * LANES, LANES)
            columns = grad_ref[:, pl.ds(start, LANES)].astype(jnp.float32)
            row = part * tok_rows
            message[row : row + tok_rows, :] = jnp.where(kept, columns, 0.0).astype(jnp.bfloat16)
        row = parts * tok_rows
        message[row : row + META_ROWS, :] = meta
        put_hidden(message, row + META_ROWS, spans[0])
    for message, span in zip(message_refs[QUART:], spans[1:]):
        put_hidden(message, 0, span)


def partial_kernel(owner_count, tok_rows, where, base, steps, plan_ref, *refs):
    totals = refs[-len(steps) :]
    own_block, own_expert = place(owner_count)
    group, groups = lax.axis_index("dp"), lax.axis_size("dp")
    rows, block_width = totals[0].shape
    parts = block_width // LANES
    chunk = next(c for c in (208, 192, 176, 128, 112, 96, 64, 48, 32, 16) if rows % c == 0)
    bits = []
    for first in range(0, len(where), 16):
        packed = jnp.zeros((META_ROWS, LANES), jnp.float32)
        for at, (_, (head, row), _) in enumerate(where[first : first + 16]):
            meta = refs[head][row + parts * tok_rows : row + parts * tok_rows + META_ROWS, :]
            packed = packed + meta.astype(jnp.float32) * float(1 << at)
        bits.append(jnp.max(packed).astype(jnp.int32))
    for total in totals:
        total[...] = jnp.zeros_like(total)
    for at, ((step, mate), (head, head_row), (tail, tail_row)) in enumerate(where):
        source_expert = own_expert ^ mate
        source = lax.rem(own_block + QUART - step, QUART) * owner_count + source_expert
        is_replica = ((bits[at // 16] >> (at % 16)) & 1) == 1
        target = jnp.where(is_replica, plan_ref[source], source_expert)

        @pl.when(target == own_expert)
        def _():
            columns = jnp.concatenate(
                [
                    refs[head][head_row + p * tok_rows : head_row + (p + 1) * tok_rows, :]
                    for p in range(parts)
                ],
                axis=1,
            )
            for total, ahead in zip(totals, steps):
                start = tail_row + base + lax.rem(group + ahead, groups) * rows

                @pl.loop(0, rows // chunk)
                def _(i):
                    term = jnp.dot(
                        refs[tail][pl.ds(pl.multiple_of(start + i * chunk, 16), chunk), :],
                        columns,
                        preferred_element_type=jnp.float32,
                    )
                    rounded = term.astype(jnp.bfloat16).astype(jnp.float32)
                    into = pl.ds(pl.multiple_of(i * chunk, 16), chunk)
                    total[into, :] += jnp.where(is_replica, rounded, term)


def update_kernel(parts, held, span, pieces, *refs):
    terms, (master, one, two) = refs[:parts], refs[parts : parts + 3]
    *outs, fresh, new_rows, sems = refs[parts + 3 + held :]
    first, _ = span
    copies = []
    for at, (start, size) in enumerate(pieces):
        inside, placed = pl.ds(start, size), pl.ds(first + start, size)
        gradient = terms[0][inside, :]
        for term in terms[1:]:
            gradient = gradient + term[inside, :]
        weights = master[placed, :]
        first_next = beta_one * one[placed, :] + (1.0 - beta_one) * gradient
        second_next = beta_two * two[placed, :] + (1.0 - beta_two) * gradient * gradient
        scaled_first = first_next / (1.0 - beta_one**step_count)
        scaled_second = second_next / (1.0 - beta_two**step_count)
        direction = scaled_first / (jnp.sqrt(scaled_second) + epsilon)
        weights_next = weights - learn_rate * (direction + decay_rate * weights)
        fresh[inside, :] = weights_next.astype(jnp.bfloat16)
        for which, value in enumerate((weights_next, first_next, second_next)):
            new_rows[which, inside, :] = value
            copies.append(
                pltpu.make_async_copy(
                    new_rows.at[which, inside, :], outs[which].at[placed, :], sems.at[which, at]
                )
            )
            copies[-1].start()
    for copy in copies:
        copy.wait()


def update(terms, states, span, held):
    length = span[1]
    rows, width = states[0].shape
    pieces = [(start, min(64, length - start)) for start in range(0, length, 64)]
    whole = jax.ShapeDtypeStruct((rows, width), jnp.float32)
    inputs = len(terms) + len(states)
    return pl.pallas_call(
        functools.partial(update_kernel, len(terms), len(held), span, pieces),
        out_shape=(whole, whole, whole, jax.ShapeDtypeStruct((length, width), jnp.bfloat16)),
        in_specs=[VMEM] * inputs + [ANYWHERE] * len(held),
        out_specs=(ANYWHERE, ANYWHERE, ANYWHERE, VMEM),
        scratch_shapes=[
            pltpu.VMEM((3, length, width), jnp.float32),
            pltpu.SemaphoreType.DMA((3, len(pieces))),
        ],
        input_output_aliases={inputs + i: i for i in range(len(held))},
        compiler_params=pltpu.CompilerParams(vmem_limit_bytes=24 << 20),
        cost_estimate=pl.CostEstimate(
            flops=length * width, bytes_accessed=length * width, transcendentals=0
        ),
    )(*terms, *states, *held)


def choose_kernel(owner_count, plan_ref, *refs):
    candidates, chosen = refs[:owner_count], refs[owner_count:]
    own_block, own_expert = place(owner_count)
    for step, out in enumerate(chosen):
        wanted = plan_ref[lax.rem(own_block + step, QUART) * owner_count + own_expert]
        for mate, candidate in enumerate(candidates):

            @pl.when(wanted == own_expert ^ mate)
            def _():
                out[...] = candidate[...]


def offer_kernel(owner_count, plan_ref, *refs):
    held, out = refs[:-1], refs[-1]
    own_block, own_expert = place(owner_count)
    wanted = plan_ref[own_block * owner_count + (own_expert ^ 1)]
    rows = out.shape[1]
    for pair, blocks in enumerate(held):

        @pl.when((wanted ^ own_expert) >> 1 == pair)
        def _():
            for step in range(QUART):
                out[step] = blocks[step * rows : (step + 1) * rows, :]


def assemble_kernel(owner_count, span, later, plan_ref, *refs):
    *blocks, out, sems = refs
    own_block, own_expert = place(owner_count)
    apart = plan_ref[own_block * owner_count + own_expert] ^ own_expert
    first, rows = span
    half = owner_count // 2

    def put(sources, start):
        copies = []
        for step, source in enumerate(sources):
            width = source.shape[1]
            column = pl.multiple_of(lax.rem(own_block + QUART - step, QUART) * width, LANES)
            target = out.at[pl.ds(start, source.shape[0]), pl.ds(column, width)]
            copies.append(pltpu.make_async_copy(source, target, sems.at[step]))
            copies[-1].start()
        for copy in copies:
            copy.wait()

    if later:
        offered, _ = blocks

        @pl.when(apart & 1 == 1)
        def _():
            put([offered.at[step] for step in range(QUART)], first)

        return

    held, received = blocks[:half], blocks[half:]
    put(received, first + rows)
    for pair in range(half):

        @pl.when(apart == 2 * pair)
        def _():
            put([held[pair].at[pl.ds(step * rows, rows), :] for step in range(QUART)], first)


def assemble(owner_count, span, plan, blocks, shape, held=None):
    later = held is not None
    inputs = [*blocks, held] if later else blocks
    return pl.pallas_call(
        functools.partial(assemble_kernel, owner_count, span, later),
        out_shape=shape,
        in_specs=[SMEM] + [VMEM] * len(blocks) + [ANYWHERE] * later,
        out_specs=ANYWHERE,
        scratch_shapes=[pltpu.SemaphoreType.DMA((QUART,))],
        input_output_aliases={1 + len(blocks): 0} if later else {},
        compiler_params=pltpu.CompilerParams(vmem_limit_bytes=vmem_for(*blocks)),
        cost_estimate=pl.CostEstimate(flops=1, bytes_accessed=1 << 14, transcendentals=0),
    )(plan, *inputs)


def per_device(
    hidden_rows, grad_rows, block_slot, live_rows, replica_plan, master, moment_one, moment_two
):
    owner_count = lax.axis_size("expert") // QUART
    groups = lax.axis_size("dp")
    hidden_units, tok_rows = hidden_rows.shape
    block_width = grad_rows.shape[1] // QUART
    share_rows = hidden_units // groups
    assert block_slot.shape[1] == 1 and tok_rows == LANES and block_width % LANES == 0
    shape = jax.ShapeDtypeStruct
    lead = share_rows * 13 // 24 // 16 * 16
    spans = ((0, lead), (lead, share_rows - lead))

    head_rows = (block_width // LANES) * tok_rows + META_ROWS
    outs = [shape((head_rows + groups * lead, LANES), jnp.bfloat16)] * QUART
    outs += [shape((groups * (share_rows - lead), LANES), jnp.bfloat16)]
    messages = call(
        functools.partial(message_kernel, owner_count, spans),
        outs,
        (block_slot, live_rows),
        (hidden_rows, grad_rows),
    )

    def across(block, step):
        return from_behind(block, "expert", step * owner_count) if step else block

    first_bit = owner_count // 2
    other_bits = [1 << i for i in reversed(range(first_bit.bit_length() - 1))]
    own = [([(0, 0)], messages[0])]
    sides = [([(step, 0)], across(messages[step], step)) for step in (1, 3)]
    keys, block = exchange(own, first_bit)
    own += [(keys, after(block, *(side for _, side in sides))), *sides]
    last = [([(2, 0)], across(after(messages[2], own[1][1]), 2))]
    crossed = [exchange(sides, first_bit)]
    last_crossed = exchange(last, first_bit)
    for bit in other_bits:
        own += [exchange(own, bit)]
        last += [exchange(last, bit)]
    later = after(messages[QUART], last[-1][1], crossed[0][1])
    rest = [([(0, 0)], messages[QUART])]
    rest += [([(step, 0)], across(later, step)) for step in (1, 2, 3)]
    keys, block = last_crossed
    crossed += [(keys, after(block, *(part for _, part in rest[1:])))]
    for bit in other_bits:
        crossed += [exchange(crossed, bit)]
    last += crossed
    heads = own + last
    head_at = places(heads, 0)
    rests, rest_at = [], {}

    def partials(at, steps, wait_for):
        rows = spans[at][1]
        packs = heads + rests if at else heads
        where = [(key, found, rest_at[key] if at else found) for key, found in head_at.items()]
        return call(
            functools.partial(
                partial_kernel, owner_count, tok_rows, where, 0 if at else head_rows, steps
            ),
            [shape((rows, block_width), jnp.float32)] * len(steps),
            (after(replica_plan, *wait_for),),
            [block for _, block in packs],
            2 * len(steps) * rows * tok_rows * block_width * QUART,
        )

    states = (master[0], moment_one[0], moment_two[0])
    ahead = tuple(range(1, groups))
    block = lambda rows: shape((rows, block_width), jnp.bfloat16)

    far_one = partials(0, ahead, ())
    came_one = [from_behind(p, "dp", step) for step, p in zip(ahead, far_one)]
    near_one = partials(0, (0,), far_one)

    keys, parts = zip(*rest)
    stack = jnp.concatenate(parts)
    rest = [(sum(keys, []), stack)]
    rest += [exchange(rest, first_bit)]
    for pack in rest:
        group = [pack]
        for bit in other_bits:
            group += [exchange(group, bit)]
        rests += group
    rest_at.update(places(rests, len(heads)))

    far_two = partials(1, ahead, near_one)
    near_two = partials(1, (0,), far_two)
    came_one = [after(term, *near_two) for term in came_one]
    came_two = [
        from_behind(after(p, *came_one), "dp", step) for step, p in zip(ahead, far_two)
    ]
    *held, fresh_one = update((*near_one, *came_one), states, spans[0], ())

    lines = [across(fresh_one, step) for step in range(QUART)]

    came_two = [after(term, fresh_one) for term in came_two]
    *held, fresh_two = update((*near_two, *came_two), states, spans[1], held)

    mates_two = gather_mates(fresh_two, "expert", owner_count)
    lines[1:] = [after(line, mates_two[owner_count // 2]) for line in lines[1:]]
    chosen = call(
        functools.partial(choose_kernel, owner_count),
        [block(spans[1][1])] * QUART,
        (after(replica_plan, *lines),),
        mates_two,
    )
    received = [across(c, step) for step, c in enumerate(chosen)]

    wide = gather_mates(jnp.concatenate(lines), "expert", owner_count, 2)[::2]
    (offer,) = call(
        functools.partial(offer_kernel, owner_count),
        [shape((QUART, spans[0][1], block_width), jnp.bfloat16)],
        (replica_plan,),
        wide,
    )
    result = shape((share_rows, QUART * block_width), jnp.bfloat16)
    placed = assemble(
        owner_count, spans[0], replica_plan, [*wide, *received], result
    )
    offer = from_mate(after(offer, *received[1:]), "expert", 1)
    replica_weight = assemble(owner_count, spans[0], replica_plan, [offer], result, placed)
    return (*(state[None] for state in held), replica_weight[None])


def solution(mesh):
    return jax.shard_map(
        per_device,
        mesh=mesh,
        in_specs=(
            P(None, ("dp", "expert")),
            P(("dp", "expert"), None),
            P(("dp", "expert"), None),
            P(("dp", "expert")),
            P(),
            P("expert", "dp", None),
            P("expert", "dp", None),
            P("expert", "dp", None),
        ),
        out_specs=(
            P("expert", "dp", None),
            P("expert", "dp", None),
            P("expert", "dp", None),
            P("expert", "dp", None),
        ),
        check_vma=False,
    )
```

```python
import functools

import jax
import jax.numpy as jnp
from jax import lax
from jax.experimental import pallas as pl
from jax.experimental.pallas import tpu as pltpu
from jax.sharding import PartitionSpec as P

QUART = 4
LANES = 128
META_ROWS = 16


beta_one = 0.9
beta_two = 0.95
learn_rate = 0.01
decay_rate = 0.1
epsilon = 1e-08
step_count = 10.0

VMEM = pl.BlockSpec(memory_space=pltpu.VMEM)
SMEM = pl.BlockSpec(memory_space=pltpu.SMEM)
ANYWHERE = pl.BlockSpec(memory_space=pl.ANY)


def vmem_for(*arrays):
    return int(sum(a.size * a.dtype.itemsize for a in arrays) * 5 // 4) + (8 << 20)


def call(kernel, out_shapes, scalars, arrays, flops=0):
    moved = sum(a.size * a.dtype.itemsize for a in (*arrays, *out_shapes))
    return pl.pallas_call(
        kernel,
        out_shape=tuple(out_shapes),
        in_specs=[SMEM] * len(scalars) + [VMEM] * len(arrays),
        out_specs=tuple([VMEM] * len(out_shapes)),
        compiler_params=pltpu.CompilerParams(vmem_limit_bytes=vmem_for(*arrays, *out_shapes)),
        cost_estimate=pl.CostEstimate(flops=flops // 64, bytes_accessed=moved // 64, transcendentals=0),
    )(*scalars, *arrays)


def from_behind(block, axis, distance):
    devices = range(lax.axis_size(axis))
    route = [((i - distance) % len(devices), i) for i in devices]
    return lax.ppermute(block, axis, route)


def from_mate(block, axis, bit):
    return lax.ppermute(block, axis, [(i ^ bit, i) for i in range(lax.axis_size(axis))])


def gather_mates(block, axis, count, least=1):
    held = {0: block}
    bit = count // 2
    while bit >= least:
        held.update({m | bit: from_mate(held[m], axis, bit) for m in list(held)})
        bit //= 2
    return [held.get(m) for m in range(count)]


def after(value, *others):
    return lax.optimization_barrier((value, *others))[0] if others else value


def exchange(packs, bit):
    keys = [(step, mate | bit) for pack, _ in packs for step, mate in pack]
    blocks = [block for _, block in packs]
    return keys, from_mate(jnp.concatenate(blocks) if len(blocks) > 1 else blocks[0], "expert", bit)


def places(packs, first):
    found = {}
    for at, (keys, block) in enumerate(packs):
        rows = block.shape[0] // len(keys)
        found.update({key: (first + at, i * rows) for i, key in enumerate(keys)})
    return found


def place(owner_count):
    own = lax.axis_index("expert")
    return own // owner_count, own % owner_count


def message_kernel(owner_count, spans, slot_ref, live_ref, hidden_ref, grad_ref, *message_refs):
    own_block, _ = place(owner_count)
    groups = lax.axis_size("dp")
    hidden_units, tok_rows = hidden_ref.shape
    share_rows = hidden_units // groups
    block_width = grad_ref.shape[1] // QUART
    parts = block_width // LANES
    live = live_ref[0]
    slot = slot_ref[0, 0]
    kept = lax.broadcasted_iota(jnp.int32, (tok_rows, LANES), 0) < live
    meta = jnp.full((META_ROWS, LANES), slot.astype(jnp.float32)).astype(jnp.bfloat16)

    def put_hidden(message, row, span):
        first, length = span
        for group in range(groups):
            start = group * share_rows + first
            message[row : row + length, :] = hidden_ref[start : start + length, :]
            row += length

    for step, message in enumerate(message_refs[:QUART]):
        target = lax.rem(own_block + step, QUART)
        for part in range(parts):
            start = pl.multiple_of(target * block_width + part * LANES, LANES)
            columns = grad_ref[:, pl.ds(start, LANES)].astype(jnp.float32)
            row = part * tok_rows
            message[row : row + tok_rows, :] = jnp.where(kept, columns, 0.0).astype(jnp.bfloat16)
        row = parts * tok_rows
        message[row : row + META_ROWS, :] = meta
        put_hidden(message, row + META_ROWS, spans[0])
    for message, span in zip(message_refs[QUART:], spans[1:]):
        put_hidden(message, 0, span)


def partial_kernel(owner_count, tok_rows, where, base, steps, plan_ref, *refs):
    totals = refs[-len(steps) :]
    own_block, own_expert = place(owner_count)
    group, groups = lax.axis_index("dp"), lax.axis_size("dp")
    rows, block_width = totals[0].shape
    parts = block_width // LANES
    chunk = next(c for c in (208, 192, 176, 128, 112, 96, 64, 48, 32, 16) if rows % c == 0)
    bits = []
    for first in range(0, len(where), 16):
        packed = jnp.zeros((META_ROWS, LANES), jnp.float32)
        for at, (_, (head, row), _) in enumerate(where[first : first + 16]):
            meta = refs[head][row + parts * tok_rows : row + parts * tok_rows + META_ROWS, :]
            packed = packed + meta.astype(jnp.float32) * float(1 << at)
        bits.append(jnp.max(packed).astype(jnp.int32))
    for total in totals:
        total[...] = jnp.zeros_like(total)
    for at, ((step, mate), (head, head_row), (tail, tail_row)) in enumerate(where):
        source_expert = own_expert ^ mate
        source = lax.rem(own_block + QUART - step, QUART) * owner_count + source_expert
        is_replica = ((bits[at // 16] >> (at % 16)) & 1) == 1
        target = jnp.where(is_replica, plan_ref[source], source_expert)

        columns = jnp.concatenate(
            [
                refs[head][head_row + p * tok_rows : head_row + (p + 1) * tok_rows, :]
                for p in range(parts)
            ],
            axis=1,
        )

        def add(rounded):
            for total, ahead in zip(totals, steps):
                start = tail_row + base + lax.rem(group + ahead, groups) * rows

                @pl.loop(0, rows // chunk)
                def _(i):
                    term = jnp.dot(
                        refs[tail][pl.ds(pl.multiple_of(start + i * chunk, 16), chunk), :],
                        columns,
                        preferred_element_type=jnp.float32,
                    )
                    if rounded:
                        term = term.astype(jnp.bfloat16).astype(jnp.float32)
                    into = pl.ds(pl.multiple_of(i * chunk, 16), chunk)
                    total[into, :] += term

        if mate == 0:
            pl.when((target == own_expert) & jnp.logical_not(is_replica))(lambda: add(False))
        pl.when((target == own_expert) & is_replica)(lambda: add(True))


def update_kernel(parts, held, span, pieces, *refs):
    terms, (master, one, two) = refs[:parts], refs[parts : parts + 3]
    *outs, fresh, new_rows, sems = refs[parts + 3 + held :]
    first, _ = span
    copies = []
    for at, (start, size) in enumerate(pieces):
        inside, placed = pl.ds(start, size), pl.ds(first + start, size)
        gradient = terms[0][inside, :]
        for term in terms[1:]:
            gradient = gradient + term[inside, :]
        weights = master[placed, :]
        first_next = beta_one * one[placed, :] + (1.0 - beta_one) * gradient
        second_next = beta_two * two[placed, :] + (1.0 - beta_two) * gradient * gradient
        scaled_first = first_next / (1.0 - beta_one**step_count)
        scaled_second = second_next / (1.0 - beta_two**step_count)
        direction = scaled_first / (jnp.sqrt(scaled_second) + epsilon)
        weights_next = weights - learn_rate * (direction + decay_rate * weights)
        fresh[inside, :] = weights_next.astype(jnp.bfloat16)
        for which, value in enumerate((weights_next, first_next, second_next)):
            new_rows[which, inside, :] = value
            copies.append(
                pltpu.make_async_copy(
                    new_rows.at[which, inside, :], outs[which].at[placed, :], sems.at[which, at]
                )
            )
            copies[-1].start()
    for copy in copies:
        copy.wait()


def update(terms, states, span, held):
    length = span[1]
    rows, width = states[0].shape
    pieces = [(start, min(64, length - start)) for start in range(0, length, 64)]
    whole = jax.ShapeDtypeStruct((rows, width), jnp.float32)
    inputs = len(terms) + len(states)
    return pl.pallas_call(
        functools.partial(update_kernel, len(terms), len(held), span, pieces),
        out_shape=(whole, whole, whole, jax.ShapeDtypeStruct((length, width), jnp.bfloat16)),
        in_specs=[VMEM] * inputs + [ANYWHERE] * len(held),
        out_specs=(ANYWHERE, ANYWHERE, ANYWHERE, VMEM),
        scratch_shapes=[
            pltpu.VMEM((3, length, width), jnp.float32),
            pltpu.SemaphoreType.DMA((3, len(pieces))),
        ],
        input_output_aliases={inputs + i: i for i in range(len(held))},
        compiler_params=pltpu.CompilerParams(vmem_limit_bytes=24 << 20),
        cost_estimate=pl.CostEstimate(
            flops=length * width, bytes_accessed=length * width, transcendentals=0
        ),
    )(*terms, *states, *held)


def choose_kernel(owner_count, plan_ref, *refs):
    candidates, chosen = refs[:owner_count], refs[owner_count:]
    own_block, own_expert = place(owner_count)
    for step, out in enumerate(chosen):
        wanted = plan_ref[lax.rem(own_block + step, QUART) * owner_count + own_expert]
        for mate, candidate in enumerate(candidates):

            @pl.when(wanted == own_expert ^ mate)
            def _():
                out[...] = candidate[...]


def offer_kernel(owner_count, plan_ref, *refs):
    held, out = refs[:-1], refs[-1]
    own_block, own_expert = place(owner_count)
    wanted = plan_ref[own_block * owner_count + (own_expert ^ 1)]
    rows = out.shape[1]
    for pair, blocks in enumerate(held):

        @pl.when((wanted ^ own_expert) >> 1 == pair)
        def _():
            for step in range(QUART):
                out[step] = blocks[step * rows : (step + 1) * rows, :]


def assemble_kernel(owner_count, span, later, plan_ref, *refs):
    *blocks, out, sems = refs
    own_block, own_expert = place(owner_count)
    apart = plan_ref[own_block * owner_count + own_expert] ^ own_expert
    first, rows = span
    half = owner_count // 2

    def put(sources, start):
        copies = []
        for step, source in enumerate(sources):
            width = source.shape[1]
            column = pl.multiple_of(lax.rem(own_block + QUART - step, QUART) * width, LANES)
            target = out.at[pl.ds(start, source.shape[0]), pl.ds(column, width)]
            copies.append(pltpu.make_async_copy(source, target, sems.at[step]))
            copies[-1].start()
        for copy in copies:
            copy.wait()

    if later:
        offered, _ = blocks

        @pl.when(apart & 1 == 1)
        def _():
            put([offered.at[step] for step in range(QUART)], first)

        return

    held, received = blocks[:half], blocks[half:]
    put(received, first + rows)
    for pair in range(half):

        @pl.when(apart == 2 * pair)
        def _():
            put([held[pair].at[pl.ds(step * rows, rows), :] for step in range(QUART)], first)


def assemble(owner_count, span, plan, blocks, shape, held=None):
    later = held is not None
    inputs = [*blocks, held] if later else blocks
    return pl.pallas_call(
        functools.partial(assemble_kernel, owner_count, span, later),
        out_shape=shape,
        in_specs=[SMEM] + [VMEM] * len(blocks) + [ANYWHERE] * later,
        out_specs=ANYWHERE,
        scratch_shapes=[pltpu.SemaphoreType.DMA((QUART,))],
        input_output_aliases={1 + len(blocks): 0} if later else {},
        compiler_params=pltpu.CompilerParams(vmem_limit_bytes=vmem_for(*blocks)),
        cost_estimate=pl.CostEstimate(flops=1, bytes_accessed=1 << 14, transcendentals=0),
    )(plan, *inputs)


def per_device(
    hidden_rows, grad_rows, block_slot, live_rows, replica_plan, master, moment_one, moment_two
):
    owner_count = lax.axis_size("expert") // QUART
    groups = lax.axis_size("dp")
    hidden_units, tok_rows = hidden_rows.shape
    block_width = grad_rows.shape[1] // QUART
    share_rows = hidden_units // groups
    assert block_slot.shape[1] == 1 and tok_rows == LANES and block_width % LANES == 0
    shape = jax.ShapeDtypeStruct
    lead = share_rows * 13 // 24 // 16 * 16
    spans = ((0, lead), (lead, share_rows - lead))

    head_rows = (block_width // LANES) * tok_rows + META_ROWS
    outs = [shape((head_rows + groups * lead, LANES), jnp.bfloat16)] * QUART
    outs += [shape((groups * (share_rows - lead), LANES), jnp.bfloat16)]
    messages = call(
        functools.partial(message_kernel, owner_count, spans),
        outs,
        (block_slot, live_rows),
        (hidden_rows, grad_rows),
    )

    def across(block, step):
        return from_behind(block, "expert", step * owner_count) if step else block

    first_bit = owner_count // 2
    other_bits = [1 << i for i in reversed(range(first_bit.bit_length() - 1))]
    own = [([(0, 0)], messages[0])]
    sides = [([(step, 0)], across(messages[step], step)) for step in (1, 3)]
    keys, block = exchange(own, first_bit)
    own += [(keys, after(block, *(side for _, side in sides))), *sides]
    last = [([(2, 0)], across(after(messages[2], own[1][1]), 2))]
    crossed = [exchange(sides, first_bit)]
    last_crossed = exchange(last, first_bit)
    for bit in other_bits:
        own += [exchange(own, bit)]
        last += [exchange(last, bit)]
    later = after(messages[QUART], last[-1][1], crossed[0][1])
    rest = [([(0, 0)], messages[QUART])]
    rest += [([(step, 0)], across(later, step)) for step in (1, 2, 3)]
    keys, block = last_crossed
    crossed += [(keys, after(block, *(part for _, part in rest[1:])))]
    for bit in other_bits:
        crossed += [exchange(crossed, bit)]
    last += crossed
    heads = own + last
    head_at = places(heads, 0)
    rests, rest_at = [], {}

    def partials(at, steps, wait_for):
        rows = spans[at][1]
        packs = heads + rests if at else heads
        where = [(key, found, rest_at[key] if at else found) for key, found in head_at.items()]
        return call(
            functools.partial(
                partial_kernel, owner_count, tok_rows, where, 0 if at else head_rows, steps
            ),
            [shape((rows, block_width), jnp.float32)] * len(steps),
            (after(replica_plan, *wait_for),),
            [block for _, block in packs],
            2 * len(steps) * rows * tok_rows * block_width * QUART,
        )

    states = (master[0], moment_one[0], moment_two[0])
    ahead = tuple(range(1, groups))
    block = lambda rows: shape((rows, block_width), jnp.bfloat16)

    far_one = partials(0, ahead, ())
    came_one = [from_behind(p, "dp", step) for step, p in zip(ahead, far_one)]
    near_one = partials(0, (0,), far_one)

    keys, parts = zip(*rest)
    stack = jnp.concatenate(parts)
    rest = [(sum(keys, []), stack)]
    rest += [exchange(rest, first_bit)]
    for pack in rest:
        group = [pack]
        for bit in other_bits:
            group += [exchange(group, bit)]
        rests += group
    rest_at.update(places(rests, len(heads)))

    far_two = partials(1, ahead, near_one)
    came_one = [after(term, *far_two) for term in came_one]
    *held, fresh_one = update((*near_one, *came_one), states, spans[0], ())
    came_two = [
        from_behind(after(p, fresh_one), "dp", step) for step, p in zip(ahead, far_two)
    ]
    near_two = partials(1, (0,), (fresh_one,))

    lines = [across(fresh_one, step) for step in range(QUART)]

    came_two = [after(term, fresh_one) for term in came_two]
    *held, fresh_two = update((*near_two, *came_two), states, spans[1], held)

    mates_two = gather_mates(fresh_two, "expert", owner_count)
    lines[1:] = [after(line, mates_two[owner_count // 2]) for line in lines[1:]]
    chosen = call(
        functools.partial(choose_kernel, owner_count),
        [block(spans[1][1])] * QUART,
        (after(replica_plan, *lines),),
        mates_two,
    )
    received = [across(c, step) for step, c in enumerate(chosen)]

    wide = gather_mates(jnp.concatenate(lines), "expert", owner_count, 2)[::2]
    (offer,) = call(
        functools.partial(offer_kernel, owner_count),
        [shape((QUART, spans[0][1], block_width), jnp.bfloat16)],
        (replica_plan,),
        wide,
    )
    result = shape((share_rows, QUART * block_width), jnp.bfloat16)
    placed = assemble(
        owner_count, spans[0], replica_plan, [*wide, *received], result
    )
    offer = from_mate(after(offer, *received[1:]), "expert", 1)
    replica_weight = assemble(owner_count, spans[0], replica_plan, [offer], result, placed)
    return (*(state[None] for state in held), replica_weight[None])


def solution(mesh):
    return jax.shard_map(
        per_device,
        mesh=mesh,
        in_specs=(
            P(None, ("dp", "expert")),
            P(("dp", "expert"), None),
            P(("dp", "expert"), None),
            P(("dp", "expert")),
            P(),
            P("expert", "dp", None),
            P("expert", "dp", None),
            P("expert", "dp", None),
        ),
        out_specs=(
            P("expert", "dp", None),
            P("expert", "dp", None),
            P("expert", "dp", None),
            P("expert", "dp", None),
        ),
        check_vma=False,
    )
```

```python
import functools

import jax
import jax.numpy as jnp
from jax import lax
from jax.experimental import pallas as pl
from jax.experimental.pallas import tpu as pltpu
from jax.sharding import PartitionSpec as P

QUART = 4
LANES = 128
META_ROWS = 16
PIECE = 64


beta_one = 0.9
beta_two = 0.95
learn_rate = 0.01
decay_rate = 0.1
epsilon = 1e-08
step_count = 10.0

VMEM = pl.BlockSpec(memory_space=pltpu.VMEM)
SMEM = pl.BlockSpec(memory_space=pltpu.SMEM)
ANYWHERE = pl.BlockSpec(memory_space=pl.ANY)


def vmem_for(*arrays):
    return int(sum(a.size * a.dtype.itemsize for a in arrays) * 5 // 4) + (8 << 20)


def call(kernel, out_shapes, scalars, arrays, flops=0):
    moved = sum(a.size * a.dtype.itemsize for a in (*arrays, *out_shapes))
    return pl.pallas_call(
        kernel,
        out_shape=tuple(out_shapes),
        in_specs=[SMEM] * len(scalars) + [VMEM] * len(arrays),
        out_specs=tuple([VMEM] * len(out_shapes)),
        compiler_params=pltpu.CompilerParams(vmem_limit_bytes=vmem_for(*arrays, *out_shapes)),
        cost_estimate=pl.CostEstimate(flops=flops // 64, bytes_accessed=moved // 64, transcendentals=0),
    )(*scalars, *arrays)


def from_behind(block, axis, distance):
    devices = range(lax.axis_size(axis))
    route = [((i - distance) % len(devices), i) for i in devices]
    return lax.ppermute(block, axis, route)


def from_mate(block, axis, bit):
    return lax.ppermute(block, axis, [(i ^ bit, i) for i in range(lax.axis_size(axis))])


def gather_mates(block, axis, count, least=1):
    held = {0: block}
    bit = count // 2
    while bit >= least:
        held.update({m | bit: from_mate(held[m], axis, bit) for m in list(held)})
        bit //= 2
    return [held.get(m) for m in range(count)]


def after(value, *others):
    return lax.optimization_barrier((value, *others))[0] if others else value


def exchange(packs, bit):
    keys = [(step, mate | bit) for pack, _ in packs for step, mate in pack]
    blocks = [block for _, block in packs]
    return keys, from_mate(jnp.concatenate(blocks) if len(blocks) > 1 else blocks[0], "expert", bit)


def places(packs, first):
    found = {}
    for at, (keys, block) in enumerate(packs):
        rows = block.shape[0] // len(keys)
        found.update({key: (first + at, i * rows) for i, key in enumerate(keys)})
    return found


def place(owner_count):
    own = lax.axis_index("expert")
    return own // owner_count, own % owner_count


def message_kernel(owner_count, spans, slot_ref, live_ref, hidden_ref, grad_ref, *message_refs):
    own_block, _ = place(owner_count)
    groups = lax.axis_size("dp")
    hidden_units, tok_rows = hidden_ref.shape
    share_rows = hidden_units // groups
    block_width = grad_ref.shape[1] // QUART
    parts = block_width // LANES
    live = live_ref[0]
    slot = slot_ref[0, 0]
    kept = lax.broadcasted_iota(jnp.int32, (tok_rows, LANES), 0) < live
    meta = jnp.full((META_ROWS, LANES), slot.astype(jnp.float32)).astype(jnp.bfloat16)

    def put_hidden(message, row, span):
        first, length = span
        for group in range(groups):
            start = group * share_rows + first
            message[row : row + length, :] = hidden_ref[start : start + length, :]
            row += length

    for step, message in enumerate(message_refs[:QUART]):
        target = lax.rem(own_block + step, QUART)
        for part in range(parts):
            start = pl.multiple_of(target * block_width + part * LANES, LANES)
            columns = grad_ref[:, pl.ds(start, LANES)].astype(jnp.float32)
            row = part * tok_rows
            message[row : row + tok_rows, :] = jnp.where(kept, columns, 0.0).astype(jnp.bfloat16)
        row = parts * tok_rows
        message[row : row + META_ROWS, :] = meta
        put_hidden(message, row + META_ROWS, spans[0])
    for message, span in zip(message_refs[QUART:], spans[1:]):
        put_hidden(message, 0, span)


def partial_kernel(owner_count, tok_rows, where, base, steps, plan_ref, *refs):
    totals = refs[-len(steps) :]
    own_block, own_expert = place(owner_count)
    group, groups = lax.axis_index("dp"), lax.axis_size("dp")
    rows, block_width = totals[0].shape
    parts = block_width // LANES
    chunk = next(c for c in (208, 192, 176, 128, 112, 96, 64, 48, 32, 16) if rows % c == 0)
    bits = []
    for first in range(0, len(where), 16):
        packed = jnp.zeros((META_ROWS, LANES), jnp.float32)
        for at, (_, (head, row), _) in enumerate(where[first : first + 16]):
            meta = refs[head][row + parts * tok_rows : row + parts * tok_rows + META_ROWS, :]
            packed = packed + meta.astype(jnp.float32) * float(1 << at)
        bits.append(jnp.max(packed).astype(jnp.int32))
    for total in totals:
        total[...] = jnp.zeros_like(total)
    for at, ((step, mate), (head, head_row), (tail, tail_row)) in enumerate(where):
        source_expert = own_expert ^ mate
        source = lax.rem(own_block + QUART - step, QUART) * owner_count + source_expert
        is_replica = ((bits[at // 16] >> (at % 16)) & 1) == 1
        target = jnp.where(is_replica, plan_ref[source], source_expert)

        columns = jnp.concatenate(
            [
                refs[head][head_row + p * tok_rows : head_row + (p + 1) * tok_rows, :]
                for p in range(parts)
            ],
            axis=1,
        )

        def add(rounded):
            for total, ahead in zip(totals, steps):
                start = tail_row + base + lax.rem(group + ahead, groups) * rows

                @pl.loop(0, rows // chunk)
                def _(i):
                    term = jnp.dot(
                        refs[tail][pl.ds(pl.multiple_of(start + i * chunk, 16), chunk), :],
                        columns,
                        preferred_element_type=jnp.float32,
                    )
                    if rounded:
                        term = term.astype(jnp.bfloat16).astype(jnp.float32)
                    into = pl.ds(pl.multiple_of(i * chunk, 16), chunk)
                    total[into, :] += term

        if mate == 0:
            pl.when((target == own_expert) & jnp.logical_not(is_replica))(lambda: add(False))
        pl.when((target == own_expert) & is_replica)(lambda: add(True))


def update_kernel(parts, held, span, pieces, *refs):
    terms, (master, one, two) = refs[:parts], refs[parts : parts + 3]
    *outs, fresh, new_rows, sems = refs[parts + 3 + held :]
    first, _ = span
    copies = []
    for at, (start, size) in enumerate(pieces):
        inside, placed = pl.ds(start, size), pl.ds(first + start, size)
        gradient = terms[0][inside, :]
        for term in terms[1:]:
            gradient = gradient + term[inside, :]
        weights = master[placed, :]
        first_next = beta_one * one[placed, :] + (1.0 - beta_one) * gradient
        second_next = beta_two * two[placed, :] + (1.0 - beta_two) * gradient * gradient
        scaled_first = first_next / (1.0 - beta_one**step_count)
        scaled_second = second_next / (1.0 - beta_two**step_count)
        direction = scaled_first / (jnp.sqrt(scaled_second) + epsilon)
        weights_next = weights - learn_rate * (direction + decay_rate * weights)
        fresh[inside, :] = weights_next.astype(jnp.bfloat16)
        for which, value in enumerate((weights_next, first_next, second_next)):
            new_rows[which, inside, :] = value
            copies.append(
                pltpu.make_async_copy(
                    new_rows.at[which, inside, :], outs[which].at[placed, :], sems.at[which, at]
                )
            )
            copies[-1].start()
    for copy in copies:
        copy.wait()


def update(terms, states, span, held):
    length = span[1]
    rows, width = states[0].shape
    pieces = [(start, min(64, length - start)) for start in range(0, length, 64)]
    whole = jax.ShapeDtypeStruct((rows, width), jnp.float32)
    inputs = len(terms) + len(states)
    return pl.pallas_call(
        functools.partial(update_kernel, len(terms), len(held), span, pieces),
        out_shape=(whole, whole, whole, jax.ShapeDtypeStruct((length, width), jnp.bfloat16)),
        in_specs=[VMEM] * inputs + [ANYWHERE] * len(held),
        out_specs=(ANYWHERE, ANYWHERE, ANYWHERE, VMEM),
        scratch_shapes=[
            pltpu.VMEM((3, length, width), jnp.float32),
            pltpu.SemaphoreType.DMA((3, len(pieces))),
        ],
        input_output_aliases={inputs + i: i for i in range(len(held))},
        compiler_params=pltpu.CompilerParams(vmem_limit_bytes=24 << 20),
        cost_estimate=pl.CostEstimate(
            flops=length * width, bytes_accessed=length * width, transcendentals=0
        ),
    )(*terms, *states, *held)


def choose_kernel(owner_count, where, plan_ref, *refs):
    candidates, chosen = refs[: len(where)], refs[len(where) :]
    own_block, own_expert = place(owner_count)
    for step, out in enumerate(chosen):
        wanted = plan_ref[lax.rem(own_block + step, QUART) * owner_count + own_expert]
        for (mate, rows), candidate in zip(where, candidates):

            @pl.when(wanted == own_expert ^ mate)
            def _():
                out[rows, :] = candidate[...]


def offer_kernel(owner_count, plan_ref, *refs):
    held, out = refs[:-1], refs[-1]
    own_block, own_expert = place(owner_count)
    wanted = plan_ref[own_block * owner_count + (own_expert ^ 1)]
    rows = out.shape[1]
    for pair, blocks in enumerate(held):

        @pl.when((wanted ^ own_expert) >> 1 == pair)
        def _():
            for step in range(QUART):
                out[step] = blocks[step * rows : (step + 1) * rows, :]


def assemble_kernel(owner_count, span, later, plan_ref, *refs):
    *blocks, out, sems = refs
    own_block, own_expert = place(owner_count)
    apart = plan_ref[own_block * owner_count + own_expert] ^ own_expert
    first, rows = span
    half = owner_count // 2

    def copies_of(sources, start, group):
        copies = []
        for step, source in enumerate(sources):
            length, width = source.shape
            column = pl.multiple_of(lax.rem(own_block + QUART - step, QUART) * width, LANES)
            for at, row in enumerate(range(0, length, PIECE)):
                size = min(PIECE, length - row)
                target = out.at[pl.ds(start + row, size), pl.ds(column, width)]
                copies.append(
                    pltpu.make_async_copy(
                        source.at[pl.ds(row, size), :], target, sems.at[group, step, at]
                    )
                )
        return copies

    def put(sources, start, group):
        for copy in copies_of(sources, start, group):
            copy.start()
        return lambda: [copy.wait() for copy in copies_of(sources, start, group)]

    if later:
        offered, _ = blocks

        @pl.when(apart & 1 == 1)
        def _():
            put([offered.at[step] for step in range(QUART)], first, 0)()

        return

    held, received = blocks[:half], blocks[half:]
    finish = put(received, first + rows, 0)
    for pair in range(half):

        @pl.when(apart == 2 * pair)
        def _():
            put([held[pair].at[pl.ds(step * rows, rows), :] for step in range(QUART)], first, 1)()

    finish()


def assemble(owner_count, span, plan, blocks, shape, held=None):
    later = held is not None
    inputs = [*blocks, held] if later else blocks
    return pl.pallas_call(
        functools.partial(assemble_kernel, owner_count, span, later),
        out_shape=shape,
        in_specs=[SMEM] + [VMEM] * len(blocks) + [ANYWHERE] * later,
        out_specs=ANYWHERE,
        scratch_shapes=[pltpu.SemaphoreType.DMA((2, QUART, pl.cdiv(shape.shape[0], PIECE)))],
        input_output_aliases={1 + len(blocks): 0} if later else {},
        compiler_params=pltpu.CompilerParams(vmem_limit_bytes=vmem_for(*blocks)),
        cost_estimate=pl.CostEstimate(flops=1, bytes_accessed=1 << 14, transcendentals=0),
    )(plan, *inputs)


def per_device(
    hidden_rows, grad_rows, block_slot, live_rows, replica_plan, master, moment_one, moment_two
):
    owner_count = lax.axis_size("expert") // QUART
    groups = lax.axis_size("dp")
    hidden_units, tok_rows = hidden_rows.shape
    block_width = grad_rows.shape[1] // QUART
    share_rows = hidden_units // groups
    assert block_slot.shape[1] == 1 and tok_rows == LANES and block_width % LANES == 0
    shape = jax.ShapeDtypeStruct
    lead = share_rows * 13 // 24 // 16 * 16
    spans = ((0, lead), (lead, share_rows - lead))

    head_rows = (block_width // LANES) * tok_rows + META_ROWS
    outs = [shape((head_rows + groups * lead, LANES), jnp.bfloat16)] * QUART
    outs += [shape((groups * (share_rows - lead), LANES), jnp.bfloat16)]
    messages = call(
        functools.partial(message_kernel, owner_count, spans),
        outs,
        (block_slot, live_rows),
        (hidden_rows, grad_rows),
    )

    def across(block, step):
        return from_behind(block, "expert", step * owner_count) if step else block

    first_bit = owner_count // 2
    other_bits = [1 << i for i in reversed(range(first_bit.bit_length() - 1))]
    own = [([(0, 0)], messages[0])]
    sides = [([(step, 0)], across(messages[step], step)) for step in (1, 3)]
    keys, block = exchange(own, first_bit)
    own += [(keys, after(block, *(side for _, side in sides))), *sides]
    last = [([(2, 0)], across(after(messages[2], own[1][1]), 2))]
    crossed = [exchange(sides, first_bit)]
    last_crossed = exchange(last, first_bit)
    for bit in other_bits:
        own += [exchange(own, bit)]
        last += [exchange(last, bit)]
    later = after(messages[QUART], last[-1][1], crossed[0][1])
    rest = [([(0, 0)], messages[QUART])]
    rest += [([(step, 0)], across(later, step)) for step in (1, 2, 3)]
    keys, block = last_crossed
    crossed += [(keys, after(block, *(part for _, part in rest[1:])))]
    for bit in other_bits:
        crossed += [exchange(crossed, bit)]
    last += crossed
    heads = own + last
    head_at = places(heads, 0)
    rests, rest_at = [], {}

    def partials(at, steps, wait_for):
        rows = spans[at][1]
        packs = heads + rests if at else heads
        where = [(key, found, rest_at[key] if at else found) for key, found in head_at.items()]
        return call(
            functools.partial(
                partial_kernel, owner_count, tok_rows, where, 0 if at else head_rows, steps
            ),
            [shape((rows, block_width), jnp.float32)] * len(steps),
            (after(replica_plan, *wait_for),),
            [block for _, block in packs],
            2 * len(steps) * rows * tok_rows * block_width * QUART,
        )

    states = (master[0], moment_one[0], moment_two[0])
    ahead = tuple(range(1, groups))
    block = lambda rows: shape((rows, block_width), jnp.bfloat16)

    far_one = partials(0, ahead, ())
    came_one = [from_behind(p, "dp", step) for step, p in zip(ahead, far_one)]
    near_one = partials(0, (0,), far_one)

    keys, parts = zip(*rest)
    stack = jnp.concatenate(parts)
    rest = [(sum(keys, []), stack)]
    rest += [exchange(rest, first_bit)]
    for pack in rest:
        group = [pack]
        for bit in other_bits:
            group += [exchange(group, bit)]
        rests += group
    rest_at.update(places(rests, len(heads)))

    far_two = partials(1, ahead, near_one)
    came_one = [after(term, *far_two) for term in came_one]
    *held, fresh_one = update((*near_one, *came_one), states, spans[0], ())
    came_two = [
        from_behind(after(p, fresh_one), "dp", step) for step, p in zip(ahead, far_two)
    ]
    near_two = partials(1, (0,), (fresh_one,))

    lines = [across(fresh_one, step) for step in range(QUART)]

    came_two = [after(term, fresh_one) for term in came_two]
    *held, fresh_two = update((*near_two, *came_two), states, spans[1], held)

    rows_two = spans[1][1]
    cut = rows_two // 32 * 16
    halves = [(slice(0, cut), fresh_two[:cut]), (slice(cut, rows_two), fresh_two[cut:])]
    mates_two = {0: [(slice(0, rows_two), fresh_two)]}
    for bit in (first_bit, *other_bits):
        mates_two.update(
            {
                m | bit: [
                    (rows, from_mate(piece, "expert", bit))
                    for rows, piece in (halves if bit == first_bit else pieces)
                ]
                for m, pieces in list(mates_two.items())
            }
        )
    crossed_two = [piece for _, piece in mates_two[first_bit]]
    where = [(m, rows) for m, pieces in mates_two.items() for rows, _ in pieces]
    chosen = call(
        functools.partial(choose_kernel, owner_count, where),
        [block(rows_two)] * QUART,
        (replica_plan,),
        [piece for pieces in mates_two.values() for _, piece in pieces],
    )
    lines[3] = after(lines[3], *crossed_two)
    lines[1:3] = [after(line, *chosen) for line in lines[1:3]]
    received = [across(c, step) for step, c in enumerate(chosen)]

    wide = gather_mates(jnp.concatenate(lines), "expert", owner_count, 2)[::2]
    (offer,) = call(
        functools.partial(offer_kernel, owner_count),
        [shape((QUART, spans[0][1], block_width), jnp.bfloat16)],
        (replica_plan,),
        wide,
    )
    result = shape((share_rows, QUART * block_width), jnp.bfloat16)
    placed = assemble(
        owner_count, spans[0], replica_plan, [*wide, *received], result
    )
    offer = from_mate(after(offer, *received[1:]), "expert", 1)
    replica_weight = assemble(owner_count, spans[0], replica_plan, [offer], result, placed)
    return (*(state[None] for state in held), replica_weight[None])


def solution(mesh):
    return jax.shard_map(
        per_device,
        mesh=mesh,
        in_specs=(
            P(None, ("dp", "expert")),
            P(("dp", "expert"), None),
            P(("dp", "expert"), None),
            P(("dp", "expert")),
            P(),
            P("expert", "dp", None),
            P("expert", "dp", None),
            P("expert", "dp", None),
        ),
        out_specs=(
            P("expert", "dp", None),
            P("expert", "dp", None),
            P("expert", "dp", None),
            P("expert", "dp", None),
        ),
        check_vma=False,
    )
```

```python
import functools

import jax
import jax.numpy as jnp
from jax import lax
from jax.experimental import pallas as pl
from jax.experimental.pallas import tpu as pltpu
from jax.sharding import PartitionSpec as P

QUART = 4
LANES = 128
META_ROWS = 16


beta_one = 0.9
beta_two = 0.95
learn_rate = 0.01
decay_rate = 0.1
epsilon = 1e-08
step_count = 10.0

VMEM = pl.BlockSpec(memory_space=pltpu.VMEM)
SMEM = pl.BlockSpec(memory_space=pltpu.SMEM)
ANYWHERE = pl.BlockSpec(memory_space=pl.ANY)


def vmem_for(*arrays):
    return int(sum(a.size * a.dtype.itemsize for a in arrays) * 5 // 4) + (8 << 20)


def call(kernel, out_shapes, scalars, arrays, flops=0):
    moved = sum(a.size * a.dtype.itemsize for a in (*arrays, *out_shapes))
    return pl.pallas_call(
        kernel,
        out_shape=tuple(out_shapes),
        in_specs=[SMEM] * len(scalars) + [VMEM] * len(arrays),
        out_specs=tuple([VMEM] * len(out_shapes)),
        compiler_params=pltpu.CompilerParams(vmem_limit_bytes=vmem_for(*arrays, *out_shapes)),
        cost_estimate=pl.CostEstimate(flops=flops // 64, bytes_accessed=moved // 64, transcendentals=0),
    )(*scalars, *arrays)


def from_behind(block, axis, distance):
    devices = range(lax.axis_size(axis))
    route = [((i - distance) % len(devices), i) for i in devices]
    return lax.ppermute(block, axis, route)


def from_mate(block, axis, bit):
    return lax.ppermute(block, axis, [(i ^ bit, i) for i in range(lax.axis_size(axis))])


def gather_mates(block, axis, count, least=1):
    held = {0: block}
    bit = count // 2
    while bit >= least:
        held.update({m | bit: from_mate(held[m], axis, bit) for m in list(held)})
        bit //= 2
    return [held.get(m) for m in range(count)]


def after(value, *others):
    return lax.optimization_barrier((value, *others))[0] if others else value


def exchange(packs, bit):
    keys = [(step, mate | bit) for pack, _ in packs for step, mate in pack]
    blocks = [block for _, block in packs]
    return keys, from_mate(jnp.concatenate(blocks) if len(blocks) > 1 else blocks[0], "expert", bit)


def places(packs, first):
    found = {}
    for at, (keys, block) in enumerate(packs):
        rows = block.shape[0] // len(keys)
        found.update({key: (first + at, i * rows) for i, key in enumerate(keys)})
    return found


def place(owner_count):
    own = lax.axis_index("expert")
    return own // owner_count, own % owner_count


def message_kernel(owner_count, spans, slot_ref, live_ref, hidden_ref, grad_ref, *message_refs):
    own_block, _ = place(owner_count)
    groups = lax.axis_size("dp")
    hidden_units, tok_rows = hidden_ref.shape
    share_rows = hidden_units // groups
    block_width = grad_ref.shape[1] // QUART
    parts = block_width // LANES
    live = live_ref[0]
    slot = slot_ref[0, 0]
    kept = lax.broadcasted_iota(jnp.int32, (tok_rows, LANES), 0) < live
    meta = jnp.full((META_ROWS, LANES), slot.astype(jnp.float32)).astype(jnp.bfloat16)

    def put_hidden(message, row, span):
        first, length = span
        for group in range(groups):
            start = group * share_rows + first
            message[row : row + length, :] = hidden_ref[start : start + length, :]
            row += length

    for step, message in enumerate(message_refs[:QUART]):
        target = lax.rem(own_block + step, QUART)
        for part in range(parts):
            start = pl.multiple_of(target * block_width + part * LANES, LANES)
            columns = grad_ref[:, pl.ds(start, LANES)].astype(jnp.float32)
            row = part * tok_rows
            message[row : row + tok_rows, :] = jnp.where(kept, columns, 0.0).astype(jnp.bfloat16)
        row = parts * tok_rows
        message[row : row + META_ROWS, :] = meta
        put_hidden(message, row + META_ROWS, spans[0])
    for message, span in zip(message_refs[QUART:], spans[1:]):
        put_hidden(message, 0, span)


def partial_kernel(owner_count, tok_rows, where, base, steps, plan_ref, *refs):
    totals = refs[-len(steps) :]
    own_block, own_expert = place(owner_count)
    group, groups = lax.axis_index("dp"), lax.axis_size("dp")
    rows, block_width = totals[0].shape
    parts = block_width // LANES
    chunk = next(c for c in (208, 192, 176, 128, 112, 96, 64, 48, 32, 16) if rows % c == 0)
    bits = []
    for first in range(0, len(where), 16):
        packed = jnp.zeros((META_ROWS, LANES), jnp.float32)
        for at, (_, (head, row), _) in enumerate(where[first : first + 16]):
            meta = refs[head][row + parts * tok_rows : row + parts * tok_rows + META_ROWS, :]
            packed = packed + meta.astype(jnp.float32) * float(1 << at)
        bits.append(jnp.max(packed).astype(jnp.int32))
    for total in totals:
        total[...] = jnp.zeros_like(total)
    for at, ((step, mate), (head, head_row), (tail, tail_row)) in enumerate(where):
        source_expert = own_expert ^ mate
        source = lax.rem(own_block + QUART - step, QUART) * owner_count + source_expert
        is_replica = ((bits[at // 16] >> (at % 16)) & 1) == 1
        target = jnp.where(is_replica, plan_ref[source], source_expert)

        columns = jnp.concatenate(
            [
                refs[head][head_row + p * tok_rows : head_row + (p + 1) * tok_rows, :]
                for p in range(parts)
            ],
            axis=1,
        )

        def add(rounded):
            for total, ahead in zip(totals, steps):
                start = tail_row + base + lax.rem(group + ahead, groups) * rows

                @pl.loop(0, rows // chunk)
                def _(i):
                    term = jnp.dot(
                        refs[tail][pl.ds(pl.multiple_of(start + i * chunk, 16), chunk), :],
                        columns,
                        preferred_element_type=jnp.float32,
                    )
                    if rounded:
                        term = term.astype(jnp.bfloat16).astype(jnp.float32)
                    into = pl.ds(pl.multiple_of(i * chunk, 16), chunk)
                    total[into, :] += term

        if mate == 0:
            pl.when((target == own_expert) & jnp.logical_not(is_replica))(lambda: add(False))
        pl.when((target == own_expert) & is_replica)(lambda: add(True))


def update_kernel(parts, held, span, pieces, *refs):
    terms, (master, one, two) = refs[:parts], refs[parts : parts + 3]
    *outs, fresh, new_rows, sems = refs[parts + 3 + held :]
    first, _ = span
    copies = []
    for at, (start, size) in enumerate(pieces):
        inside, placed = pl.ds(start, size), pl.ds(first + start, size)
        gradient = terms[0][inside, :]
        for term in terms[1:]:
            gradient = gradient + term[inside, :]
        weights = master[placed, :]
        first_next = beta_one * one[placed, :] + (1.0 - beta_one) * gradient
        second_next = beta_two * two[placed, :] + (1.0 - beta_two) * gradient * gradient
        scaled_first = first_next / (1.0 - beta_one**step_count)
        scaled_second = second_next / (1.0 - beta_two**step_count)
        direction = scaled_first / (jnp.sqrt(scaled_second) + epsilon)
        weights_next = weights - learn_rate * (direction + decay_rate * weights)
        fresh[inside, :] = weights_next.astype(jnp.bfloat16)
        for which, value in enumerate((weights_next, first_next, second_next)):
            new_rows[which, inside, :] = value
            copies.append(
                pltpu.make_async_copy(
                    new_rows.at[which, inside, :], outs[which].at[placed, :], sems.at[which, at]
                )
            )
            copies[-1].start()
    for copy in copies:
        copy.wait()


def update(terms, states, span, held):
    length = span[1]
    rows, width = states[0].shape
    pieces = [(start, min(64, length - start)) for start in range(0, length, 64)]
    whole = jax.ShapeDtypeStruct((rows, width), jnp.float32)
    inputs = len(terms) + len(states)
    return pl.pallas_call(
        functools.partial(update_kernel, len(terms), len(held), span, pieces),
        out_shape=(whole, whole, whole, jax.ShapeDtypeStruct((length, width), jnp.bfloat16)),
        in_specs=[VMEM] * inputs + [ANYWHERE] * len(held),
        out_specs=(ANYWHERE, ANYWHERE, ANYWHERE, VMEM),
        scratch_shapes=[
            pltpu.VMEM((3, length, width), jnp.float32),
            pltpu.SemaphoreType.DMA((3, len(pieces))),
        ],
        input_output_aliases={inputs + i: i for i in range(len(held))},
        compiler_params=pltpu.CompilerParams(vmem_limit_bytes=24 << 20),
        cost_estimate=pl.CostEstimate(
            flops=length * width, bytes_accessed=length * width, transcendentals=0
        ),
    )(*terms, *states, *held)


def choose_kernel(owner_count, plan_ref, *refs):
    candidates, chosen = refs[:owner_count], refs[owner_count:]
    own_block, own_expert = place(owner_count)
    for step, out in enumerate(chosen):
        wanted = plan_ref[lax.rem(own_block + step, QUART) * owner_count + own_expert]
        for mate, candidate in enumerate(candidates):

            @pl.when(wanted == own_expert ^ mate)
            def _():
                out[...] = candidate[...]


def offer_kernel(owner_count, plan_ref, *refs):
    held, out = refs[:-1], refs[-1]
    own_block, own_expert = place(owner_count)
    wanted = plan_ref[own_block * owner_count + (own_expert ^ 1)]
    rows = out.shape[1]
    for pair, blocks in enumerate(held):

        @pl.when((wanted ^ own_expert) >> 1 == pair)
        def _():
            for step in range(QUART):
                out[step] = blocks[step * rows : (step + 1) * rows, :]


def assemble_kernel(owner_count, span, later, plan_ref, *refs):
    *blocks, out, sems = refs
    own_block, own_expert = place(owner_count)
    apart = plan_ref[own_block * owner_count + own_expert] ^ own_expert
    first, rows = span
    half = owner_count // 2

    def put(sources, start, group):
        copies = []
        for step, source in enumerate(sources):
            width = source.shape[1]
            column = pl.multiple_of(lax.rem(own_block + QUART - step, QUART) * width, LANES)
            target = out.at[pl.ds(start, source.shape[0]), pl.ds(column, width)]
            copies.append(pltpu.make_async_copy(source, target, sems.at[group, step]))
            copies[-1].start()
        return copies

    def finish(copies):
        for copy in copies:
            copy.wait()

    if later:
        offered, _ = blocks

        @pl.when(apart & 1 == 1)
        def _():
            finish(put([offered.at[step] for step in range(QUART)], first, 0))

        return

    held, received = blocks[:half], blocks[half:]
    others = put(received, first + rows, 0)
    for pair in range(half):

        @pl.when(apart == 2 * pair)
        def _():
            lines = [held[pair].at[pl.ds(step * rows, rows), :] for step in range(QUART)]
            finish(put(lines, first, 1))

    finish(others)


def assemble(owner_count, span, plan, blocks, shape, held=None):
    later = held is not None
    inputs = [*blocks, held] if later else blocks
    return pl.pallas_call(
        functools.partial(assemble_kernel, owner_count, span, later),
        out_shape=shape,
        in_specs=[SMEM] + [VMEM] * len(blocks) + [ANYWHERE] * later,
        out_specs=ANYWHERE,
        scratch_shapes=[pltpu.SemaphoreType.DMA((2, QUART))],
        input_output_aliases={1 + len(blocks): 0} if later else {},
        compiler_params=pltpu.CompilerParams(vmem_limit_bytes=vmem_for(*blocks)),
        cost_estimate=pl.CostEstimate(flops=1, bytes_accessed=1 << 14, transcendentals=0),
    )(plan, *inputs)


def per_device(
    hidden_rows, grad_rows, block_slot, live_rows, replica_plan, master, moment_one, moment_two
):
    owner_count = lax.axis_size("expert") // QUART
    groups = lax.axis_size("dp")
    hidden_units, tok_rows = hidden_rows.shape
    block_width = grad_rows.shape[1] // QUART
    share_rows = hidden_units // groups
    assert block_slot.shape[1] == 1 and tok_rows == LANES and block_width % LANES == 0
    shape = jax.ShapeDtypeStruct
    lead = share_rows * 13 // 24 // 16 * 16
    spans = ((0, lead), (lead, share_rows - lead))

    head_rows = (block_width // LANES) * tok_rows + META_ROWS
    outs = [shape((head_rows + groups * lead, LANES), jnp.bfloat16)] * QUART
    outs += [shape((groups * (share_rows - lead), LANES), jnp.bfloat16)]
    messages = call(
        functools.partial(message_kernel, owner_count, spans),
        outs,
        (block_slot, live_rows),
        (hidden_rows, grad_rows),
    )

    def across(block, step):
        return from_behind(block, "expert", step * owner_count) if step else block

    first_bit = owner_count // 2
    other_bits = [1 << i for i in reversed(range(first_bit.bit_length() - 1))]
    own = [([(0, 0)], messages[0])]
    sides = [([(step, 0)], across(messages[step], step)) for step in (1, 3)]
    keys, block = exchange(own, first_bit)
    own += [(keys, after(block, *(side for _, side in sides))), *sides]
    last = [([(2, 0)], across(after(messages[2], own[1][1]), 2))]
    crossed = [exchange(sides, first_bit)]
    last_crossed = exchange(last, first_bit)
    for bit in other_bits:
        own += [exchange(own, bit)]
        last += [exchange(last, bit)]
    later = after(messages[QUART], last[-1][1], crossed[0][1])
    rest = [([(0, 0)], messages[QUART])]
    rest += [([(step, 0)], across(later, step)) for step in (1, 2, 3)]
    keys, block = last_crossed
    crossed += [(keys, after(block, *(part for _, part in rest[1:])))]
    for bit in other_bits:
        crossed += [exchange(crossed, bit)]
    last += crossed
    heads = own + last
    head_at = places(heads, 0)
    rests, rest_at = [], {}

    def partials(at, steps, wait_for):
        rows = spans[at][1]
        packs = heads + rests if at else heads
        where = [(key, found, rest_at[key] if at else found) for key, found in head_at.items()]
        return call(
            functools.partial(
                partial_kernel, owner_count, tok_rows, where, 0 if at else head_rows, steps
            ),
            [shape((rows, block_width), jnp.float32)] * len(steps),
            (after(replica_plan, *wait_for),),
            [block for _, block in packs],
            2 * len(steps) * rows * tok_rows * block_width * QUART,
        )

    states = (master[0], moment_one[0], moment_two[0])
    ahead = tuple(range(1, groups))
    block = lambda rows: shape((rows, block_width), jnp.bfloat16)

    far_one = partials(0, ahead, ())
    came_one = [from_behind(p, "dp", step) for step, p in zip(ahead, far_one)]
    near_one = partials(0, (0,), far_one)

    rest[1:] = [(keys, after(part, *far_one)) for keys, part in rest[1:]]
    for pair in (rest[:2], rest[2:]):
        keys, parts = zip(*pair)
        pair = [(sum(keys, []), jnp.concatenate(parts))]
        pair += [exchange(pair, first_bit)]
        for pack in pair:
            group = [pack]
            for bit in other_bits:
                group += [exchange(group, bit)]
            rests += group
    rest_at.update(places(rests, len(heads)))

    far_two = partials(1, ahead, near_one)
    came_one = [after(term, *far_two) for term in came_one]
    *held, fresh_one = update((*near_one, *came_one), states, spans[0], ())
    came_two = [
        from_behind(after(p, fresh_one), "dp", step) for step, p in zip(ahead, far_two)
    ]
    near_two = partials(1, (0,), (fresh_one,))

    lines = [across(fresh_one, step) for step in range(QUART)]

    came_two = [after(term, fresh_one) for term in came_two]
    *held, fresh_two = update((*near_two, *came_two), states, spans[1], held)

    mates_two = gather_mates(fresh_two, "expert", owner_count)
    lines[1:] = [after(line, mates_two[owner_count // 2]) for line in lines[1:]]
    chosen = call(
        functools.partial(choose_kernel, owner_count),
        [block(spans[1][1])] * QUART,
        (after(replica_plan, *lines),),
        mates_two,
    )
    received = [across(c, step) for step, c in enumerate(chosen)]

    wide = gather_mates(jnp.concatenate(lines), "expert", owner_count, 2)[::2]
    (offer,) = call(
        functools.partial(offer_kernel, owner_count),
        [shape((QUART, spans[0][1], block_width), jnp.bfloat16)],
        (replica_plan,),
        wide,
    )
    result = shape((share_rows, QUART * block_width), jnp.bfloat16)
    placed = assemble(
        owner_count, spans[0], replica_plan, [*wide, *received], result
    )
    offer = from_mate(after(offer, *received[1:]), "expert", 1)
    replica_weight = assemble(owner_count, spans[0], replica_plan, [offer], result, placed)
    return (*(state[None] for state in held), replica_weight[None])


def solution(mesh):
    return jax.shard_map(
        per_device,
        mesh=mesh,
        in_specs=(
            P(None, ("dp", "expert")),
            P(("dp", "expert"), None),
            P(("dp", "expert"), None),
            P(("dp", "expert")),
            P(),
            P("expert", "dp", None),
            P("expert", "dp", None),
            P("expert", "dp", None),
        ),
        out_specs=(
            P("expert", "dp", None),
            P("expert", "dp", None),
            P("expert", "dp", None),
            P("expert", "dp", None),
        ),
        check_vma=False,
    )
```

```python
import functools

import jax
import jax.numpy as jnp
from jax import lax
from jax.experimental import pallas as pl
from jax.experimental.pallas import tpu as pltpu
from jax.sharding import PartitionSpec as P

QUART = 4
LANES = 128
META_ROWS = 16


beta_one = 0.9
beta_two = 0.95
learn_rate = 0.01
decay_rate = 0.1
epsilon = 1e-08
step_count = 10.0

VMEM = pl.BlockSpec(memory_space=pltpu.VMEM)
SMEM = pl.BlockSpec(memory_space=pltpu.SMEM)
ANYWHERE = pl.BlockSpec(memory_space=pl.ANY)


def vmem_for(*arrays):
    return int(sum(a.size * a.dtype.itemsize for a in arrays) * 5 // 4) + (8 << 20)


def call(kernel, out_shapes, scalars, arrays, flops=0):
    moved = sum(a.size * a.dtype.itemsize for a in (*arrays, *out_shapes))
    return pl.pallas_call(
        kernel,
        out_shape=tuple(out_shapes),
        in_specs=[SMEM] * len(scalars) + [VMEM] * len(arrays),
        out_specs=tuple([VMEM] * len(out_shapes)),
        compiler_params=pltpu.CompilerParams(vmem_limit_bytes=vmem_for(*arrays, *out_shapes)),
        cost_estimate=pl.CostEstimate(flops=flops // 64, bytes_accessed=moved // 64, transcendentals=0),
    )(*scalars, *arrays)


def from_behind(block, axis, distance):
    devices = range(lax.axis_size(axis))
    route = [((i - distance) % len(devices), i) for i in devices]
    return lax.ppermute(block, axis, route)


def from_mate(block, axis, bit):
    return lax.ppermute(block, axis, [(i ^ bit, i) for i in range(lax.axis_size(axis))])


def gather_mates(block, axis, count, least=1):
    held = {0: block}
    bit = count // 2
    while bit >= least:
        held.update({m | bit: from_mate(held[m], axis, bit) for m in list(held)})
        bit //= 2
    return [held.get(m) for m in range(count)]


def after(value, *others):
    return lax.optimization_barrier((value, *others))[0] if others else value


def exchange(packs, bit):
    keys = [(step, mate | bit) for pack, _ in packs for step, mate in pack]
    blocks = [block for _, block in packs]
    return keys, from_mate(jnp.concatenate(blocks) if len(blocks) > 1 else blocks[0], "expert", bit)


def places(packs, first):
    found = {}
    for at, (keys, block) in enumerate(packs):
        rows = block.shape[0] // len(keys)
        found.update({key: (first + at, i * rows) for i, key in enumerate(keys)})
    return found


def place(owner_count):
    own = lax.axis_index("expert")
    return own // owner_count, own % owner_count


def message_kernel(owner_count, spans, slot_ref, live_ref, hidden_ref, grad_ref, *message_refs):
    own_block, _ = place(owner_count)
    groups = lax.axis_size("dp")
    hidden_units, tok_rows = hidden_ref.shape
    share_rows = hidden_units // groups
    block_width = grad_ref.shape[1] // QUART
    parts = block_width // LANES
    live = live_ref[0]
    slot = slot_ref[0, 0]
    kept = lax.broadcasted_iota(jnp.int32, (tok_rows, LANES), 0) < live
    meta = jnp.full((META_ROWS, LANES), slot.astype(jnp.float32)).astype(jnp.bfloat16)

    def put_hidden(message, row, span):
        first, length = span
        for group in range(groups):
            start = group * share_rows + first
            message[row : row + length, :] = hidden_ref[start : start + length, :]
            row += length

    for step, message in enumerate(message_refs[:QUART]):
        target = lax.rem(own_block + step, QUART)
        for part in range(parts):
            start = pl.multiple_of(target * block_width + part * LANES, LANES)
            columns = grad_ref[:, pl.ds(start, LANES)].astype(jnp.float32)
            row = part * tok_rows
            message[row : row + tok_rows, :] = jnp.where(kept, columns, 0.0).astype(jnp.bfloat16)
        row = parts * tok_rows
        message[row : row + META_ROWS, :] = meta
        put_hidden(message, row + META_ROWS, spans[0])
    for message, span in zip(message_refs[QUART:], spans[1:]):
        put_hidden(message, 0, span)


def partial_kernel(owner_count, tok_rows, where, base, steps, plan_ref, *refs):
    totals = refs[-len(steps) :]
    own_block, own_expert = place(owner_count)
    group, groups = lax.axis_index("dp"), lax.axis_size("dp")
    rows, block_width = totals[0].shape
    parts = block_width // LANES
    chunk = next(c for c in (208, 192, 176, 128, 112, 96, 64, 48, 32, 16) if rows % c == 0)
    bits = []
    for first in range(0, len(where), 16):
        packed = jnp.zeros((META_ROWS, LANES), jnp.float32)
        for at, (_, (head, row), _) in enumerate(where[first : first + 16]):
            meta = refs[head][row + parts * tok_rows : row + parts * tok_rows + META_ROWS, :]
            packed = packed + meta.astype(jnp.float32) * float(1 << at)
        bits.append(jnp.max(packed).astype(jnp.int32))
    for total in totals:
        total[...] = jnp.zeros_like(total)
    for at, ((step, mate), (head, head_row), (tail, tail_row)) in enumerate(where):
        source_expert = own_expert ^ mate
        source = lax.rem(own_block + QUART - step, QUART) * owner_count + source_expert
        is_replica = ((bits[at // 16] >> (at % 16)) & 1) == 1
        target = jnp.where(is_replica, plan_ref[source], source_expert)

        columns = jnp.concatenate(
            [
                refs[head][head_row + p * tok_rows : head_row + (p + 1) * tok_rows, :]
                for p in range(parts)
            ],
            axis=1,
        )

        def add(rounded):
            for total, ahead in zip(totals, steps):
                start = tail_row + base + lax.rem(group + ahead, groups) * rows

                @pl.loop(0, rows // chunk)
                def _(i):
                    term = jnp.dot(
                        refs[tail][pl.ds(pl.multiple_of(start + i * chunk, 16), chunk), :],
                        columns,
                        preferred_element_type=jnp.float32,
                    )
                    if rounded:
                        term = term.astype(jnp.bfloat16).astype(jnp.float32)
                    into = pl.ds(pl.multiple_of(i * chunk, 16), chunk)
                    total[into, :] += term

        if mate == 0:
            pl.when((target == own_expert) & jnp.logical_not(is_replica))(lambda: add(False))
        pl.when((target == own_expert) & is_replica)(lambda: add(True))


def update_kernel(parts, held, span, pieces, *refs):
    terms, (master, one, two) = refs[:parts], refs[parts : parts + 3]
    *outs, fresh, new_rows, sems = refs[parts + 3 + held :]
    first, _ = span
    copies = []
    for at, (start, size) in enumerate(pieces):
        inside, placed = pl.ds(start, size), pl.ds(first + start, size)
        gradient = terms[0][inside, :]
        for term in terms[1:]:
            gradient = gradient + term[inside, :]
        weights = master[placed, :]
        first_next = beta_one * one[placed, :] + (1.0 - beta_one) * gradient
        second_next = beta_two * two[placed, :] + (1.0 - beta_two) * gradient * gradient
        scaled_first = first_next / (1.0 - beta_one**step_count)
        scaled_second = second_next / (1.0 - beta_two**step_count)
        direction = scaled_first / (jnp.sqrt(scaled_second) + epsilon)
        weights_next = weights - learn_rate * (direction + decay_rate * weights)
        fresh[inside, :] = weights_next.astype(jnp.bfloat16)
        for which, value in enumerate((weights_next, first_next, second_next)):
            new_rows[which, inside, :] = value
            copies.append(
                pltpu.make_async_copy(
                    new_rows.at[which, inside, :], outs[which].at[placed, :], sems.at[which, at]
                )
            )
            copies[-1].start()
    for copy in copies:
        copy.wait()


def update(terms, states, span, held):
    length = span[1]
    rows, width = states[0].shape
    pieces = [(start, min(64, length - start)) for start in range(0, length, 64)]
    whole = jax.ShapeDtypeStruct((rows, width), jnp.float32)
    inputs = len(terms) + len(states)
    return pl.pallas_call(
        functools.partial(update_kernel, len(terms), len(held), span, pieces),
        out_shape=(whole, whole, whole, jax.ShapeDtypeStruct((length, width), jnp.bfloat16)),
        in_specs=[VMEM] * inputs + [ANYWHERE] * len(held),
        out_specs=(ANYWHERE, ANYWHERE, ANYWHERE, VMEM),
        scratch_shapes=[
            pltpu.VMEM((3, length, width), jnp.float32),
            pltpu.SemaphoreType.DMA((3, len(pieces))),
        ],
        input_output_aliases={inputs + i: i for i in range(len(held))},
        compiler_params=pltpu.CompilerParams(vmem_limit_bytes=24 << 20),
        cost_estimate=pl.CostEstimate(
            flops=length * width, bytes_accessed=length * width, transcendentals=0
        ),
    )(*terms, *states, *held)


def choose_kernel(owner_count, plan_ref, *refs):
    candidates, chosen = refs[:owner_count], refs[owner_count:]
    own_block, own_expert = place(owner_count)
    for step, out in enumerate(chosen):
        wanted = plan_ref[lax.rem(own_block + step, QUART) * owner_count + own_expert]
        for mate, candidate in enumerate(candidates):

            @pl.when(wanted == own_expert ^ mate)
            def _():
                out[...] = candidate[...]


def offer_kernel(owner_count, plan_ref, *refs):
    held, out = refs[:-1], refs[-1]
    own_block, own_expert = place(owner_count)
    wanted = plan_ref[own_block * owner_count + (own_expert ^ 1)]
    rows = out.shape[0]
    for pair, blocks in enumerate(held):

        @pl.when((wanted ^ own_expert) >> 1 == pair)
        def _():
            for step in range(QUART):
                width = blocks.shape[1]
                column = pl.multiple_of(lax.rem(own_block + QUART - step, QUART) * width, LANES)
                out[:, pl.ds(column, width)] = blocks[step * rows : (step + 1) * rows, :]


def assemble_kernel(owner_count, span, later, plan_ref, *refs):
    *blocks, out, sems = refs
    own_block, own_expert = place(owner_count)
    apart = plan_ref[own_block * owner_count + own_expert] ^ own_expert
    first, rows = span
    half = owner_count // 2

    def put(sources, start, group):
        copies = []
        for step, source in enumerate(sources):
            width = source.shape[1]
            column = pl.multiple_of(lax.rem(own_block + QUART - step, QUART) * width, LANES)
            target = out.at[pl.ds(start, source.shape[0]), pl.ds(column, width)]
            copies.append(pltpu.make_async_copy(source, target, sems.at[group, step]))
            copies[-1].start()
        return copies

    def finish(copies):
        for copy in copies:
            copy.wait()

    if later:
        offered, _ = blocks

        @pl.when(apart & 1 == 1)
        def _():
            copy = pltpu.make_async_copy(offered, out.at[pl.ds(first, rows), :], sems.at[0, 0])
            copy.start()
            copy.wait()

        return

    held, received = blocks[:half], blocks[half:]
    others = put(received, first + rows, 0)
    for pair in range(half):

        @pl.when(apart == 2 * pair)
        def _():
            lines = [held[pair].at[pl.ds(step * rows, rows), :] for step in range(QUART)]
            finish(put(lines, first, 1))

    finish(others)


def assemble(owner_count, span, plan, blocks, shape, held=None):
    later = held is not None
    inputs = [*blocks, held] if later else blocks
    return pl.pallas_call(
        functools.partial(assemble_kernel, owner_count, span, later),
        out_shape=shape,
        in_specs=[SMEM] + [VMEM] * len(blocks) + [ANYWHERE] * later,
        out_specs=ANYWHERE,
        scratch_shapes=[pltpu.SemaphoreType.DMA((2, QUART))],
        input_output_aliases={1 + len(blocks): 0} if later else {},
        compiler_params=pltpu.CompilerParams(vmem_limit_bytes=vmem_for(*blocks)),
        cost_estimate=pl.CostEstimate(flops=1, bytes_accessed=1 << 14, transcendentals=0),
    )(plan, *inputs)


def per_device(
    hidden_rows, grad_rows, block_slot, live_rows, replica_plan, master, moment_one, moment_two
):
    owner_count = lax.axis_size("expert") // QUART
    groups = lax.axis_size("dp")
    hidden_units, tok_rows = hidden_rows.shape
    block_width = grad_rows.shape[1] // QUART
    share_rows = hidden_units // groups
    assert block_slot.shape[1] == 1 and tok_rows == LANES and block_width % LANES == 0
    shape = jax.ShapeDtypeStruct
    lead = share_rows * 13 // 24 // 16 * 16
    spans = ((0, lead), (lead, share_rows - lead))

    head_rows = (block_width // LANES) * tok_rows + META_ROWS
    outs = [shape((head_rows + groups * lead, LANES), jnp.bfloat16)] * QUART
    outs += [shape((groups * (share_rows - lead), LANES), jnp.bfloat16)]
    messages = call(
        functools.partial(message_kernel, owner_count, spans),
        outs,
        (block_slot, live_rows),
        (hidden_rows, grad_rows),
    )

    def across(block, step):
        return from_behind(block, "expert", step * owner_count) if step else block

    first_bit = owner_count // 2
    other_bits = [1 << i for i in reversed(range(first_bit.bit_length() - 1))]
    own = [([(0, 0)], messages[0])]
    sides = [([(step, 0)], across(messages[step], step)) for step in (1, 3)]
    keys, block = exchange(own, first_bit)
    own += [(keys, after(block, *(side for _, side in sides))), *sides]
    last = [([(2, 0)], across(after(messages[2], own[1][1]), 2))]
    crossed = [exchange(sides, first_bit)]
    last_crossed = exchange(last, first_bit)
    for bit in other_bits:
        own += [exchange(own, bit)]
        last += [exchange(last, bit)]
    later = after(messages[QUART], last[-1][1], crossed[0][1])
    rest = [([(0, 0)], messages[QUART])]
    rest += [([(step, 0)], across(later, step)) for step in (1, 2, 3)]
    keys, block = last_crossed
    crossed += [(keys, after(block, *(part for _, part in rest[1:])))]
    for bit in other_bits:
        crossed += [exchange(crossed, bit)]
    last += crossed
    heads = own + last
    head_at = places(heads, 0)
    rests, rest_at = [], {}

    def partials(at, steps, wait_for):
        rows = spans[at][1]
        packs = heads + rests if at else heads
        where = [(key, found, rest_at[key] if at else found) for key, found in head_at.items()]
        return call(
            functools.partial(
                partial_kernel, owner_count, tok_rows, where, 0 if at else head_rows, steps
            ),
            [shape((rows, block_width), jnp.float32)] * len(steps),
            (after(replica_plan, *wait_for),),
            [block for _, block in packs],
            2 * len(steps) * rows * tok_rows * block_width * QUART,
        )

    states = (master[0], moment_one[0], moment_two[0])
    ahead = tuple(range(1, groups))
    block = lambda rows: shape((rows, block_width), jnp.bfloat16)

    far_one = partials(0, ahead, ())
    came_one = [from_behind(p, "dp", step) for step, p in zip(ahead, far_one)]
    near_one = partials(0, (0,), far_one)

    keys, parts = zip(*rest)
    stack = jnp.concatenate(parts)
    rest = [(sum(keys, []), stack)]
    rest += [exchange(rest, first_bit)]
    for pack in rest:
        group = [pack]
        for bit in other_bits:
            group += [exchange(group, bit)]
        rests += group
    rest_at.update(places(rests, len(heads)))

    far_two = partials(1, ahead, near_one)
    came_one = [after(term, *far_two) for term in came_one]
    *held, fresh_one = update((*near_one, *came_one), states, spans[0], ())
    came_two = [
        from_behind(after(p, fresh_one), "dp", step) for step, p in zip(ahead, far_two)
    ]
    near_two = partials(1, (0,), (fresh_one,))

    lines = [across(fresh_one, step) for step in range(QUART)]

    came_two = [after(term, fresh_one) for term in came_two]
    *held, fresh_two = update((*near_two, *came_two), states, spans[1], held)

    mates_two = gather_mates(fresh_two, "expert", owner_count)
    lines[1:] = [after(line, mates_two[owner_count // 2]) for line in lines[1:]]
    chosen = call(
        functools.partial(choose_kernel, owner_count),
        [block(spans[1][1])] * QUART,
        (after(replica_plan, *lines),),
        mates_two,
    )
    received = [across(c, step) for step, c in enumerate(chosen)]

    wide = gather_mates(jnp.concatenate(lines), "expert", owner_count, 2)[::2]
    (offer,) = call(
        functools.partial(offer_kernel, owner_count),
        [shape((spans[0][1], QUART * block_width), jnp.bfloat16)],
        (replica_plan,),
        wide,
    )
    result = shape((share_rows, QUART * block_width), jnp.bfloat16)
    placed = assemble(
        owner_count, spans[0], replica_plan, [*wide, *received], result
    )
    offer = from_mate(after(offer, *received[1:]), "expert", 1)
    replica_weight = assemble(owner_count, spans[0], replica_plan, [offer], result, placed)
    return (*(state[None] for state in held), replica_weight[None])


def solution(mesh):
    return jax.shard_map(
        per_device,
        mesh=mesh,
        in_specs=(
            P(None, ("dp", "expert")),
            P(("dp", "expert"), None),
            P(("dp", "expert"), None),
            P(("dp", "expert")),
            P(),
            P("expert", "dp", None),
            P("expert", "dp", None),
            P("expert", "dp", None),
        ),
        out_specs=(
            P("expert", "dp", None),
            P("expert", "dp", None),
            P("expert", "dp", None),
            P("expert", "dp", None),
        ),
        check_vma=False,
    )
```

```python
import functools

import jax
import jax.numpy as jnp
from jax import lax
from jax.experimental import pallas as pl
from jax.experimental.pallas import tpu as pltpu
from jax.sharding import PartitionSpec as P

QUART = 4
LANES = 128
META_ROWS = 16


beta_one = 0.9
beta_two = 0.95
learn_rate = 0.01
decay_rate = 0.1
epsilon = 1e-08
step_count = 10.0

VMEM = pl.BlockSpec(memory_space=pltpu.VMEM)
SMEM = pl.BlockSpec(memory_space=pltpu.SMEM)
ANYWHERE = pl.BlockSpec(memory_space=pl.ANY)


def vmem_for(*arrays):
    return int(sum(a.size * a.dtype.itemsize for a in arrays) * 5 // 4) + (8 << 20)


def call(kernel, out_shapes, scalars, arrays, flops=0):
    moved = sum(a.size * a.dtype.itemsize for a in (*arrays, *out_shapes))
    return pl.pallas_call(
        kernel,
        out_shape=tuple(out_shapes),
        in_specs=[SMEM] * len(scalars) + [VMEM] * len(arrays),
        out_specs=tuple([VMEM] * len(out_shapes)),
        compiler_params=pltpu.CompilerParams(vmem_limit_bytes=vmem_for(*arrays, *out_shapes)),
        cost_estimate=pl.CostEstimate(flops=flops // 64, bytes_accessed=moved // 64, transcendentals=0),
    )(*scalars, *arrays)


def from_behind(block, axis, distance):
    devices = range(lax.axis_size(axis))
    route = [((i - distance) % len(devices), i) for i in devices]
    return lax.ppermute(block, axis, route)


def from_mate(block, axis, bit):
    return lax.ppermute(block, axis, [(i ^ bit, i) for i in range(lax.axis_size(axis))])


def gather_mates(block, axis, count, least=1):
    held = {0: block}
    bit = count // 2
    while bit >= least:
        held.update({m | bit: from_mate(held[m], axis, bit) for m in list(held)})
        bit //= 2
    return [held.get(m) for m in range(count)]


def after(value, *others):
    return lax.optimization_barrier((value, *others))[0] if others else value


def exchange(packs, bit):
    keys = [(step, mate | bit) for pack, _ in packs for step, mate in pack]
    blocks = [block for _, block in packs]
    return keys, from_mate(jnp.concatenate(blocks) if len(blocks) > 1 else blocks[0], "expert", bit)


def places(packs, first):
    found = {}
    for at, (keys, block) in enumerate(packs):
        rows = block.shape[0] // len(keys)
        found.update({key: (first + at, i * rows) for i, key in enumerate(keys)})
    return found


def place(owner_count):
    own = lax.axis_index("expert")
    return own // owner_count, own % owner_count


def message_kernel(owner_count, spans, slot_ref, live_ref, hidden_ref, grad_ref, *message_refs):
    own_block, _ = place(owner_count)
    groups = lax.axis_size("dp")
    hidden_units, tok_rows = hidden_ref.shape
    share_rows = hidden_units // groups
    block_width = grad_ref.shape[1] // QUART
    parts = block_width // LANES
    live = live_ref[0]
    slot = slot_ref[0, 0]
    kept = lax.broadcasted_iota(jnp.int32, (tok_rows, LANES), 0) < live
    meta = jnp.full((META_ROWS, LANES), slot.astype(jnp.float32)).astype(jnp.bfloat16)

    def put_hidden(message, row, span):
        first, length = span
        for group in range(groups):
            start = group * share_rows + first
            message[row : row + length, :] = hidden_ref[start : start + length, :]
            row += length

    for step, message in enumerate(message_refs[:QUART]):
        target = lax.rem(own_block + step, QUART)
        for part in range(parts):
            start = pl.multiple_of(target * block_width + part * LANES, LANES)
            columns = grad_ref[:, pl.ds(start, LANES)].astype(jnp.float32)
            row = part * tok_rows
            message[row : row + tok_rows, :] = jnp.where(kept, columns, 0.0).astype(jnp.bfloat16)
        row = parts * tok_rows
        message[row : row + META_ROWS, :] = meta
        put_hidden(message, row + META_ROWS, spans[0])
    for message, span in zip(message_refs[QUART:], spans[1:]):
        put_hidden(message, 0, span)


def partial_kernel(owner_count, tok_rows, where, base, steps, plan_ref, *refs):
    totals = refs[-len(steps) :]
    own_block, own_expert = place(owner_count)
    group, groups = lax.axis_index("dp"), lax.axis_size("dp")
    rows, block_width = totals[0].shape
    parts = block_width // LANES
    chunk = next(c for c in (208, 192, 176, 128, 112, 96, 64, 48, 32, 16) if rows % c == 0)
    bits = []
    for first in range(0, len(where), 16):
        packed = jnp.zeros((META_ROWS, LANES), jnp.float32)
        for at, (_, (head, row), _) in enumerate(where[first : first + 16]):
            meta = refs[head][row + parts * tok_rows : row + parts * tok_rows + META_ROWS, :]
            packed = packed + meta.astype(jnp.float32) * float(1 << at)
        bits.append(jnp.max(packed).astype(jnp.int32))
    for total in totals:
        total[...] = jnp.zeros_like(total)
    for at, ((step, mate), (head, head_row), (tail, tail_row)) in enumerate(where):
        source_expert = own_expert ^ mate
        source = lax.rem(own_block + QUART - step, QUART) * owner_count + source_expert
        is_replica = ((bits[at // 16] >> (at % 16)) & 1) == 1
        target = jnp.where(is_replica, plan_ref[source], source_expert)

        columns = jnp.concatenate(
            [
                refs[head][head_row + p * tok_rows : head_row + (p + 1) * tok_rows, :]
                for p in range(parts)
            ],
            axis=1,
        )

        def add(rounded):
            for total, ahead in zip(totals, steps):
                start = tail_row + base + lax.rem(group + ahead, groups) * rows

                @pl.loop(0, rows // chunk)
                def _(i):
                    term = jnp.dot(
                        refs[tail][pl.ds(pl.multiple_of(start + i * chunk, 16), chunk), :],
                        columns,
                        preferred_element_type=jnp.float32,
                    )
                    if rounded:
                        term = term.astype(jnp.bfloat16).astype(jnp.float32)
                    into = pl.ds(pl.multiple_of(i * chunk, 16), chunk)
                    total[into, :] += term

        if mate == 0:
            pl.when((target == own_expert) & jnp.logical_not(is_replica))(lambda: add(False))
        pl.when((target == own_expert) & is_replica)(lambda: add(True))


def new_rows(terms, states, first, start, size):
    inside, placed = pl.ds(start, size), pl.ds(first + start, size)
    master, one, two = states
    gradient = terms[0][inside, :]
    for term in terms[1:]:
        gradient = gradient + term[inside, :]
    weights = master[placed, :]
    first_next = beta_one * one[placed, :] + (1.0 - beta_one) * gradient
    second_next = beta_two * two[placed, :] + (1.0 - beta_two) * gradient * gradient
    scaled_first = first_next / (1.0 - beta_one**step_count)
    scaled_second = second_next / (1.0 - beta_two**step_count)
    direction = scaled_first / (jnp.sqrt(scaled_second) + epsilon)
    weights_next = weights - learn_rate * (direction + decay_rate * weights)
    return weights_next, first_next, second_next


def update_kernel(parts, first, pieces, *refs):
    terms, states, outs = refs[:parts], refs[parts : parts + 3], refs[parts + 3 :]
    for start, size in pieces:
        values = new_rows(terms, states, first, start, size)
        for out, value in zip(outs, (*values, values[0].astype(jnp.bfloat16))):
            out[pl.ds(start, size), :] = value


def finish_kernel(parts, first, pieces, *refs):
    terms, states, made = refs[:parts], refs[parts : parts + 3], refs[parts + 3 : parts + 6]
    *outs, fresh, fresh_states, sems = refs[parts + 6 :]
    copies = [
        pltpu.make_async_copy(rows, out.at[pl.ds(0, first), :], sems.at[which, 0])
        for which, (rows, out) in enumerate(zip(made, outs))
    ]
    for copy in copies:
        copy.start()
    for at, (start, size) in enumerate(pieces):
        inside, placed = pl.ds(start, size), pl.ds(first + start, size)
        values = new_rows(terms, states, first, start, size)
        fresh[inside, :] = values[0].astype(jnp.bfloat16)
        for which, value in enumerate(values):
            fresh_states[which, inside, :] = value
            copies.append(
                pltpu.make_async_copy(
                    fresh_states.at[which, inside, :],
                    outs[which].at[placed, :],
                    sems.at[which, at + 1],
                )
            )
            copies[-1].start()
    for copy in copies:
        copy.wait()


def update(terms, states, span, made=()):
    first, length = span
    rows, width = states[0].shape
    pieces = [(start, min(64, length - start)) for start in range(0, length, 64)]
    part = jax.ShapeDtypeStruct((length, width), jnp.float32)
    whole = jax.ShapeDtypeStruct((rows, width), jnp.float32)
    scratch = [
        pltpu.VMEM((3, length, width), jnp.float32),
        pltpu.SemaphoreType.DMA((3, len(pieces) + 1)),
    ]
    return pl.pallas_call(
        functools.partial(finish_kernel if made else update_kernel, len(terms), first, pieces),
        out_shape=(
            *([whole if made else part] * 3),
            jax.ShapeDtypeStruct((length, width), jnp.bfloat16),
        ),
        in_specs=[VMEM] * (len(terms) + len(states) + len(made)),
        out_specs=(*([ANYWHERE if made else VMEM] * 3), VMEM),
        scratch_shapes=scratch if made else [],
        compiler_params=pltpu.CompilerParams(vmem_limit_bytes=24 << 20),
        cost_estimate=pl.CostEstimate(
            flops=length * width, bytes_accessed=length * width, transcendentals=0
        ),
    )(*terms, *states, *made)


def choose_kernel(owner_count, plan_ref, *refs):
    candidates, chosen = refs[:owner_count], refs[owner_count:]
    own_block, own_expert = place(owner_count)
    for step, out in enumerate(chosen):
        wanted = plan_ref[lax.rem(own_block + step, QUART) * owner_count + own_expert]
        for mate, candidate in enumerate(candidates):

            @pl.when(wanted == own_expert ^ mate)
            def _():
                out[...] = candidate[...]


def offer_kernel(owner_count, plan_ref, *refs):
    held, out = refs[:-1], refs[-1]
    own_block, own_expert = place(owner_count)
    wanted = plan_ref[own_block * owner_count + (own_expert ^ 1)]
    rows = out.shape[0]
    for pair, blocks in enumerate(held):

        @pl.when((wanted ^ own_expert) >> 1 == pair)
        def _():
            for step in range(QUART):
                width = blocks.shape[1]
                column = pl.multiple_of(lax.rem(own_block + QUART - step, QUART) * width, LANES)
                out[:, pl.ds(column, width)] = blocks[step * rows : (step + 1) * rows, :]


def assemble_kernel(owner_count, span, later, plan_ref, *refs):
    *blocks, out, sems = refs
    own_block, own_expert = place(owner_count)
    apart = plan_ref[own_block * owner_count + own_expert] ^ own_expert
    first, rows = span
    half = owner_count // 2

    def put(sources, start, group):
        copies = []
        for step, source in enumerate(sources):
            width = source.shape[1]
            column = pl.multiple_of(lax.rem(own_block + QUART - step, QUART) * width, LANES)
            target = out.at[pl.ds(start, source.shape[0]), pl.ds(column, width)]
            copies.append(pltpu.make_async_copy(source, target, sems.at[group, step]))
            copies[-1].start()
        return copies

    def finish(copies):
        for copy in copies:
            copy.wait()

    if later:
        offered, _ = blocks

        @pl.when(apart & 1 == 1)
        def _():
            copy = pltpu.make_async_copy(offered, out.at[pl.ds(first, rows), :], sems.at[0, 0])
            copy.start()
            copy.wait()

        return

    held, received = blocks[:half], blocks[half:]
    others = put(received, first + rows, 0)
    for pair in range(half):

        @pl.when(apart == 2 * pair)
        def _():
            lines = [held[pair].at[pl.ds(step * rows, rows), :] for step in range(QUART)]
            finish(put(lines, first, 1))

    finish(others)


def assemble(owner_count, span, plan, blocks, shape, held=None):
    later = held is not None
    inputs = [*blocks, held] if later else blocks
    return pl.pallas_call(
        functools.partial(assemble_kernel, owner_count, span, later),
        out_shape=shape,
        in_specs=[SMEM] + [VMEM] * len(blocks) + [ANYWHERE] * later,
        out_specs=ANYWHERE,
        scratch_shapes=[pltpu.SemaphoreType.DMA((2, QUART))],
        input_output_aliases={1 + len(blocks): 0} if later else {},
        compiler_params=pltpu.CompilerParams(vmem_limit_bytes=vmem_for(*blocks)),
        cost_estimate=pl.CostEstimate(flops=1, bytes_accessed=1 << 14, transcendentals=0),
    )(plan, *inputs)


def per_device(
    hidden_rows, grad_rows, block_slot, live_rows, replica_plan, master, moment_one, moment_two
):
    owner_count = lax.axis_size("expert") // QUART
    groups = lax.axis_size("dp")
    hidden_units, tok_rows = hidden_rows.shape
    block_width = grad_rows.shape[1] // QUART
    share_rows = hidden_units // groups
    assert block_slot.shape[1] == 1 and tok_rows == LANES and block_width % LANES == 0
    shape = jax.ShapeDtypeStruct
    lead = share_rows * 13 // 24 // 16 * 16
    spans = ((0, lead), (lead, share_rows - lead))

    head_rows = (block_width // LANES) * tok_rows + META_ROWS
    outs = [shape((head_rows + groups * lead, LANES), jnp.bfloat16)] * QUART
    outs += [shape((groups * (share_rows - lead), LANES), jnp.bfloat16)]
    messages = call(
        functools.partial(message_kernel, owner_count, spans),
        outs,
        (block_slot, live_rows),
        (hidden_rows, grad_rows),
    )

    def across(block, step):
        return from_behind(block, "expert", step * owner_count) if step else block

    first_bit = owner_count // 2
    other_bits = [1 << i for i in reversed(range(first_bit.bit_length() - 1))]
    own = [([(0, 0)], messages[0])]
    sides = [([(step, 0)], across(messages[step], step)) for step in (1, 3)]
    keys, block = exchange(own, first_bit)
    own += [(keys, after(block, *(side for _, side in sides))), *sides]
    last = [([(2, 0)], across(after(messages[2], own[1][1]), 2))]
    crossed = [exchange(sides, first_bit)]
    last_crossed = exchange(last, first_bit)
    for bit in other_bits:
        own += [exchange(own, bit)]
        last += [exchange(last, bit)]
    later = after(messages[QUART], last[-1][1], crossed[0][1])
    rest = [([(0, 0)], messages[QUART])]
    rest += [([(step, 0)], across(later, step)) for step in (1, 2, 3)]
    keys, block = last_crossed
    crossed += [(keys, after(block, *(part for _, part in rest[1:])))]
    for bit in other_bits:
        crossed += [exchange(crossed, bit)]
    last += crossed
    heads = own + last
    head_at = places(heads, 0)
    rests, rest_at = [], {}

    def partials(at, steps, wait_for):
        rows = spans[at][1]
        packs = heads + rests if at else heads
        where = [(key, found, rest_at[key] if at else found) for key, found in head_at.items()]
        return call(
            functools.partial(
                partial_kernel, owner_count, tok_rows, where, 0 if at else head_rows, steps
            ),
            [shape((rows, block_width), jnp.float32)] * len(steps),
            (after(replica_plan, *wait_for),),
            [block for _, block in packs],
            2 * len(steps) * rows * tok_rows * block_width * QUART,
        )

    states = (master[0], moment_one[0], moment_two[0])
    ahead = tuple(range(1, groups))
    block = lambda rows: shape((rows, block_width), jnp.bfloat16)

    far_one = partials(0, ahead, ())
    came_one = [from_behind(p, "dp", step) for step, p in zip(ahead, far_one)]
    near_one = partials(0, (0,), far_one)

    keys, parts = zip(*rest)
    stack = jnp.concatenate(parts)
    rest = [(sum(keys, []), stack)]
    rest += [exchange(rest, first_bit)]
    for pack in rest:
        group = [pack]
        for bit in other_bits:
            group += [exchange(group, bit)]
        rests += group
    rest_at.update(places(rests, len(heads)))

    far_two = partials(1, ahead, near_one)
    came_one = [after(term, *far_two) for term in came_one]
    *made, fresh_one = update((*near_one, *came_one), states, spans[0])
    came_two = [
        from_behind(after(p, fresh_one), "dp", step) for step, p in zip(ahead, far_two)
    ]
    near_two = partials(1, (0,), (fresh_one,))

    lines = [across(fresh_one, step) for step in range(QUART)]

    came_two = [after(term, fresh_one) for term in came_two]
    *held, fresh_two = update((*near_two, *came_two), states, spans[1], made)

    mates_two = gather_mates(fresh_two, "expert", owner_count)
    lines[1:] = [after(line, mates_two[owner_count // 2]) for line in lines[1:]]
    chosen = call(
        functools.partial(choose_kernel, owner_count),
        [block(spans[1][1])] * QUART,
        (after(replica_plan, *lines),),
        mates_two,
    )
    received = [across(c, step) for step, c in enumerate(chosen)]

    wide = gather_mates(jnp.concatenate(lines), "expert", owner_count, 2)[::2]
    (offer,) = call(
        functools.partial(offer_kernel, owner_count),
        [shape((spans[0][1], QUART * block_width), jnp.bfloat16)],
        (replica_plan,),
        wide,
    )
    result = shape((share_rows, QUART * block_width), jnp.bfloat16)
    placed = assemble(
        owner_count, spans[0], replica_plan, [*wide, *received], result
    )
    offer = from_mate(after(offer, *received[1:]), "expert", 1)
    replica_weight = assemble(owner_count, spans[0], replica_plan, [offer], result, placed)
    return (*(state[None] for state in held), replica_weight[None])


def solution(mesh):
    return jax.shard_map(
        per_device,
        mesh=mesh,
        in_specs=(
            P(None, ("dp", "expert")),
            P(("dp", "expert"), None),
            P(("dp", "expert"), None),
            P(("dp", "expert")),
            P(),
            P("expert", "dp", None),
            P("expert", "dp", None),
            P("expert", "dp", None),
        ),
        out_specs=(
            P("expert", "dp", None),
            P("expert", "dp", None),
            P("expert", "dp", None),
            P("expert", "dp", None),
        ),
        check_vma=False,
    )
```

```python
import functools

import jax
import jax.numpy as jnp
from jax import lax
from jax.experimental import pallas as pl
from jax.experimental.pallas import tpu as pltpu
from jax.sharding import PartitionSpec as P

QUART = 4
LANES = 128
META_ROWS = 16


beta_one = 0.9
beta_two = 0.95
learn_rate = 0.01
decay_rate = 0.1
epsilon = 1e-08
step_count = 10.0

VMEM = pl.BlockSpec(memory_space=pltpu.VMEM)
SMEM = pl.BlockSpec(memory_space=pltpu.SMEM)
ANYWHERE = pl.BlockSpec(memory_space=pl.ANY)


def vmem_for(*arrays):
    return int(sum(a.size * a.dtype.itemsize for a in arrays) * 5 // 4) + (8 << 20)


def call(kernel, out_shapes, scalars, arrays, flops=0):
    moved = sum(a.size * a.dtype.itemsize for a in (*arrays, *out_shapes))
    return pl.pallas_call(
        kernel,
        out_shape=tuple(out_shapes),
        in_specs=[SMEM] * len(scalars) + [VMEM] * len(arrays),
        out_specs=tuple([VMEM] * len(out_shapes)),
        compiler_params=pltpu.CompilerParams(vmem_limit_bytes=vmem_for(*arrays, *out_shapes)),
        cost_estimate=pl.CostEstimate(flops=flops // 64, bytes_accessed=moved // 64, transcendentals=0),
    )(*scalars, *arrays)


def from_behind(block, axis, distance):
    devices = range(lax.axis_size(axis))
    route = [((i - distance) % len(devices), i) for i in devices]
    return lax.ppermute(block, axis, route)


def from_mate(block, axis, bit):
    return lax.ppermute(block, axis, [(i ^ bit, i) for i in range(lax.axis_size(axis))])


def gather_mates(block, axis, count, least=1):
    held = {0: block}
    bit = count // 2
    while bit >= least:
        held.update({m | bit: from_mate(held[m], axis, bit) for m in list(held)})
        bit //= 2
    return [held.get(m) for m in range(count)]


def after(value, *others):
    return lax.optimization_barrier((value, *others))[0] if others else value


def exchange(packs, bit):
    keys = [(step, mate | bit) for pack, _ in packs for step, mate in pack]
    blocks = [block for _, block in packs]
    return keys, from_mate(jnp.concatenate(blocks) if len(blocks) > 1 else blocks[0], "expert", bit)


def places(packs, first):
    found = {}
    for at, (keys, block) in enumerate(packs):
        rows = block.shape[0] // len(keys)
        found.update({key: (first + at, i * rows) for i, key in enumerate(keys)})
    return found


def place(owner_count):
    own = lax.axis_index("expert")
    return own // owner_count, own % owner_count


def message_kernel(owner_count, spans, slot_ref, live_ref, hidden_ref, grad_ref, *message_refs):
    own_block, _ = place(owner_count)
    groups = lax.axis_size("dp")
    hidden_units, tok_rows = hidden_ref.shape
    share_rows = hidden_units // groups
    block_width = grad_ref.shape[1] // QUART
    parts = block_width // LANES
    live = live_ref[0]
    slot = slot_ref[0, 0]
    kept = lax.broadcasted_iota(jnp.int32, (tok_rows, LANES), 0) < live
    meta = jnp.full((META_ROWS, LANES), slot.astype(jnp.float32)).astype(jnp.bfloat16)

    def put_hidden(message, row, span):
        first, length = span
        for group in range(groups):
            start = group * share_rows + first
            message[row : row + length, :] = hidden_ref[start : start + length, :]
            row += length

    for step, message in enumerate(message_refs[:QUART]):
        target = lax.rem(own_block + step, QUART)
        for part in range(parts):
            start = pl.multiple_of(target * block_width + part * LANES, LANES)
            columns = grad_ref[:, pl.ds(start, LANES)].astype(jnp.float32)
            row = part * tok_rows
            message[row : row + tok_rows, :] = jnp.where(kept, columns, 0.0).astype(jnp.bfloat16)
        row = parts * tok_rows
        message[row : row + META_ROWS, :] = meta
        put_hidden(message, row + META_ROWS, spans[0])
    for message, span in zip(message_refs[QUART:], spans[1:]):
        put_hidden(message, 0, span)


def partial_kernel(owner_count, tok_rows, where, base, steps, plan_ref, *refs):
    totals = refs[-len(steps) :]
    own_block, own_expert = place(owner_count)
    group, groups = lax.axis_index("dp"), lax.axis_size("dp")
    rows, block_width = totals[0].shape
    parts = block_width // LANES
    chunk = next(c for c in (208, 192, 176, 128, 112, 96, 64, 48, 32, 16) if rows % c == 0)
    bits = []
    for first in range(0, len(where), 16):
        packed = jnp.zeros((META_ROWS, LANES), jnp.float32)
        for at, (_, (head, row), _) in enumerate(where[first : first + 16]):
            meta = refs[head][row + parts * tok_rows : row + parts * tok_rows + META_ROWS, :]
            packed = packed + meta.astype(jnp.float32) * float(1 << at)
        bits.append(jnp.max(packed).astype(jnp.int32))
    for total in totals:
        total[...] = jnp.zeros_like(total)
    for at, ((step, mate), (head, head_row), (tail, tail_row)) in enumerate(where):
        source_expert = own_expert ^ mate
        source = lax.rem(own_block + QUART - step, QUART) * owner_count + source_expert
        is_replica = ((bits[at // 16] >> (at % 16)) & 1) == 1
        target = jnp.where(is_replica, plan_ref[source], source_expert)

        columns = jnp.concatenate(
            [
                refs[head][head_row + p * tok_rows : head_row + (p + 1) * tok_rows, :]
                for p in range(parts)
            ],
            axis=1,
        )

        def add(rounded):
            for total, ahead in zip(totals, steps):
                start = tail_row + base + lax.rem(group + ahead, groups) * rows

                @pl.loop(0, rows // chunk)
                def _(i):
                    term = jnp.dot(
                        refs[tail][pl.ds(pl.multiple_of(start + i * chunk, 16), chunk), :],
                        columns,
                        preferred_element_type=jnp.float32,
                    )
                    if rounded:
                        term = term.astype(jnp.bfloat16).astype(jnp.float32)
                    into = pl.ds(pl.multiple_of(i * chunk, 16), chunk)
                    total[into, :] += term

        if mate == 0:
            pl.when((target == own_expert) & jnp.logical_not(is_replica))(lambda: add(False))
        pl.when((target == own_expert) & is_replica)(lambda: add(True))


def new_rows(terms, states, first, start, size):
    inside, placed = pl.ds(start, size), pl.ds(first + start, size)
    master, one, two = states
    gradient = terms[0][inside, :]
    for term in terms[1:]:
        gradient = gradient + term[inside, :]
    weights = master[placed, :]
    first_next = beta_one * one[placed, :] + (1.0 - beta_one) * gradient
    second_next = beta_two * two[placed, :] + (1.0 - beta_two) * gradient * gradient
    scaled_first = first_next / (1.0 - beta_one**step_count)
    scaled_second = second_next / (1.0 - beta_two**step_count)
    direction = scaled_first / (jnp.sqrt(scaled_second) + epsilon)
    weights_next = weights - learn_rate * (direction + decay_rate * weights)
    return weights_next, first_next, second_next


def update_kernel(parts, first, pieces, *refs):
    terms, states, outs = refs[:parts], refs[parts : parts + 3], refs[parts + 3 :]
    for start, size in pieces:
        values = new_rows(terms, states, first, start, size)
        for out, value in zip(outs, (*values, values[0].astype(jnp.bfloat16))):
            out[pl.ds(start, size), :] = value


def finish_kernel(parts, first, pieces, *refs):
    terms, states, made = refs[:parts], refs[parts : parts + 3], refs[parts + 3 : parts + 6]
    *outs, fresh, fresh_states, sems = refs[parts + 6 :]
    copies = [
        pltpu.make_async_copy(rows, out.at[pl.ds(0, first), :], sems.at[which, 0])
        for which, (rows, out) in enumerate(zip(made, outs))
    ]
    for copy in copies:
        copy.start()
    for at, (start, size) in enumerate(pieces):
        inside, placed = pl.ds(start, size), pl.ds(first + start, size)
        values = new_rows(terms, states, first, start, size)
        fresh[inside, :] = values[0].astype(jnp.bfloat16)
        for which, value in enumerate(values):
            fresh_states[which, inside, :] = value
            copies.append(
                pltpu.make_async_copy(
                    fresh_states.at[which, inside, :],
                    outs[which].at[placed, :],
                    sems.at[which, at + 1],
                )
            )
            copies[-1].start()
    for copy in copies:
        copy.wait()


def update(terms, states, span, made=()):
    first, length = span
    rows, width = states[0].shape
    pieces = [(start, min(64, length - start)) for start in range(0, length, 64)]
    part = jax.ShapeDtypeStruct((length, width), jnp.float32)
    whole = jax.ShapeDtypeStruct((rows, width), jnp.float32)
    scratch = [
        pltpu.VMEM((3, length, width), jnp.float32),
        pltpu.SemaphoreType.DMA((3, len(pieces) + 1)),
    ]
    return pl.pallas_call(
        functools.partial(finish_kernel if made else update_kernel, len(terms), first, pieces),
        out_shape=(
            *([whole if made else part] * 3),
            jax.ShapeDtypeStruct((length, width), jnp.bfloat16),
        ),
        in_specs=[VMEM] * (len(terms) + len(states) + len(made)),
        out_specs=(*([ANYWHERE if made else VMEM] * 3), VMEM),
        scratch_shapes=scratch if made else [],
        compiler_params=pltpu.CompilerParams(vmem_limit_bytes=24 << 20),
        cost_estimate=pl.CostEstimate(
            flops=length * width, bytes_accessed=length * width, transcendentals=0
        ),
    )(*terms, *states, *made)


def choose_kernel(owner_count, where, plan_ref, *refs):
    candidates, chosen = refs[: len(where)], refs[len(where) :]
    own_block, own_expert = place(owner_count)
    for step, out in enumerate(chosen):
        wanted = plan_ref[lax.rem(own_block + step, QUART) * owner_count + own_expert]
        for (mate, rows), candidate in zip(where, candidates):

            @pl.when(wanted == own_expert ^ mate)
            def _():
                out[rows, :] = candidate[...]


def offer_kernel(owner_count, plan_ref, *refs):
    held, out = refs[:-1], refs[-1]
    own_block, own_expert = place(owner_count)
    wanted = plan_ref[own_block * owner_count + (own_expert ^ 1)]
    rows = out.shape[0]
    for pair, blocks in enumerate(held):

        @pl.when((wanted ^ own_expert) >> 1 == pair)
        def _():
            for step in range(QUART):
                width = blocks.shape[1]
                column = pl.multiple_of(lax.rem(own_block + QUART - step, QUART) * width, LANES)
                out[:, pl.ds(column, width)] = blocks[step * rows : (step + 1) * rows, :]


def assemble_kernel(owner_count, span, later, plan_ref, *refs):
    *blocks, out, sems = refs
    own_block, own_expert = place(owner_count)
    apart = plan_ref[own_block * owner_count + own_expert] ^ own_expert
    first, rows = span
    half = owner_count // 2

    def put(sources, start, group):
        copies = []
        for step, source in enumerate(sources):
            width = source.shape[1]
            column = pl.multiple_of(lax.rem(own_block + QUART - step, QUART) * width, LANES)
            target = out.at[pl.ds(start, source.shape[0]), pl.ds(column, width)]
            copies.append(pltpu.make_async_copy(source, target, sems.at[group, step]))
            copies[-1].start()
        return copies

    def finish(copies):
        for copy in copies:
            copy.wait()

    if later:
        offered, _ = blocks

        @pl.when(apart & 1 == 1)
        def _():
            copy = pltpu.make_async_copy(offered, out.at[pl.ds(first, rows), :], sems.at[0, 0])
            copy.start()
            copy.wait()

        return

    held, received = blocks[:half], blocks[half:]
    others = put(received, first + rows, 0)
    for pair in range(half):

        @pl.when(apart == 2 * pair)
        def _():
            lines = [held[pair].at[pl.ds(step * rows, rows), :] for step in range(QUART)]
            finish(put(lines, first, 1))

    finish(others)


def assemble(owner_count, span, plan, blocks, shape, held=None):
    later = held is not None
    inputs = [*blocks, held] if later else blocks
    return pl.pallas_call(
        functools.partial(assemble_kernel, owner_count, span, later),
        out_shape=shape,
        in_specs=[SMEM] + [VMEM] * len(blocks) + [ANYWHERE] * later,
        out_specs=ANYWHERE,
        scratch_shapes=[pltpu.SemaphoreType.DMA((2, QUART))],
        input_output_aliases={1 + len(blocks): 0} if later else {},
        compiler_params=pltpu.CompilerParams(vmem_limit_bytes=vmem_for(*blocks)),
        cost_estimate=pl.CostEstimate(flops=1, bytes_accessed=1 << 14, transcendentals=0),
    )(plan, *inputs)


def per_device(
    hidden_rows, grad_rows, block_slot, live_rows, replica_plan, master, moment_one, moment_two
):
    owner_count = lax.axis_size("expert") // QUART
    groups = lax.axis_size("dp")
    hidden_units, tok_rows = hidden_rows.shape
    block_width = grad_rows.shape[1] // QUART
    share_rows = hidden_units // groups
    assert block_slot.shape[1] == 1 and tok_rows == LANES and block_width % LANES == 0
    shape = jax.ShapeDtypeStruct
    lead = share_rows * 11 // 24 // 16 * 16
    spans = ((0, lead), (lead, share_rows - lead))

    head_rows = (block_width // LANES) * tok_rows + META_ROWS
    outs = [shape((head_rows + groups * lead, LANES), jnp.bfloat16)] * QUART
    outs += [shape((groups * (share_rows - lead), LANES), jnp.bfloat16)]
    messages = call(
        functools.partial(message_kernel, owner_count, spans),
        outs,
        (block_slot, live_rows),
        (hidden_rows, grad_rows),
    )

    def across(block, step):
        return from_behind(block, "expert", step * owner_count) if step else block

    first_bit = owner_count // 2
    other_bits = [1 << i for i in reversed(range(first_bit.bit_length() - 1))]
    own = [([(0, 0)], messages[0])]
    sides = [([(step, 0)], across(messages[step], step)) for step in (1, 3)]
    keys, block = exchange(own, first_bit)
    own += [(keys, after(block, *(side for _, side in sides))), *sides]
    last = [([(2, 0)], across(after(messages[2], own[1][1]), 2))]
    crossed = [exchange(sides, first_bit)]
    last_crossed = exchange(last, first_bit)
    for bit in other_bits:
        own += [exchange(own, bit)]
        last += [exchange(last, bit)]
    later = after(messages[QUART], last[-1][1], crossed[0][1])
    rest = [([(0, 0)], messages[QUART])]
    rest += [([(step, 0)], across(later, step)) for step in (1, 2, 3)]
    keys, block = last_crossed
    crossed += [(keys, after(block, *(part for _, part in rest[1:])))]
    for bit in other_bits:
        crossed += [exchange(crossed, bit)]
    last += crossed
    heads = own + last
    head_at = places(heads, 0)
    rests, rest_at = [], {}

    def partials(at, steps, wait_for):
        rows = spans[at][1]
        packs = heads + rests if at else heads
        where = [(key, found, rest_at[key] if at else found) for key, found in head_at.items()]
        return call(
            functools.partial(
                partial_kernel, owner_count, tok_rows, where, 0 if at else head_rows, steps
            ),
            [shape((rows, block_width), jnp.float32)] * len(steps),
            (after(replica_plan, *wait_for),),
            [block for _, block in packs],
            2 * len(steps) * rows * tok_rows * block_width * QUART,
        )

    states = (master[0], moment_one[0], moment_two[0])
    ahead = tuple(range(1, groups))
    block = lambda rows: shape((rows, block_width), jnp.bfloat16)

    far_one = partials(0, ahead, ())
    came_one = [from_behind(p, "dp", step) for step, p in zip(ahead, far_one)]
    near_one = partials(0, (0,), far_one)

    keys, parts = zip(*rest)
    stack = jnp.concatenate(parts)
    rest = [(sum(keys, []), stack)]
    rest += [exchange(rest, first_bit)]
    for pack in rest:
        group = [pack]
        for bit in other_bits:
            group += [exchange(group, bit)]
        rests += group
    rest_at.update(places(rests, len(heads)))

    far_two = partials(1, ahead, near_one)
    came_one = [after(term, *far_two) for term in came_one]
    *made, fresh_one = update((*near_one, *came_one), states, spans[0])
    came_two = [
        from_behind(after(p, fresh_one), "dp", step) for step, p in zip(ahead, far_two)
    ]
    near_two = partials(1, (0,), (fresh_one,))

    lines = [across(fresh_one, step) for step in range(QUART)]

    came_two = [after(term, fresh_one) for term in came_two]
    *held, fresh_two = update((*near_two, *came_two), states, spans[1], made)

    rows_two = spans[1][1]
    cut = rows_two // 32 * 16
    halves = [(slice(0, cut), fresh_two[:cut]), (slice(cut, rows_two), fresh_two[cut:])]
    mates_two = {0: [(slice(0, rows_two), fresh_two)]}
    for bit in (first_bit, *other_bits):
        mates_two.update(
            {
                m | bit: [
                    (rows, from_mate(piece, "expert", bit))
                    for rows, piece in (halves if bit == first_bit else pieces)
                ]
                for m, pieces in list(mates_two.items())
            }
        )
    crossed_two = [piece for _, piece in mates_two[first_bit]]
    where = [(m, rows) for m, pieces in mates_two.items() for rows, _ in pieces]
    lines[1:] = [after(line, *crossed_two) for line in lines[1:]]
    chosen = call(
        functools.partial(choose_kernel, owner_count, where),
        [block(rows_two)] * QUART,
        (after(replica_plan, *lines),),
        [piece for pieces in mates_two.values() for _, piece in pieces],
    )
    received = [across(c, step) for step, c in enumerate(chosen)]

    wide = gather_mates(jnp.concatenate(lines), "expert", owner_count, 2)[::2]
    (offer,) = call(
        functools.partial(offer_kernel, owner_count),
        [shape((spans[0][1], QUART * block_width), jnp.bfloat16)],
        (replica_plan,),
        wide,
    )
    result = shape((share_rows, QUART * block_width), jnp.bfloat16)
    placed = assemble(
        owner_count, spans[0], replica_plan, [*wide, *received], result
    )
    offer = from_mate(after(offer, *received[1:]), "expert", 1)
    replica_weight = assemble(owner_count, spans[0], replica_plan, [offer], result, placed)
    return (*(state[None] for state in held), replica_weight[None])


def solution(mesh):
    return jax.shard_map(
        per_device,
        mesh=mesh,
        in_specs=(
            P(None, ("dp", "expert")),
            P(("dp", "expert"), None),
            P(("dp", "expert"), None),
            P(("dp", "expert")),
            P(),
            P("expert", "dp", None),
            P("expert", "dp", None),
            P("expert", "dp", None),
        ),
        out_specs=(
            P("expert", "dp", None),
            P("expert", "dp", None),
            P("expert", "dp", None),
            P("expert", "dp", None),
        ),
        check_vma=False,
    )
```

```python
import functools

import jax
import jax.numpy as jnp
from jax import lax
from jax.experimental import pallas as pl
from jax.experimental.pallas import tpu as pltpu
from jax.sharding import PartitionSpec as P

QUART = 4
LANES = 128
META_ROWS = 16


beta_one = 0.9
beta_two = 0.95
learn_rate = 0.01
decay_rate = 0.1
epsilon = 1e-08
step_count = 10.0

VMEM = pl.BlockSpec(memory_space=pltpu.VMEM)
SMEM = pl.BlockSpec(memory_space=pltpu.SMEM)
ANYWHERE = pl.BlockSpec(memory_space=pl.ANY)


def vmem_for(*arrays):
    return int(sum(a.size * a.dtype.itemsize for a in arrays) * 5 // 4) + (8 << 20)


def call(kernel, out_shapes, scalars, arrays, flops=0):
    moved = sum(a.size * a.dtype.itemsize for a in (*arrays, *out_shapes))
    return pl.pallas_call(
        kernel,
        out_shape=tuple(out_shapes),
        in_specs=[SMEM] * len(scalars) + [VMEM] * len(arrays),
        out_specs=tuple([VMEM] * len(out_shapes)),
        compiler_params=pltpu.CompilerParams(vmem_limit_bytes=vmem_for(*arrays, *out_shapes)),
        cost_estimate=pl.CostEstimate(flops=flops // 64, bytes_accessed=moved // 64, transcendentals=0),
    )(*scalars, *arrays)


def from_behind(block, axis, distance):
    devices = range(lax.axis_size(axis))
    route = [((i - distance) % len(devices), i) for i in devices]
    return lax.ppermute(block, axis, route)


def from_mate(block, axis, bit):
    return lax.ppermute(block, axis, [(i ^ bit, i) for i in range(lax.axis_size(axis))])


def gather_mates(block, axis, count, least=1):
    held = {0: block}
    bit = count // 2
    while bit >= least:
        held.update({m | bit: from_mate(held[m], axis, bit) for m in list(held)})
        bit //= 2
    return [held.get(m) for m in range(count)]


def after(value, *others):
    return lax.optimization_barrier((value, *others))[0] if others else value


def exchange(packs, bit):
    keys = [(step, mate | bit) for pack, _ in packs for step, mate in pack]
    blocks = [block for _, block in packs]
    return keys, from_mate(jnp.concatenate(blocks) if len(blocks) > 1 else blocks[0], "expert", bit)


def places(packs, first):
    found = {}
    for at, (keys, block) in enumerate(packs):
        rows = block.shape[0] // len(keys)
        found.update({key: (first + at, i * rows) for i, key in enumerate(keys)})
    return found


def place(owner_count):
    own = lax.axis_index("expert")
    return own // owner_count, own % owner_count


def message_kernel(owner_count, spans, slot_ref, live_ref, hidden_ref, grad_ref, *message_refs):
    own_block, _ = place(owner_count)
    groups = lax.axis_size("dp")
    hidden_units, tok_rows = hidden_ref.shape
    share_rows = hidden_units // groups
    block_width = grad_ref.shape[1] // QUART
    parts = block_width // LANES
    live = live_ref[0]
    slot = slot_ref[0, 0]
    kept = lax.broadcasted_iota(jnp.int32, (tok_rows, LANES), 0) < live
    meta = jnp.full((META_ROWS, LANES), slot.astype(jnp.float32)).astype(jnp.bfloat16)

    def put_hidden(message, row, span):
        first, length = span
        for group in range(groups):
            start = group * share_rows + first
            message[row : row + length, :] = hidden_ref[start : start + length, :]
            row += length

    for step, message in enumerate(message_refs[:QUART]):
        target = lax.rem(own_block + step, QUART)
        for part in range(parts):
            start = pl.multiple_of(target * block_width + part * LANES, LANES)
            columns = grad_ref[:, pl.ds(start, LANES)].astype(jnp.float32)
            row = part * tok_rows
            message[row : row + tok_rows, :] = jnp.where(kept, columns, 0.0).astype(jnp.bfloat16)
        row = parts * tok_rows
        message[row : row + META_ROWS, :] = meta
        put_hidden(message, row + META_ROWS, spans[0])
    for message, span in zip(message_refs[QUART:], spans[1:]):
        put_hidden(message, 0, span)


def partial_kernel(owner_count, tok_rows, where, base, steps, plan_ref, *refs):
    totals = refs[-len(steps) :]
    own_block, own_expert = place(owner_count)
    group, groups = lax.axis_index("dp"), lax.axis_size("dp")
    rows, block_width = totals[0].shape
    parts = block_width // LANES
    chunk = next(c for c in (208, 192, 176, 128, 112, 96, 64, 48, 32, 16) if rows % c == 0)
    bits = []
    for first in range(0, len(where), 16):
        packed = jnp.zeros((META_ROWS, LANES), jnp.float32)
        for at, (_, (head, row), _) in enumerate(where[first : first + 16]):
            meta = refs[head][row + parts * tok_rows : row + parts * tok_rows + META_ROWS, :]
            packed = packed + meta.astype(jnp.float32) * float(1 << at)
        bits.append(jnp.max(packed).astype(jnp.int32))
    for total in totals:
        total[...] = jnp.zeros_like(total)
    for at, ((step, mate), (head, head_row), (tail, tail_row)) in enumerate(where):
        source_expert = own_expert ^ mate
        source = lax.rem(own_block + QUART - step, QUART) * owner_count + source_expert
        is_replica = ((bits[at // 16] >> (at % 16)) & 1) == 1
        target = jnp.where(is_replica, plan_ref[source], source_expert)

        columns = jnp.concatenate(
            [
                refs[head][head_row + p * tok_rows : head_row + (p + 1) * tok_rows, :]
                for p in range(parts)
            ],
            axis=1,
        )

        def add(rounded):
            for total, ahead in zip(totals, steps):
                start = tail_row + base + lax.rem(group + ahead, groups) * rows

                @pl.loop(0, rows // chunk)
                def _(i):
                    term = jnp.dot(
                        refs[tail][pl.ds(pl.multiple_of(start + i * chunk, 16), chunk), :],
                        columns,
                        preferred_element_type=jnp.float32,
                    )
                    if rounded:
                        term = term.astype(jnp.bfloat16).astype(jnp.float32)
                    into = pl.ds(pl.multiple_of(i * chunk, 16), chunk)
                    total[into, :] += term

        if mate == 0:
            pl.when((target == own_expert) & jnp.logical_not(is_replica))(lambda: add(False))
        pl.when((target == own_expert) & is_replica)(lambda: add(True))


def new_rows(terms, states, first, start, size):
    inside, placed = pl.ds(start, size), pl.ds(first + start, size)
    master, one, two = states
    gradient = terms[0][inside, :]
    for term in terms[1:]:
        gradient = gradient + term[inside, :]
    weights = master[placed, :]
    first_next = beta_one * one[placed, :] + (1.0 - beta_one) * gradient
    second_next = beta_two * two[placed, :] + (1.0 - beta_two) * gradient * gradient
    scaled_first = first_next / (1.0 - beta_one**step_count)
    scaled_second = second_next / (1.0 - beta_two**step_count)
    direction = scaled_first / (jnp.sqrt(scaled_second) + epsilon)
    weights_next = weights - learn_rate * (direction + decay_rate * weights)
    return weights_next, first_next, second_next


def update_kernel(parts, first, pieces, *refs):
    terms, states, outs = refs[:parts], refs[parts : parts + 3], refs[parts + 3 :]
    for start, size in pieces:
        values = new_rows(terms, states, first, start, size)
        for out, value in zip(outs, (*values, values[0].astype(jnp.bfloat16))):
            out[pl.ds(start, size), :] = value


def finish_kernel(parts, first, pieces, *refs):
    terms, states, made = refs[:parts], refs[parts : parts + 3], refs[parts + 3 : parts + 6]
    *outs, fresh, fresh_states, sems = refs[parts + 6 :]
    copies = [
        pltpu.make_async_copy(rows, out.at[pl.ds(0, first), :], sems.at[which, 0])
        for which, (rows, out) in enumerate(zip(made, outs))
    ]
    for copy in copies:
        copy.start()
    for at, (start, size) in enumerate(pieces):
        inside, placed = pl.ds(start, size), pl.ds(first + start, size)
        values = new_rows(terms, states, first, start, size)
        fresh[inside, :] = values[0].astype(jnp.bfloat16)
        for which, value in enumerate(values):
            fresh_states[which, inside, :] = value
            copies.append(
                pltpu.make_async_copy(
                    fresh_states.at[which, inside, :],
                    outs[which].at[placed, :],
                    sems.at[which, at + 1],
                )
            )
            copies[-1].start()
    for copy in copies:
        copy.wait()


def update(terms, states, span, made=()):
    first, length = span
    rows, width = states[0].shape
    pieces = [(start, min(64, length - start)) for start in range(0, length, 64)]
    part = jax.ShapeDtypeStruct((length, width), jnp.float32)
    whole = jax.ShapeDtypeStruct((rows, width), jnp.float32)
    scratch = [
        pltpu.VMEM((3, length, width), jnp.float32),
        pltpu.SemaphoreType.DMA((3, len(pieces) + 1)),
    ]
    return pl.pallas_call(
        functools.partial(finish_kernel if made else update_kernel, len(terms), first, pieces),
        out_shape=(
            *([whole if made else part] * 3),
            jax.ShapeDtypeStruct((length, width), jnp.bfloat16),
        ),
        in_specs=[VMEM] * (len(terms) + len(states) + len(made)),
        out_specs=(*([ANYWHERE if made else VMEM] * 3), VMEM),
        scratch_shapes=scratch if made else [],
        compiler_params=pltpu.CompilerParams(vmem_limit_bytes=24 << 20),
        cost_estimate=pl.CostEstimate(
            flops=length * width, bytes_accessed=length * width, transcendentals=0
        ),
    )(*terms, *states, *made)


def choose_kernel(owner_count, where, plan_ref, *refs):
    candidates, chosen = refs[: len(where)], refs[len(where) :]
    own_block, own_expert = place(owner_count)
    for step, out in enumerate(chosen):
        wanted = plan_ref[lax.rem(own_block + step, QUART) * owner_count + own_expert]
        for (mate, rows), candidate in zip(where, candidates):

            @pl.when(wanted == own_expert ^ mate)
            def _():
                out[rows, :] = candidate[...]


def offer_kernel(owner_count, plan_ref, *refs):
    held, out = refs[:-1], refs[-1]
    own_block, own_expert = place(owner_count)
    wanted = plan_ref[own_block * owner_count + (own_expert ^ 1)]
    rows = out.shape[0]
    for pair, blocks in enumerate(held):

        @pl.when((wanted ^ own_expert) >> 1 == pair)
        def _():
            for step in range(QUART):
                width = blocks.shape[1]
                column = pl.multiple_of(lax.rem(own_block + QUART - step, QUART) * width, LANES)
                out[:, pl.ds(column, width)] = blocks[step * rows : (step + 1) * rows, :]


def assemble_kernel(owner_count, span, later, plan_ref, *refs):
    *blocks, out, sems = refs
    own_block, own_expert = place(owner_count)
    apart = plan_ref[own_block * owner_count + own_expert] ^ own_expert
    first, rows = span
    half = owner_count // 2

    def put(sources, start, group):
        copies = []
        for step, source in enumerate(sources):
            width = source.shape[1]
            column = pl.multiple_of(lax.rem(own_block + QUART - step, QUART) * width, LANES)
            target = out.at[pl.ds(start, source.shape[0]), pl.ds(column, width)]
            copies.append(pltpu.make_async_copy(source, target, sems.at[group, step]))
            copies[-1].start()
        return copies

    def finish(copies):
        for copy in copies:
            copy.wait()

    if later:
        offered, _ = blocks

        @pl.when(apart & 1 == 1)
        def _():
            copy = pltpu.make_async_copy(offered, out.at[pl.ds(first, rows), :], sems.at[0, 0])
            copy.start()
            copy.wait()

        return

    held, received = blocks[:half], blocks[half:]
    others = put(received, first + rows, 0)
    for pair in range(half):

        @pl.when(apart == 2 * pair)
        def _():
            lines = [held[pair].at[pl.ds(step * rows, rows), :] for step in range(QUART)]
            finish(put(lines, first, 1))

    finish(others)


def assemble(owner_count, span, plan, blocks, shape, held=None):
    later = held is not None
    inputs = [*blocks, held] if later else blocks
    return pl.pallas_call(
        functools.partial(assemble_kernel, owner_count, span, later),
        out_shape=shape,
        in_specs=[SMEM] + [VMEM] * len(blocks) + [ANYWHERE] * later,
        out_specs=ANYWHERE,
        scratch_shapes=[pltpu.SemaphoreType.DMA((2, QUART))],
        input_output_aliases={1 + len(blocks): 0} if later else {},
        compiler_params=pltpu.CompilerParams(vmem_limit_bytes=vmem_for(*blocks)),
        cost_estimate=pl.CostEstimate(flops=1, bytes_accessed=1 << 14, transcendentals=0),
    )(plan, *inputs)


def per_device(
    hidden_rows, grad_rows, block_slot, live_rows, replica_plan, master, moment_one, moment_two
):
    owner_count = lax.axis_size("expert") // QUART
    groups = lax.axis_size("dp")
    hidden_units, tok_rows = hidden_rows.shape
    block_width = grad_rows.shape[1] // QUART
    share_rows = hidden_units // groups
    assert block_slot.shape[1] == 1 and tok_rows == LANES and block_width % LANES == 0
    shape = jax.ShapeDtypeStruct
    lead = share_rows * 11 // 24 // 16 * 16
    spans = ((0, lead), (lead, share_rows - lead))

    head_rows = (block_width // LANES) * tok_rows + META_ROWS
    outs = [shape((head_rows + groups * lead, LANES), jnp.bfloat16)] * QUART
    outs += [shape((groups * (share_rows - lead), LANES), jnp.bfloat16)]
    messages = call(
        functools.partial(message_kernel, owner_count, spans),
        outs,
        (block_slot, live_rows),
        (hidden_rows, grad_rows),
    )

    def across(block, step):
        return from_behind(block, "expert", step * owner_count) if step else block

    first_bit = owner_count // 2
    other_bits = [1 << i for i in reversed(range(first_bit.bit_length() - 1))]
    own = [([(0, 0)], messages[0])]
    sides = [([(step, 0)], across(messages[step], step)) for step in (1, 3)]
    keys, block = exchange(own, first_bit)
    own += [(keys, after(block, *(side for _, side in sides))), *sides]
    rest = [([(0, 0)], messages[QUART])]
    rest_crossed = exchange(rest, first_bit)
    last = [([(2, 0)], across(after(messages[2], own[1][1], rest_crossed[1]), 2))]
    crossed = [exchange(sides, first_bit)]
    last_crossed = exchange(last, first_bit)
    for bit in other_bits:
        own += [exchange(own, bit)]
        last += [exchange(last, bit)]
    later = after(messages[QUART], last[-1][1], crossed[0][1])
    rest += [([(step, 0)], across(later, step)) for step in (1, 2, 3)]
    keys, block = last_crossed
    crossed += [(keys, after(block, *(part for _, part in rest[1:])))]
    for bit in other_bits:
        crossed += [exchange(crossed, bit)]
    last += crossed
    heads = own + last
    head_at = places(heads, 0)
    rests, rest_at = [], {}

    def partials(at, steps, wait_for):
        rows = spans[at][1]
        packs = heads + rests if at else heads
        where = [(key, found, rest_at[key] if at else found) for key, found in head_at.items()]
        return call(
            functools.partial(
                partial_kernel, owner_count, tok_rows, where, 0 if at else head_rows, steps
            ),
            [shape((rows, block_width), jnp.float32)] * len(steps),
            (after(replica_plan, *wait_for),),
            [block for _, block in packs],
            2 * len(steps) * rows * tok_rows * block_width * QUART,
        )

    states = (master[0], moment_one[0], moment_two[0])
    ahead = tuple(range(1, groups))
    block = lambda rows: shape((rows, block_width), jnp.bfloat16)

    far_one = partials(0, ahead, ())
    came_one = [from_behind(p, "dp", step) for step, p in zip(ahead, far_one)]
    near_one = partials(0, (0,), far_one)

    keys, parts = zip(*rest)
    crossed = [rest_crossed, exchange(rest[1:], first_bit)]
    for group in ([(sum(keys, []), jnp.concatenate(parts))], crossed):
        for bit in other_bits:
            group += [exchange(group, bit)]
        rests += group
    rest_at.update(places(rests, len(heads)))

    far_two = partials(1, ahead, near_one)
    came_one = [after(term, *far_two) for term in came_one]
    *made, fresh_one = update((*near_one, *came_one), states, spans[0])
    came_two = [
        from_behind(after(p, fresh_one), "dp", step) for step, p in zip(ahead, far_two)
    ]
    near_two = partials(1, (0,), (fresh_one,))

    lines = [across(fresh_one, step) for step in range(QUART)]

    came_two = [after(term, fresh_one) for term in came_two]
    *held, fresh_two = update((*near_two, *came_two), states, spans[1], made)

    rows_two = spans[1][1]
    cut = rows_two // 32 * 16
    halves = [(slice(0, cut), fresh_two[:cut]), (slice(cut, rows_two), fresh_two[cut:])]
    mates_two = {0: [(slice(0, rows_two), fresh_two)]}
    for bit in (first_bit, *other_bits):
        mates_two.update(
            {
                m | bit: [
                    (rows, from_mate(piece, "expert", bit))
                    for rows, piece in (halves if bit == first_bit else pieces)
                ]
                for m, pieces in list(mates_two.items())
            }
        )
    crossed_two = [piece for _, piece in mates_two[first_bit]]
    where = [(m, rows) for m, pieces in mates_two.items() for rows, _ in pieces]
    lines[1:] = [after(line, *crossed_two) for line in lines[1:]]
    chosen = call(
        functools.partial(choose_kernel, owner_count, where),
        [block(rows_two)] * QUART,
        (after(replica_plan, *lines),),
        [piece for pieces in mates_two.values() for _, piece in pieces],
    )
    received = [across(c, step) for step, c in enumerate(chosen)]

    wide = gather_mates(jnp.concatenate(lines), "expert", owner_count, 2)[::2]
    (offer,) = call(
        functools.partial(offer_kernel, owner_count),
        [shape((spans[0][1], QUART * block_width), jnp.bfloat16)],
        (replica_plan,),
        wide,
    )
    result = shape((share_rows, QUART * block_width), jnp.bfloat16)
    placed = assemble(
        owner_count, spans[0], replica_plan, [*wide, *received], result
    )
    offer = from_mate(after(offer, *received[1:]), "expert", 1)
    replica_weight = assemble(owner_count, spans[0], replica_plan, [offer], result, placed)
    return (*(state[None] for state in held), replica_weight[None])


def solution(mesh):
    return jax.shard_map(
        per_device,
        mesh=mesh,
        in_specs=(
            P(None, ("dp", "expert")),
            P(("dp", "expert"), None),
            P(("dp", "expert"), None),
            P(("dp", "expert")),
            P(),
            P("expert", "dp", None),
            P("expert", "dp", None),
            P("expert", "dp", None),
        ),
        out_specs=(
            P("expert", "dp", None),
            P("expert", "dp", None),
            P("expert", "dp", None),
            P("expert", "dp", None),
        ),
        check_vma=False,
    )
```

```python
import functools

import jax
import jax.numpy as jnp
from jax import lax
from jax.experimental import pallas as pl
from jax.experimental.pallas import tpu as pltpu
from jax.sharding import PartitionSpec as P

QUART = 4
LANES = 128
META_ROWS = 16


beta_one = 0.9
beta_two = 0.95
learn_rate = 0.01
decay_rate = 0.1
epsilon = 1e-08
step_count = 10.0

VMEM = pl.BlockSpec(memory_space=pltpu.VMEM)
SMEM = pl.BlockSpec(memory_space=pltpu.SMEM)
ANYWHERE = pl.BlockSpec(memory_space=pl.ANY)


def vmem_for(*arrays):
    return int(sum(a.size * a.dtype.itemsize for a in arrays) * 5 // 4) + (8 << 20)


def call(kernel, out_shapes, scalars, arrays, flops=0):
    moved = sum(a.size * a.dtype.itemsize for a in (*arrays, *out_shapes))
    return pl.pallas_call(
        kernel,
        out_shape=tuple(out_shapes),
        in_specs=[SMEM] * len(scalars) + [VMEM] * len(arrays),
        out_specs=tuple([VMEM] * len(out_shapes)),
        compiler_params=pltpu.CompilerParams(vmem_limit_bytes=vmem_for(*arrays, *out_shapes)),
        cost_estimate=pl.CostEstimate(flops=flops // 64, bytes_accessed=moved // 64, transcendentals=0),
    )(*scalars, *arrays)


def from_behind(block, axis, distance):
    devices = range(lax.axis_size(axis))
    route = [((i - distance) % len(devices), i) for i in devices]
    return lax.ppermute(block, axis, route)


def from_mate(block, axis, bit):
    return lax.ppermute(block, axis, [(i ^ bit, i) for i in range(lax.axis_size(axis))])


def gather_mates(block, axis, count, least=1):
    held = {0: block}
    bit = count // 2
    while bit >= least:
        held.update({m | bit: from_mate(held[m], axis, bit) for m in list(held)})
        bit //= 2
    return [held.get(m) for m in range(count)]


def after(value, *others):
    return lax.optimization_barrier((value, *others))[0] if others else value


def exchange(packs, bit):
    keys = [(step, mate | bit) for pack, _ in packs for step, mate in pack]
    blocks = [block for _, block in packs]
    return keys, from_mate(jnp.concatenate(blocks) if len(blocks) > 1 else blocks[0], "expert", bit)


def places(packs, first):
    found = {}
    for at, (keys, block) in enumerate(packs):
        rows = block.shape[0] // len(keys)
        found.update({key: (first + at, i * rows) for i, key in enumerate(keys)})
    return found


def place(owner_count):
    own = lax.axis_index("expert")
    return own // owner_count, own % owner_count


def message_kernel(owner_count, spans, slot_ref, live_ref, hidden_ref, grad_ref, *message_refs):
    own_block, _ = place(owner_count)
    groups = lax.axis_size("dp")
    hidden_units, tok_rows = hidden_ref.shape
    share_rows = hidden_units // groups
    block_width = grad_ref.shape[1] // QUART
    parts = block_width // LANES
    live = live_ref[0]
    slot = slot_ref[0, 0]
    kept = lax.broadcasted_iota(jnp.int32, (tok_rows, LANES), 0) < live
    meta = jnp.full((META_ROWS, LANES), slot.astype(jnp.float32)).astype(jnp.bfloat16)

    def put_hidden(message, row, span):
        first, length = span
        for group in range(groups):
            start = group * share_rows + first
            message[row : row + length, :] = hidden_ref[start : start + length, :]
            row += length

    for step, message in enumerate(message_refs[:QUART]):
        target = lax.rem(own_block + step, QUART)
        for part in range(parts):
            start = pl.multiple_of(target * block_width + part * LANES, LANES)
            columns = grad_ref[:, pl.ds(start, LANES)].astype(jnp.float32)
            row = part * tok_rows
            message[row : row + tok_rows, :] = jnp.where(kept, columns, 0.0).astype(jnp.bfloat16)
        row = parts * tok_rows
        message[row : row + META_ROWS, :] = meta
        put_hidden(message, row + META_ROWS, spans[0])
    for message, span in zip(message_refs[QUART:], spans[1:]):
        put_hidden(message, 0, span)


def partial_kernel(owner_count, tok_rows, where, base, steps, plan_ref, *refs):
    totals = refs[-len(steps) :]
    own_block, own_expert = place(owner_count)
    group, groups = lax.axis_index("dp"), lax.axis_size("dp")
    rows, block_width = totals[0].shape
    parts = block_width // LANES
    chunk = next(c for c in (208, 192, 176, 128, 112, 96, 64, 48, 32, 16) if rows % c == 0)
    bits = []
    for first in range(0, len(where), 16):
        packed = jnp.zeros((META_ROWS, LANES), jnp.float32)
        for at, (_, (head, row), _) in enumerate(where[first : first + 16]):
            meta = refs[head][row + parts * tok_rows : row + parts * tok_rows + META_ROWS, :]
            packed = packed + meta.astype(jnp.float32) * float(1 << at)
        bits.append(jnp.max(packed).astype(jnp.int32))
    for total in totals:
        total[...] = jnp.zeros_like(total)
    for at, ((step, mate), (head, head_row), (tail, tail_row)) in enumerate(where):
        source_expert = own_expert ^ mate
        source = lax.rem(own_block + QUART - step, QUART) * owner_count + source_expert
        is_replica = ((bits[at // 16] >> (at % 16)) & 1) == 1
        target = jnp.where(is_replica, plan_ref[source], source_expert)

        columns = jnp.concatenate(
            [
                refs[head][head_row + p * tok_rows : head_row + (p + 1) * tok_rows, :]
                for p in range(parts)
            ],
            axis=1,
        )

        def add(rounded):
            for total, ahead in zip(totals, steps):
                start = tail_row + base + lax.rem(group + ahead, groups) * rows

                @pl.loop(0, rows // chunk)
                def _(i):
                    term = jnp.dot(
                        refs[tail][pl.ds(pl.multiple_of(start + i * chunk, 16), chunk), :],
                        columns,
                        preferred_element_type=jnp.float32,
                    )
                    if rounded:
                        term = term.astype(jnp.bfloat16).astype(jnp.float32)
                    into = pl.ds(pl.multiple_of(i * chunk, 16), chunk)
                    total[into, :] += term

        if mate == 0:
            pl.when((target == own_expert) & jnp.logical_not(is_replica))(lambda: add(False))
        pl.when((target == own_expert) & is_replica)(lambda: add(True))


def new_rows(terms, states, first, start, size):
    inside, placed = pl.ds(start, size), pl.ds(first + start, size)
    master, one, two = states
    gradient = terms[0][inside, :]
    for term in terms[1:]:
        gradient = gradient + term[inside, :]
    weights = master[placed, :]
    first_next = beta_one * one[placed, :] + (1.0 - beta_one) * gradient
    second_next = beta_two * two[placed, :] + (1.0 - beta_two) * gradient * gradient
    scaled_first = first_next / (1.0 - beta_one**step_count)
    scaled_second = second_next / (1.0 - beta_two**step_count)
    direction = scaled_first / (jnp.sqrt(scaled_second) + epsilon)
    weights_next = weights - learn_rate * (direction + decay_rate * weights)
    return weights_next, first_next, second_next


def update_kernel(parts, first, pieces, *refs):
    terms, states, outs = refs[:parts], refs[parts : parts + 3], refs[parts + 3 :]
    for start, size in pieces:
        values = new_rows(terms, states, first, start, size)
        for out, value in zip(outs, (*values, values[0].astype(jnp.bfloat16))):
            out[pl.ds(start, size), :] = value


def finish_kernel(parts, first, pieces, *refs):
    terms, states, made = refs[:parts], refs[parts : parts + 3], refs[parts + 3 : parts + 6]
    *outs, fresh, fresh_states, sems = refs[parts + 6 :]
    copies = [
        pltpu.make_async_copy(rows, out.at[pl.ds(0, first), :], sems.at[which, 0])
        for which, (rows, out) in enumerate(zip(made, outs))
    ]
    for copy in copies:
        copy.start()
    for at, (start, size) in enumerate(pieces):
        inside, placed = pl.ds(start, size), pl.ds(first + start, size)
        values = new_rows(terms, states, first, start, size)
        fresh[inside, :] = values[0].astype(jnp.bfloat16)
        for which, value in enumerate(values):
            fresh_states[which, inside, :] = value
            copies.append(
                pltpu.make_async_copy(
                    fresh_states.at[which, inside, :],
                    outs[which].at[placed, :],
                    sems.at[which, at + 1],
                )
            )
            copies[-1].start()
    for copy in copies:
        copy.wait()


def update(terms, states, span, made=()):
    first, length = span
    rows, width = states[0].shape
    pieces = [(start, min(64, length - start)) for start in range(0, length, 64)]
    part = jax.ShapeDtypeStruct((length, width), jnp.float32)
    whole = jax.ShapeDtypeStruct((rows, width), jnp.float32)
    scratch = [
        pltpu.VMEM((3, length, width), jnp.float32),
        pltpu.SemaphoreType.DMA((3, len(pieces) + 1)),
    ]
    return pl.pallas_call(
        functools.partial(finish_kernel if made else update_kernel, len(terms), first, pieces),
        out_shape=(
            *([whole if made else part] * 3),
            jax.ShapeDtypeStruct((length, width), jnp.bfloat16),
        ),
        in_specs=[VMEM] * (len(terms) + len(states) + len(made)),
        out_specs=(*([ANYWHERE if made else VMEM] * 3), VMEM),
        scratch_shapes=scratch if made else [],
        compiler_params=pltpu.CompilerParams(vmem_limit_bytes=24 << 20),
        cost_estimate=pl.CostEstimate(
            flops=length * width, bytes_accessed=length * width, transcendentals=0
        ),
    )(*terms, *states, *made)


def choose_kernel(owner_count, where, plan_ref, *refs):
    candidates, chosen = refs[: len(where)], refs[len(where) :]
    own_block, own_expert = place(owner_count)
    for step, out in enumerate(chosen):
        wanted = plan_ref[lax.rem(own_block + step, QUART) * owner_count + own_expert]
        for (mate, rows), candidate in zip(where, candidates):

            @pl.when(wanted == own_expert ^ mate)
            def _():
                out[rows, :] = candidate[...]


def offer_kernel(owner_count, plan_ref, *refs):
    held, out = refs[:-1], refs[-1]
    own_block, own_expert = place(owner_count)
    wanted = plan_ref[own_block * owner_count + (own_expert ^ 1)]
    rows = out.shape[0]
    for pair, blocks in enumerate(held):

        @pl.when((wanted ^ own_expert) >> 1 == pair)
        def _():
            for step in range(QUART):
                width = blocks.shape[1]
                column = pl.multiple_of(lax.rem(own_block + QUART - step, QUART) * width, LANES)
                out[:, pl.ds(column, width)] = blocks[step * rows : (step + 1) * rows, :]


def assemble_kernel(owner_count, span, later, plan_ref, *refs):
    *blocks, out, sems = refs
    own_block, own_expert = place(owner_count)
    apart = plan_ref[own_block * owner_count + own_expert] ^ own_expert
    first, rows = span
    half = owner_count // 2

    def put(sources, start, group):
        copies = []
        for step, source in enumerate(sources):
            width = source.shape[1]
            column = pl.multiple_of(lax.rem(own_block + QUART - step, QUART) * width, LANES)
            target = out.at[pl.ds(start, source.shape[0]), pl.ds(column, width)]
            copies.append(pltpu.make_async_copy(source, target, sems.at[group, step]))
            copies[-1].start()
        return copies

    def finish(copies):
        for copy in copies:
            copy.wait()

    if later:
        offered, _ = blocks

        @pl.when(apart & 1 == 1)
        def _():
            copy = pltpu.make_async_copy(offered, out.at[pl.ds(first, rows), :], sems.at[0, 0])
            copy.start()
            copy.wait()

        return

    held, received = blocks[:half], blocks[half:]
    others = put(received, first + rows, 0)
    for pair in range(half):

        @pl.when(apart == 2 * pair)
        def _():
            lines = [held[pair].at[pl.ds(step * rows, rows), :] for step in range(QUART)]
            finish(put(lines, first, 1))

    finish(others)


def assemble(owner_count, span, plan, blocks, shape, held=None):
    later = held is not None
    inputs = [*blocks, held] if later else blocks
    return pl.pallas_call(
        functools.partial(assemble_kernel, owner_count, span, later),
        out_shape=shape,
        in_specs=[SMEM] + [VMEM] * len(blocks) + [ANYWHERE] * later,
        out_specs=ANYWHERE,
        scratch_shapes=[pltpu.SemaphoreType.DMA((2, QUART))],
        input_output_aliases={1 + len(blocks): 0} if later else {},
        compiler_params=pltpu.CompilerParams(vmem_limit_bytes=vmem_for(*blocks)),
        cost_estimate=pl.CostEstimate(flops=1, bytes_accessed=1 << 14, transcendentals=0),
    )(plan, *inputs)


def per_device(
    hidden_rows, grad_rows, block_slot, live_rows, replica_plan, master, moment_one, moment_two
):
    owner_count = lax.axis_size("expert") // QUART
    groups = lax.axis_size("dp")
    hidden_units, tok_rows = hidden_rows.shape
    block_width = grad_rows.shape[1] // QUART
    share_rows = hidden_units // groups
    assert block_slot.shape[1] == 1 and tok_rows == LANES and block_width % LANES == 0
    shape = jax.ShapeDtypeStruct
    lead = share_rows * 11 // 24 // 16 * 16
    spans = ((0, lead), (lead, share_rows - lead))

    head_rows = (block_width // LANES) * tok_rows + META_ROWS
    outs = [shape((head_rows + groups * lead, LANES), jnp.bfloat16)] * QUART
    outs += [shape((groups * (share_rows - lead), LANES), jnp.bfloat16)]
    messages = call(
        functools.partial(message_kernel, owner_count, spans),
        outs,
        (block_slot, live_rows),
        (hidden_rows, grad_rows),
    )

    def across(block, step):
        return from_behind(block, "expert", step * owner_count) if step else block

    first_bit = owner_count // 2
    other_bits = [1 << i for i in reversed(range(first_bit.bit_length() - 1))]
    own = [([(0, 0)], messages[0])]
    sides = [([(step, 0)], across(messages[step], step)) for step in (1, 3)]
    keys, block = exchange(own, first_bit)
    own += [(keys, after(block, *(side for _, side in sides))), *sides]
    rest = [([(0, 0)], messages[QUART])]
    rest_crossed = exchange(rest, first_bit)
    last = [([(2, 0)], across(after(messages[2], own[1][1], rest_crossed[1]), 2))]
    crossed = [exchange(sides, first_bit)]
    last_crossed = exchange(last, first_bit)
    for bit in other_bits:
        last += [exchange(last, bit)]
    later = after(messages[QUART], last[-1][1], crossed[0][1])
    sides_crossed = [(keys, after(block, last[-1][1])) for keys, block in crossed]
    for bit in other_bits:
        own += [exchange(own, bit)]
        sides_crossed += [exchange(sides_crossed, bit)]
    own += sides_crossed
    rest += [([(step, 0)], across(later, step)) for step in (1, 2, 3)]
    keys, block = last_crossed
    crossed = [(keys, after(block, *(part for _, part in rest[1:])))]
    for bit in other_bits:
        crossed += [exchange(crossed, bit)]
    last += crossed
    heads = own + last
    head_at = places(heads, 0)
    rests, rest_at = [], {}

    def partials(at, steps, wait_for):
        rows = spans[at][1]
        packs = heads + rests if at else heads
        where = [(key, found, rest_at[key] if at else found) for key, found in head_at.items()]
        return call(
            functools.partial(
                partial_kernel, owner_count, tok_rows, where, 0 if at else head_rows, steps
            ),
            [shape((rows, block_width), jnp.float32)] * len(steps),
            (after(replica_plan, *wait_for),),
            [block for _, block in packs],
            2 * len(steps) * rows * tok_rows * block_width * QUART,
        )

    states = (master[0], moment_one[0], moment_two[0])
    ahead = tuple(range(1, groups))
    block = lambda rows: shape((rows, block_width), jnp.bfloat16)

    far_one = partials(0, ahead, ())
    came_one = [from_behind(p, "dp", step) for step, p in zip(ahead, far_one)]
    near_one = partials(0, (0,), far_one)

    keys, parts = zip(*rest)
    crossed = [rest_crossed, exchange(rest[1:], first_bit)]
    for group in ([(sum(keys, []), jnp.concatenate(parts))], crossed):
        for bit in other_bits:
            group += [exchange(group, bit)]
        rests += group
    rest_at.update(places(rests, len(heads)))

    far_two = partials(1, ahead, near_one)
    came_one = [after(term, *far_two) for term in came_one]
    *made, fresh_one = update((*near_one, *came_one), states, spans[0])
    came_two = [
        from_behind(after(p, fresh_one), "dp", step) for step, p in zip(ahead, far_two)
    ]
    near_two = partials(1, (0,), (fresh_one,))

    lines = [across(fresh_one, step) for step in range(QUART)]

    came_two = [after(term, fresh_one) for term in came_two]
    *held, fresh_two = update((*near_two, *came_two), states, spans[1], made)

    rows_two = spans[1][1]
    cut = rows_two // 32 * 16
    halves = [(slice(0, cut), fresh_two[:cut]), (slice(cut, rows_two), fresh_two[cut:])]
    mates_two = {0: [(slice(0, rows_two), fresh_two)]}
    for bit in (first_bit, *other_bits):
        mates_two.update(
            {
                m | bit: [
                    (rows, from_mate(piece, "expert", bit))
                    for rows, piece in (halves if bit == first_bit else pieces)
                ]
                for m, pieces in list(mates_two.items())
            }
        )
    crossed_two = [piece for _, piece in mates_two[first_bit]]
    where = [(m, rows) for m, pieces in mates_two.items() for rows, _ in pieces]
    lines[1:] = [after(line, *crossed_two) for line in lines[1:]]
    chosen = call(
        functools.partial(choose_kernel, owner_count, where),
        [block(rows_two)] * QUART,
        (after(replica_plan, *lines),),
        [piece for pieces in mates_two.values() for _, piece in pieces],
    )
    received = [across(c, step) for step, c in enumerate(chosen)]

    wide = gather_mates(jnp.concatenate(lines), "expert", owner_count, 2)[::2]
    (offer,) = call(
        functools.partial(offer_kernel, owner_count),
        [shape((spans[0][1], QUART * block_width), jnp.bfloat16)],
        (replica_plan,),
        wide,
    )
    result = shape((share_rows, QUART * block_width), jnp.bfloat16)
    placed = assemble(
        owner_count, spans[0], replica_plan, [*wide, *received], result
    )
    offer = from_mate(after(offer, *received[1:]), "expert", 1)
    replica_weight = assemble(owner_count, spans[0], replica_plan, [offer], result, placed)
    return (*(state[None] for state in held), replica_weight[None])


def solution(mesh):
    return jax.shard_map(
        per_device,
        mesh=mesh,
        in_specs=(
            P(None, ("dp", "expert")),
            P(("dp", "expert"), None),
            P(("dp", "expert"), None),
            P(("dp", "expert")),
            P(),
            P("expert", "dp", None),
            P("expert", "dp", None),
            P("expert", "dp", None),
        ),
        out_specs=(
            P("expert", "dp", None),
            P("expert", "dp", None),
            P("expert", "dp", None),
            P("expert", "dp", None),
        ),
        check_vma=False,
    )
```
